32 devices in a mesh: tok: 4 (over y, x), tp: 8 (over z, core).
Axes of the slice: x: 2, y: 2, z: 4, core: 2. Of those that a mesh axis runs over, the one named last changes fastest.
Arguments:
- source: bfloat16 [1024, 8192], P('tp', 'tok'), may hold values from -6 to 6
- row_token: int32 [1024], replicated, may hold values from 0 to 1023, each once
- seg_ids: int32 [4, 256], P('tok'), may hold values from 0 to 3, never falling along the last dimension, each value on 1 to 128 neighbouring positions
- stitch_weight: bfloat16 [8192, 8192], P('tok', 'tp'), may hold values from -0.0625 to 0.0625
- norm_gain: float32 [8192], replicated, may hold values from 0.5 to 1.5
- q_weight: bfloat16 [8192, 8192], P(None, 'tp'), may hold values from -2 to 2
- kv_weight: bfloat16 [8192, 2048], P(None, 'tp'), may hold values from -2 to 2
- o_weight: bfloat16 [8192, 8192], P('tp'), may hold values from -0.0625 to 0.0625
- out_grad: bfloat16 [1024, 8192], P('tok', 'tp'), may hold values from -6 to 6
Outputs:
- layer_out: bfloat16 [1024, 8192], P('tok', 'tp')
- stitch_grad: float32 [8192, 8192], P('tok', 'tp')
The draws below stay inside these ranges and needn't reach their ends.
Inputs may be any that keep to these rules, and one draw needn't show every extreme that they name: `row_token`: each token index appears exactly once. `seg_ids`: within a pack the ids never fall; a document holds 1 to 128 tokens.
All inputs are finite; a program needn't handle non-finite values.
Results may differ from the reference program's by a relative error of at most 0.024.
Values may be sent and summed in bfloat16 or wider, within the bound.
No kernel may reach another device: no remote copies, remote signals or barrier semaphores. Data moves between devices by JAX's collectives and lax.ppermute only.
A program may use at most 128 MiB of HBM per device.

```python
import math
import jax
import jax.numpy as jnp
import numpy as np
from jax import lax

DS = 8192
D = 8192
HEADS = 64
KV = 8
HD = 128
TOK_DEV = 256
DOCS = 4
PACKS = 4
TOKENS = 1024


def draw_q_weight(key, part):
    result = jax.random.normal(jax.random.fold_in(key, 1), (D, HEADS * HD), jnp.float32) * D ** (-0.5)
    return jnp.clip(result, -2.0, 2.0).astype(jnp.bfloat16)


def draw_kv_weight(key, part):
    key_cols = jax.random.normal(jax.random.fold_in(key, 2), (D, KV, HD), jnp.float32) * D ** (-0.5)
    value_cols = jax.random.normal(jax.random.fold_in(key, 4), (D, KV, HD), jnp.float32) * D ** (-0.5)
    result = jnp.stack([key_cols, value_cols], axis=2).reshape(D, 2 * KV * HD)
    return jnp.clip(result, -2.0, 2.0).astype(jnp.bfloat16)


def steps_of(stream_key, dims, split, low, high):
    loudness, own = 1.0, jax.random.fold_in(stream_key, 6)
    for position, shards_of in split:
        heights = jnp.exp(jax.random.uniform(jax.random.fold_in(own, position), (shards_of,), jnp.float32, low / len(split), high / len(split)))
        loudness = loudness * jnp.repeat(heights, dims[position] // shards_of).reshape([-1 if axis == position else 1 for axis in range(len(dims))])
    return loudness


def length_profile(amount, total, limit, slope):
    loads = [(1 << 20) // math.isqrt(grade ** slope) + 1 for grade in range(2, amount + 1)]
    spare, counts = total - limit - (amount - 1), [1] * (amount - 1)
    while spare > 0:
        candidates = [i for i in range(amount - 1) if counts[i] < limit]
        pool, budget = sum([loads[i] for i in candidates]), spare
        for i in candidates:
            addition = min(limit - counts[i], max(1, budget * loads[i] // pool), spare)
            counts[i] = counts[i] + addition
            spare = spare - addition
    return np.array([limit] + counts)


def ragged(stream_key, amount, total, reach, lean):
    if amount == 2:
        one = jax.random.randint(stream_key, (), max(1, total - reach), min(reach, total - 1) + 1)
        return jnp.stack([one, total - one])
    sizes = jnp.asarray(length_profile(amount, total, reach, lean), jnp.int32)
    twos = (amount - 1) // 2
    source_of, taker = sizes[1:1 + 2 * twos:2], sizes[2:2 + 2 * twos:2]
    room = jnp.minimum(source_of - 1, reach - taker)
    passed = jax.random.randint(jax.random.fold_in(stream_key, 1), (twos,), 0, 1 << 20) % (room + 1)
    sizes = sizes.at[1:1 + 2 * twos:2].set(source_of - passed).at[2:2 + 2 * twos:2].set(taker + passed)
    return sizes[jax.random.permutation(jax.random.fold_in(stream_key, 2), amount)]


def bell_draw(own_key, shape, spread, most, shards=(), kind=jnp.bfloat16):
    values = jax.random.normal(own_key, shape, jnp.float32) * spread
    if len(shards) > 0:
        values = steps_of(own_key, shape, shards, -0.22, 0.18) * values
    return jnp.clip(values, min=-most, max=most).astype(kind)


def setup_inputs(seed: int = 0) -> dict:
    key_of = jax.random.split(jax.random.key(seed), 10)
    return {
        "source": bell_draw(key_of[0], (TOKENS, DS), 1.0, 6.0, ((0, 8), (1, 4))),
        "row_token": jax.random.permutation(key_of[1], TOKENS).astype(jnp.int32),
        "seg_ids": jax.vmap(lambda own: jnp.searchsorted(jnp.cumsum(ragged(own, DOCS, TOK_DEV, TOK_DEV // 2, 1)), jnp.arange(TOK_DEV), side="right"))(jax.random.split(key_of[2], PACKS)).reshape((PACKS, TOK_DEV)).astype(jnp.int32),
        "stitch_weight": bell_draw(key_of[3], (DS, D), DS ** -0.5, 0.0625, ((0, 4), (1, 8))),
        "norm_gain": jnp.clip(1.0 + 0.1 * jax.random.normal(key_of[4], (D,), jnp.float32), 0.5, 1.5),
        "q_weight": draw_q_weight(jax.random.fold_in(key_of[9], 71), 0),
        "kv_weight": draw_kv_weight(jax.random.fold_in(key_of[9], 71), 0),
        "o_weight": bell_draw(key_of[7], (HEADS * HD, D), (HEADS * HD) ** -0.5, 0.0625, ((0, 8),)),
        "out_grad": bell_draw(key_of[8], (TOKENS, D), 1.0, 6.0, ((0, 4), (1, 8))),
    }


epsilon = 1e-05

def to_wide(narrow):
    return lax.optimization_barrier(narrow).astype(jnp.float32)

def frequencies():
    exponent = jnp.arange(0, HD, 2).astype(jnp.float32) / HD
    plain_rate = 500000.0 ** (-exponent)
    wavelength = 2.0 * math.pi / plain_rate
    smoothing = (8192.0 / wavelength - 1.0) / 3.0
    blended = (1.0 - smoothing) * plain_rate / 8.0 + smoothing * plain_rate
    return jnp.where(wavelength < 2048.0, plain_rate, jnp.where(wavelength > 8192.0, plain_rate / 8.0, blended))

def rotate(vector_in, cosine_table, sine_table):
    half_size = vector_in.shape[-1] // 2
    first_half = vector_in[..., :half_size]
    second = vector_in[..., half_size:]
    return jnp.concatenate([first_half * cosine_table - second * sine_table, second * cosine_table + first_half * sine_table], axis=-1)

def unrotate(vector_in, cosine_table, sine_table):
    half_size = vector_in.shape[-1] // 2
    first_half = vector_in[..., :half_size]
    second = vector_in[..., half_size:]
    return jnp.concatenate([first_half * cosine_table + second * sine_table, second * cosine_table - first_half * sine_table], axis=-1)

def positions(seg_rows):
    earlier = lax.optimization_barrier(jnp.sum((seg_rows[:, None, :] < seg_rows[:, :, None]).astype(jnp.int32), axis=2))
    return jnp.arange(seg_rows.shape[1], dtype=jnp.int32)[None, :] - earlier

def allowed_mask(seg_rows):
    same_doc = seg_rows[:, :, None] == seg_rows[:, None, :]
    index_row = jnp.arange(seg_rows.shape[1], dtype=jnp.int32)
    return (same_doc & (index_row[None, None, :] <= index_row[None, :, None])).astype(jnp.int32)

def reference(source, row_token, seg_ids, stitch_weight, norm_gain, q_weight, kv_weight, o_weight, out_grad):
    group_size = HEADS // KV
    score_scale = 1.0 / math.sqrt(HD)
    source_tok = jnp.zeros_like(source).at[row_token].set(source)
    hidden_in = jnp.dot(source_tok, stitch_weight, preferred_element_type=jnp.float32).astype(jnp.bfloat16)
    hidden_f = to_wide(hidden_in)
    inv_rms = lax.rsqrt(lax.optimization_barrier(jnp.mean(hidden_f * hidden_f, axis=1, keepdims=True)) + epsilon)
    normed = (hidden_f * inv_rms * norm_gain).astype(jnp.bfloat16)
    angles = positions(seg_ids).reshape(TOKENS).astype(jnp.float32)[:, None] * frequencies()[None, :]
    cosines = jnp.cos(angles)[:, None, :]
    sine_table = jnp.sin(angles)[:, None, :]
    queries = rotate(jnp.dot(normed, q_weight, preferred_element_type=jnp.float32).reshape(TOKENS, HEADS, HD), cosines, sine_table).astype(jnp.bfloat16)
    pair_proj = jnp.dot(normed, kv_weight, preferred_element_type=jnp.float32).reshape(TOKENS, KV, 2, HD)
    keys_bf = rotate(pair_proj[:, :, 0], cosines, sine_table).astype(jnp.bfloat16)
    values = pair_proj[:, :, 1].astype(jnp.bfloat16)
    query_f = to_wide(queries).reshape(PACKS, TOK_DEV, KV, group_size, HD)
    key_f = to_wide(keys_bf).reshape(PACKS, TOK_DEV, KV, HD)
    value_f = to_wide(values).reshape(PACKS, TOK_DEV, KV, HD)
    scores = jnp.einsum('ptgrd,psgd->pgrts', query_f, key_f) * score_scale
    allowed = allowed_mask(seg_ids)[:, None, None]
    scores = jnp.where(allowed != 0, scores, -1e+30)
    row_max = lax.optimization_barrier(jnp.max(scores, axis=-1, keepdims=True))
    exponents = jnp.exp(scores - row_max)
    attention = exponents / lax.optimization_barrier(jnp.sum(exponents, axis=-1, keepdims=True))
    attention_half_precision = attention.astype(jnp.bfloat16)
    attention_w = to_wide(attention_half_precision)
    context = jnp.einsum('pgrts,psgd->ptgrd', attention_w, value_f).astype(jnp.bfloat16).reshape(TOKENS, HEADS * HD)
    attended = jnp.dot(context, o_weight, preferred_element_type=jnp.float32)
    layer_out = (hidden_f + attended).astype(jnp.bfloat16)
    grad_context = jnp.dot(out_grad, o_weight.T, preferred_element_type=jnp.float32).astype(jnp.bfloat16)
    context_gradient = to_wide(grad_context).reshape(PACKS, TOK_DEV, KV, group_size, HD)
    grad_probs = jnp.einsum('ptgrd,psgd->pgrts', context_gradient, value_f)
    centered = grad_probs - lax.optimization_barrier(jnp.sum(grad_probs * attention, axis=-1, keepdims=True))
    score_gradient = to_wide((attention * centered * score_scale).astype(jnp.bfloat16))
    grad_queries = unrotate(jnp.einsum('pgrts,psgd->ptgrd', score_gradient, key_f).reshape(TOKENS, HEADS, HD), cosines, sine_table).astype(jnp.bfloat16)
    grad_keys = unrotate(jnp.einsum('pgrts,ptgrd->psgd', score_gradient, query_f).reshape(TOKENS, KV, HD), cosines, sine_table).astype(jnp.bfloat16)
    grad_values = jnp.einsum('pgrts,ptgrd->psgd', attention_w, context_gradient).reshape(TOKENS, KV, HD).astype(jnp.bfloat16)
    grad_pairs = jnp.stack([grad_keys, grad_values], axis=2).reshape(TOKENS, 2 * KV * HD)
    grad_normed = jnp.dot(grad_queries.reshape(TOKENS, HEADS * HD), q_weight.T, preferred_element_type=jnp.float32)
    grad_normed = grad_normed + jnp.dot(grad_pairs, kv_weight.T, preferred_element_type=jnp.float32)
    weighted = norm_gain * grad_normed
    cubed = inv_rms * inv_rms * inv_rms
    grad_hidden = (to_wide(out_grad) + inv_rms * weighted - hidden_f * cubed * lax.optimization_barrier(jnp.mean(weighted * hidden_f, axis=1, keepdims=True))).astype(jnp.bfloat16)

    def add_pack(running, pack_index):
        row_start = (pack_index * TOK_DEV).astype(jnp.int32)
        rows_here = lax.dynamic_slice_in_dim(source_tok, row_start, TOK_DEV, 0)
        grads_here = lax.dynamic_slice_in_dim(grad_hidden, row_start, TOK_DEV, 0)
        product = lax.dot_general(rows_here, grads_here, (((0,), (0,)), ((), ())), preferred_element_type=jnp.float32).astype(jnp.bfloat16)
        return (running + to_wide(product), None)
    stitch_grad, unused_out = lax.scan(add_pack, jnp.zeros((DS, D), jnp.float32), jnp.arange(PACKS, dtype=jnp.int32))
    return (layer_out, stitch_grad)
```

```python
import math

import jax
import jax.numpy as jnp
from jax import lax
from jax.sharding import PartitionSpec as P

HD = 128


epsilon = 1e-05


def swapped(value, axis, mask):
    pairs = [(source, source ^ mask) for source in range(lax.axis_size(axis))]
    return lax.ppermute(value, axis, pairs)


def summed(value, axis):
    mask = 1
    while mask < lax.axis_size(axis):
        value = value + swapped(value, axis, mask)
        mask *= 2
    return value


def frequencies():
    exponent = jnp.arange(0, HD, 2).astype(jnp.float32) / HD
    plain_rate = 500000.0 ** (-exponent)
    wavelength = 2.0 * math.pi / plain_rate
    smoothing = (8192.0 / wavelength - 1.0) / 3.0
    blended = (1.0 - smoothing) * plain_rate / 8.0 + smoothing * plain_rate
    return jnp.where(
        wavelength < 2048.0, plain_rate, jnp.where(wavelength > 8192.0, plain_rate / 8.0, blended)
    )


def rotate(vector_in, cosine_table, sine_table):
    half_size = vector_in.shape[-1] // 2
    first_half = vector_in[..., :half_size]
    second = vector_in[..., half_size:]
    return jnp.concatenate(
        [
            first_half * cosine_table - second * sine_table,
            second * cosine_table + first_half * sine_table,
        ],
        axis=-1,
    )


def unrotate(vector_in, cosine_table, sine_table):
    return rotate(vector_in, cosine_table, -sine_table)


def body(
    source, row_token, seg_ids, stitch_weight, norm_gain, q_weight, kv_weight, o_weight, out_grad
):
    tok_rank = lax.axis_index("tok")
    tp_rank = lax.axis_index("tp")
    packs = lax.axis_size("tok")
    pack_len = seg_ids.shape[1]
    width = q_weight.shape[0]
    own_cols = stitch_weight.shape[1]
    score_scale = 1.0 / math.sqrt(HD)
    own_gain = lax.dynamic_slice_in_dim(norm_gain, tp_rank * own_cols, own_cols)

    gathered = lax.all_gather(source, "tp", axis=0, tiled=True)
    partial = jnp.dot(gathered, stitch_weight, preferred_element_type=jnp.float32).astype(
        jnp.bfloat16
    )
    within = jnp.arange(pack_len, dtype=jnp.int32)
    hidden = None
    for distance in range(packs):
        pack = tok_rank ^ distance
        rows = (row_token[None, :] == (pack * pack_len + within)[:, None]).astype(jnp.bfloat16)
        placed = jnp.dot(rows, partial, preferred_element_type=jnp.float32)
        if distance:
            placed = swapped(placed.astype(jnp.bfloat16), "tok", distance).astype(jnp.float32)
        hidden = placed if hidden is None else hidden + placed
    hidden_bf = hidden.astype(jnp.bfloat16)
    hidden_f = hidden_bf.astype(jnp.float32)
    square_sum = summed(jnp.sum(hidden_f * hidden_f, axis=1), "tp")
    inv_rms = lax.rsqrt(square_sum / width + epsilon)[:, None]
    gained = lax.all_gather((hidden_f * own_gain).astype(jnp.bfloat16), "tp", axis=1, tiled=True)

    order = (row_token[:, None] == jnp.arange(row_token.shape[0], dtype=jnp.int32)[None, :]).astype(
        jnp.bfloat16
    )
    tokens_last = lax.dot_general(
        gathered, order, (((0,), (0,)), ((), ())), preferred_element_type=jnp.float32
    ).astype(jnp.bfloat16)

    seg_row = seg_ids[0]
    earlier = jnp.sum((seg_row[None, :] < seg_row[:, None]).astype(jnp.int32), axis=1)
    angles = (within - earlier).astype(jnp.float32)[:, None] * frequencies()[None, :]
    cosines = jnp.cos(angles)[:, None, :]
    sine_table = jnp.sin(angles)[:, None, :]
    allowed = (seg_row[:, None] == seg_row[None, :]) & (within[None, :] <= within[:, None])
    local_heads = q_weight.shape[1] // HD
    kv_cols = kv_weight.shape[1]
    paired = kv_cols == HD
    kv_local = 1 if paired else kv_cols // (2 * HD)
    repeat = local_heads // kv_local
    query_pre = (
        jnp.dot(gained, q_weight, preferred_element_type=jnp.float32) * inv_rms
    ).reshape(pack_len, local_heads, HD)
    queries = rotate(query_pre, cosines, sine_table).astype(jnp.bfloat16)
    projected = jnp.dot(gained, kv_weight, preferred_element_type=jnp.float32) * inv_rms
    is_key = tp_rank % 2 == 0
    if paired:
        own_part = jnp.where(
            is_key, rotate(projected, cosines[:, 0], sine_table[:, 0]), projected
        ).astype(jnp.bfloat16)
        partner = swapped(own_part, "tp", 1)
        per_head_keys = jnp.where(is_key, own_part, partner)[:, None, :]
        per_head_values = jnp.where(is_key, partner, own_part)[:, None, :]
    else:
        halves = projected.reshape(pack_len, kv_local, 2, HD)
        per_head_keys = rotate(halves[:, :, 0], cosines, sine_table).astype(jnp.bfloat16)
        per_head_values = halves[:, :, 1].astype(jnp.bfloat16)
    per_head_queries = queries.reshape(pack_len, kv_local, repeat, HD)
    scores = (
        jnp.einsum(
            "nkej,wkj->kenw", per_head_queries, per_head_keys, preferred_element_type=jnp.float32
        )
        * score_scale
    )
    scores = jnp.where(allowed, scores, -1e30)
    row_max = jnp.max(scores, axis=-1, keepdims=True)
    exponents = jnp.exp(scores - row_max)
    attention = exponents / jnp.sum(exponents, axis=-1, keepdims=True)
    attention_half_precision = attention.astype(jnp.bfloat16)
    context = jnp.einsum(
        "cnfo,och->fcnh",
        attention_half_precision,
        per_head_values,
        preferred_element_type=jnp.float32,
    ).astype(jnp.bfloat16)
    context = context.reshape(pack_len, local_heads * HD)
    attended = lax.psum_scatter(
        jnp.dot(context, o_weight, preferred_element_type=jnp.float32).astype(jnp.bfloat16),
        "tp",
        scatter_dimension=1,
        tiled=True,
    ).astype(jnp.float32)
    layer_out = (hidden_f + attended).astype(jnp.bfloat16)

    every_grad = lax.all_gather(out_grad, "tp", axis=1, tiled=True)
    grad_context = lax.dot_general(
        every_grad, o_weight, (((1,), (1,)), ((), ())), preferred_element_type=jnp.float32
    ).astype(jnp.bfloat16)
    context_gradient = grad_context.reshape(pack_len, kv_local, repeat, HD)
    grad_probs = jnp.einsum(
        "nkej,wkj->kenw", context_gradient, per_head_values, preferred_element_type=jnp.float32
    )
    centered = grad_probs - jnp.sum(grad_probs * attention, axis=-1, keepdims=True)
    score_gradient = (attention * centered * score_scale).astype(jnp.bfloat16)
    query_grad = jnp.einsum(
        "cnfo,och->fcnh", score_gradient, per_head_keys, preferred_element_type=jnp.float32
    )
    grad_queries = unrotate(
        query_grad.reshape(pack_len, local_heads, HD), cosines, sine_table
    ).astype(jnp.bfloat16)
    key_part = jnp.einsum(
        "bwlf,lbwj->fbj", score_gradient, per_head_queries, preferred_element_type=jnp.float32
    )
    value_part = jnp.einsum(
        "bwlf,lbwj->fbj",
        attention_half_precision,
        context_gradient,
        preferred_element_type=jnp.float32,
    )
    if paired:
        outgoing = jnp.where(is_key, value_part, key_part)[:, 0]
        incoming = swapped(outgoing.astype(jnp.bfloat16), "tp", 1).astype(outgoing.dtype)
        own_sum = jnp.where(is_key, key_part, value_part)[:, 0] + incoming
        grad_pairs = jnp.where(
            is_key, unrotate(own_sum, cosines[:, 0], sine_table[:, 0]), own_sum
        ).astype(jnp.bfloat16)
    else:
        grad_keys = unrotate(key_part, cosines, sine_table).astype(jnp.bfloat16)
        grad_pairs = jnp.stack([grad_keys, value_part.astype(jnp.bfloat16)], axis=2).reshape(
            pack_len, kv_cols
        )
    aligned = jnp.sum(grad_queries.astype(jnp.float32) * query_pre, axis=(1, 2)) + jnp.sum(
        grad_pairs.astype(jnp.float32) * projected, axis=1
    )
    aligned = summed(aligned, "tp")[:, None]
    grad_normed = lax.dot_general(
        grad_queries.reshape(pack_len, local_heads * HD),
        q_weight,
        (((1,), (1,)), ((), ())),
        preferred_element_type=jnp.float32,
    ) + lax.dot_general(
        grad_pairs, kv_weight, (((1,), (1,)), ((), ())), preferred_element_type=jnp.float32
    )
    grad_sum = lax.psum_scatter(
        grad_normed.astype(jnp.bfloat16), "tp", scatter_dimension=1, tiled=True
    ).astype(jnp.float32)
    grad_hidden = (
        out_grad.astype(jnp.float32)
        + inv_rms * own_gain * grad_sum
        - hidden_f * (inv_rms * inv_rms * aligned / width)
    ).astype(jnp.bfloat16)
    every_pack = lax.all_gather(grad_hidden, "tok", axis=0, tiled=True)
    stitch_grad = jnp.dot(tokens_last, every_pack, preferred_element_type=jnp.float32)
    return (layer_out, stitch_grad)


def solution(mesh):
    placed = (
        P("tp", "tok"),
        P(),
        P("tok", None),
        P("tok", "tp"),
        P(),
        P(None, "tp"),
        P(None, "tp"),
        P("tp", None),
        P("tok", "tp"),
    )
    return jax.shard_map(
        body,
        mesh=mesh,
        in_specs=placed,
        out_specs=(P("tok", "tp"), P("tok", "tp")),
        check_vma=False,
    )
```

```python
import functools
import math

import jax
import jax.numpy as jnp
from jax import lax
from jax.experimental import pallas as pl
from jax.experimental.pallas import tpu as pltpu
from jax.sharding import PartitionSpec as P

HD = 128


epsilon = 1e-05


def swapped(value, axis, mask):
    pairs = [(source, source ^ mask) for source in range(lax.axis_size(axis))]
    return lax.ppermute(value, axis, pairs)


def summed(value, axis):
    mask = 1
    while mask < lax.axis_size(axis):
        value = value + swapped(value, axis, mask)
        mask *= 2
    return value


def frequencies():
    exponent = jnp.arange(0, HD, 2).astype(jnp.float32) / HD
    plain_rate = 500000.0 ** (-exponent)
    wavelength = 2.0 * math.pi / plain_rate
    smoothing = (8192.0 / wavelength - 1.0) / 3.0
    blended = (1.0 - smoothing) * plain_rate / 8.0 + smoothing * plain_rate
    return jnp.where(
        wavelength < 2048.0, plain_rate, jnp.where(wavelength > 8192.0, plain_rate / 8.0, blended)
    )


def rotate(vector_in, cosine_table, sine_table):
    half_size = vector_in.shape[-1] // 2
    first_half = vector_in[..., :half_size]
    second = vector_in[..., half_size:]
    return jnp.concatenate(
        [
            first_half * cosine_table - second * sine_table,
            second * cosine_table + first_half * sine_table,
        ],
        axis=-1,
    )


def unrotate(vector_in, cosine_table, sine_table):
    return rotate(vector_in, cosine_table, -sine_table)


VMEM_LIMIT = 56 * 2**20
ROWS_BY_ROWS = (((1,), (1,)), ((), ()))
COLS_BY_COLS = (((0,), (0,)), ((), ()))


def dot_f32(left, right, dims=(((1,), (0,)), ((), ()))):
    return lax.dot_general(left, right, dims, preferred_element_type=jnp.float32)


def attend(
    repeat, read_query, cosines, sines, seg_row, seg_col, keys, values, grad_ref, context_ref,
    query_grad_ref,
):
    rows = cosines.shape[0]
    score_scale = 1.0 / math.sqrt(HD)
    later = lax.broadcasted_iota(jnp.int32, (rows, rows), 0)
    sooner = lax.broadcasted_iota(jnp.int32, (rows, rows), 1)
    allowed = (seg_col == seg_row) & (sooner <= later)
    aligned = jnp.zeros((rows, HD), jnp.float32)
    key_parts, value_parts = [], []
    for group in range(len(keys)):
        key_part = jnp.zeros((rows, HD), jnp.float32)
        value_part = jnp.zeros((rows, HD), jnp.float32)
        for member in range(repeat):
            own = pl.ds((group * repeat + member) * HD, HD)
            plain = read_query(own)
            query = turn(plain, cosines, sines).astype(jnp.bfloat16)
            scores = dot_f32(query, keys[group], ROWS_BY_ROWS) * score_scale
            scores = jnp.where(allowed, scores, -1e30)
            exponents = jnp.exp(scores - jnp.max(scores, axis=1, keepdims=True))
            attention = exponents / jnp.sum(exponents, axis=1, keepdims=True)
            attention_bf = attention.astype(jnp.bfloat16)
            context_ref[:, own] = dot_f32(attention_bf, values[group]).astype(jnp.bfloat16)
            context_grad = grad_ref[:, own]
            grad_probs = dot_f32(context_grad, values[group], ROWS_BY_ROWS)
            mean = jnp.sum(grad_probs * attention, axis=1, keepdims=True)
            score_grad = (attention * (grad_probs - mean) * score_scale).astype(jnp.bfloat16)
            query_grad = turn(dot_f32(score_grad, keys[group]), cosines, -sines).astype(
                jnp.bfloat16
            )
            query_grad_ref[:, own] = query_grad
            aligned += query_grad.astype(jnp.float32) * plain
            key_part += dot_f32(score_grad, query, COLS_BY_COLS)
            value_part += dot_f32(attention_bf, context_grad, COLS_BY_COLS)
        key_parts.append(key_part)
        value_parts.append(value_part)
    return aligned, key_parts, value_parts


def turn(vector_in, cosines, sines):
    return vector_in * cosines + pltpu.roll(vector_in, HD // 2, 1) * sines


def attention_kernel(
    repeat, query_ref, scale_ref, cos_ref, sin_ref, seg_row_ref, seg_col_ref, key_ref, value_ref,
    grad_ref, context_ref, query_grad_ref, key_part_ref, value_part_ref, aligned_ref,
):
    row_scale = scale_ref[...]
    groups = [pl.ds(group * HD, HD) for group in range(key_ref.shape[1] // HD)]
    aligned, key_parts, value_parts = attend(
        repeat, lambda own: query_ref[:, own] * row_scale, cos_ref[...], sin_ref[...],
        seg_row_ref[...], seg_col_ref[...], [key_ref[:, shared] for shared in groups],
        [value_ref[:, shared] for shared in groups], grad_ref, context_ref, query_grad_ref,
    )
    for shared, key_part, value_part in zip(groups, key_parts, value_parts):
        key_part_ref[:, shared] = key_part
        value_part_ref[:, shared] = value_part
    aligned_ref[...] = jnp.sum(aligned, axis=1, keepdims=True)


def attention_parts(repeat, query_pre, inv_rms, cosines, sines, seg_row, keys, values, context_grad):
    rows = query_pre.shape[0]
    whole = pl.BlockSpec(memory_space=pltpu.VMEM)
    return pl.pallas_call(
        functools.partial(attention_kernel, repeat),
        in_specs=[whole] * 9,
        out_specs=[whole] * 5,
        out_shape=[
            jax.ShapeDtypeStruct(query_pre.shape, jnp.bfloat16),
            jax.ShapeDtypeStruct(query_pre.shape, jnp.bfloat16),
            jax.ShapeDtypeStruct(keys.shape, jnp.float32),
            jax.ShapeDtypeStruct(keys.shape, jnp.float32),
            jax.ShapeDtypeStruct((rows, 1), jnp.float32),
        ],
        compiler_params=pltpu.CompilerParams(vmem_limit_bytes=VMEM_LIMIT),
    )(
        query_pre, inv_rms, cosines, sines, seg_row[None, :], seg_row[:, None], keys, values,
        context_grad,
    )


def middle_kernel(
    repeat, gained_ref, q_weight_ref, kv_weight_ref, scale_ref, cos_ref, sin_ref, seg_row_ref,
    seg_col_ref, grad_ref, context_ref, aligned_ref, out_ref, gained, q_weight, kv_weight, out,
    query_sum, pair_sum, query_grad, sems,
):
    width, heads_cols = q_weight.shape
    pieces = sems.shape[1]
    step = width // pieces

    def part(piece):
        return pl.ds(pl.multiple_of(piece * step, step), step)

    def fetches(piece):
        span = part(piece)
        return (
            pltpu.make_async_copy(
                gained_ref.at[:, span], gained.at[:, span], sems.at[0, piece]
            ),
            pltpu.make_async_copy(q_weight_ref.at[span], q_weight.at[span], sems.at[1, piece]),
            pltpu.make_async_copy(kv_weight_ref.at[span], kv_weight.at[span], sems.at[2, piece]),
        )

    def returned(piece):
        span = part(piece)
        return pltpu.make_async_copy(out.at[:, span], out_ref.at[:, span], sems.at[3, piece])

    @pl.loop(0, pieces)
    def _(piece):
        for fetch in fetches(piece):
            fetch.start()

    query_sum[...] = jnp.zeros_like(query_sum)
    pair_sum[...] = jnp.zeros_like(pair_sum)

    @pl.loop(0, pieces)
    def _(piece):
        for fetch in fetches(piece):
            fetch.wait()
        span = part(piece)
        features = gained[:, span]
        query_sum[...] += dot_f32(features, q_weight[span, :])
        pair_sum[...] += dot_f32(features, kv_weight[span, :])

    row_scale = scale_ref[...]
    cosines, sines = cos_ref[...], sin_ref[...]
    groups = kv_weight.shape[1] // (2 * HD)
    pair_plain = pair_sum[...] * row_scale
    halves = [pair_plain[:, i * HD : (i + 1) * HD] for i in range(2 * groups)]
    aligned, key_parts, value_parts = attend(
        repeat, lambda own: query_sum[:, own] * row_scale, cosines, sines, seg_row_ref[...],
        seg_col_ref[...], [turn(half, cosines, sines).astype(jnp.bfloat16) for half in halves[::2]],
        [half.astype(jnp.bfloat16) for half in halves[1::2]], grad_ref, context_ref, query_grad,
    )
    pair_grads = []
    for key_part, value_part in zip(key_parts, value_parts):
        pair_grads.append(turn(key_part, cosines, -sines).astype(jnp.bfloat16))
        pair_grads.append(value_part.astype(jnp.bfloat16))
    for half, pair_grad in zip(halves, pair_grads):
        aligned += half * pair_grad.astype(jnp.float32)
    aligned_ref[...] = jnp.sum(aligned, axis=1, keepdims=True)
    pair_grad = jnp.concatenate(pair_grads, axis=1)

    @pl.loop(0, pieces)
    def _(piece):
        span = part(piece)
        out[:, span] = (
            dot_f32(query_grad[...], q_weight[span, :], ROWS_BY_ROWS)
            + dot_f32(pair_grad, kv_weight[span, :], ROWS_BY_ROWS)
        ).astype(out.dtype)
        returned(piece).start()

    @pl.loop(0, pieces)
    def _(piece):
        returned(piece).wait()


def middle(
    repeat, gained, q_weight, kv_weight, inv_rms, cosines, sines, seg_row, context_grad
):
    rows, width = gained.shape
    heads_cols, kv_cols = q_weight.shape[1], kv_weight.shape[1]
    whole, far = pl.BlockSpec(memory_space=pltpu.VMEM), pl.BlockSpec(memory_space=pl.ANY)
    return pl.pallas_call(
        functools.partial(middle_kernel, repeat),
        in_specs=[far] * 3 + [whole] * 6,
        out_specs=[whole] * 2 + [far],
        out_shape=[
            jax.ShapeDtypeStruct((rows, heads_cols), jnp.bfloat16),
            jax.ShapeDtypeStruct((rows, 1), jnp.float32),
            jax.ShapeDtypeStruct((rows, width), jnp.bfloat16),
        ],
        scratch_shapes=[
            pltpu.VMEM(gained.shape, jnp.bfloat16),
            pltpu.VMEM(q_weight.shape, jnp.bfloat16),
            pltpu.VMEM(kv_weight.shape, jnp.bfloat16),
            pltpu.VMEM(gained.shape, jnp.bfloat16),
            pltpu.VMEM((rows, heads_cols), jnp.float32),
            pltpu.VMEM((rows, kv_cols), jnp.float32),
            pltpu.VMEM((rows, heads_cols), jnp.bfloat16),
            pltpu.SemaphoreType.DMA((4, 8)),
        ],
        compiler_params=pltpu.CompilerParams(vmem_limit_bytes=VMEM_LIMIT),
    )(
        gained, q_weight, kv_weight, inv_rms, cosines, sines, seg_row[None, :], seg_row[:, None],
        context_grad,
    )


def stitch_kernel(packs, rank_ref, token_ref, source_ref, weight_ref, *refs):
    out_refs, product = refs[:packs], refs[-1]
    block = source_ref.shape[0]
    step = pl.program_id(0)
    here = pl.ds(pl.multiple_of(step * block, block), block)
    product[here, :] = dot_f32(source_ref[...], weight_ref[...]).astype(jnp.bfloat16)

    @pl.when(step == pl.num_programs(0) - 1)
    def _():
        pack_len = out_refs[0].shape[0]
        shape = (pack_len, product.shape[0])
        place = token_ref[...] - lax.broadcasted_iota(jnp.int32, shape, 0)
        for distance in range(packs):
            first = (rank_ref[0] ^ distance) * pack_len
            rows = (place == first).astype(jnp.float32).astype(jnp.bfloat16)
            out_refs[distance][...] = dot_f32(rows, product[...]).astype(jnp.bfloat16)


def stitched(packs, pack_len, rank, row_token, source, weight):
    rows, features = source.shape
    cols = weight.shape[1]
    block = min(512, rows)
    fixed = lambda i: (0, 0)
    return pl.pallas_call(
        functools.partial(stitch_kernel, packs),
        grid=(rows // block,),
        in_specs=[
            pl.BlockSpec(memory_space=pltpu.SMEM),
            pl.BlockSpec((1, rows), fixed),
            pl.BlockSpec((block, features), lambda i: (i, 0)),
            pl.BlockSpec(weight.shape, fixed),
        ],
        out_specs=[pl.BlockSpec((pack_len, cols), fixed)] * packs,
        out_shape=[jax.ShapeDtypeStruct((pack_len, cols), jnp.bfloat16)] * packs,
        scratch_shapes=[pltpu.VMEM((rows, cols), jnp.bfloat16)],
        compiler_params=pltpu.CompilerParams(vmem_limit_bytes=VMEM_LIMIT),
    )(rank.reshape(1), row_token[None, :], source, weight)


def back_kernel(query_ref, pair_ref, q_weight_ref, kv_weight_ref, out_ref):
    out_ref[...] = (
        dot_f32(query_ref[...], q_weight_ref[...], ROWS_BY_ROWS)
        + dot_f32(pair_ref[...], kv_weight_ref[...], ROWS_BY_ROWS)
    ).astype(out_ref.dtype)


def back_projected(grad_queries, grad_pairs, q_weight, kv_weight):
    rows = grad_queries.shape[0]
    width = q_weight.shape[0]
    block = 2048
    fixed = lambda i: (0, 0)
    return pl.pallas_call(
        back_kernel,
        grid=(width // block,),
        in_specs=[
            pl.BlockSpec(grad_queries.shape, fixed),
            pl.BlockSpec(grad_pairs.shape, fixed),
            pl.BlockSpec((block, q_weight.shape[1]), lambda i: (i, 0)),
            pl.BlockSpec((block, kv_weight.shape[1]), lambda i: (i, 0)),
        ],
        out_specs=pl.BlockSpec((rows, block), lambda i: (0, i)),
        out_shape=jax.ShapeDtypeStruct((rows, width), jnp.bfloat16),
        compiler_params=pltpu.CompilerParams(vmem_limit_bytes=VMEM_LIMIT),
    )(grad_queries, grad_pairs, q_weight, kv_weight)


def outer_kernel(*refs):
    features_ref, out_ref = refs[0], refs[-1]
    total = None
    for place, grad_ref in enumerate(refs[1:-1]):
        rows = grad_ref.shape[0]
        term = dot_f32(features_ref[:, pl.ds(place * rows, rows)], grad_ref[...])
        total = term if total is None else total + term
    out_ref[...] = total


def outer_summed(features, grads):
    block = min(512, features.shape[0])
    cols = grads[0].shape[1]
    return pl.pallas_call(
        outer_kernel,
        grid=(features.shape[0] // block,),
        in_specs=[pl.BlockSpec((block, features.shape[1]), lambda i: (i, 0))]
        + [pl.BlockSpec(grad.shape, lambda i: (0, 0)) for grad in grads],
        out_specs=pl.BlockSpec((block, cols), lambda i: (i, 0)),
        out_shape=jax.ShapeDtypeStruct((features.shape[0], cols), jnp.float32),
        compiler_params=pltpu.CompilerParams(vmem_limit_bytes=VMEM_LIMIT),
    )(features, *grads)


FIRST, SECOND, LAST = (1, 3, 0, 2), (2, 0, 3, 1), (3, 2, 1, 0)


def along(value, pairs):
    both = [(2 * start + core, 2 * end + core) for start, end in pairs for core in range(2)]
    return lax.ppermute(value, "tp", both)


def towards(table):
    return [(start, end) for start, end in enumerate(table)]


def arriving(table):
    return [(start, end) for end, start in enumerate(table)]


def after(value, done):
    value, done = lax.optimization_barrier((value, done))
    return value, done


def line_gather(block):
    beside = swapped(block, "tp", 1)
    first = along(block, arriving(FIRST))
    block, first = after(block, first)
    far = along(first, [(2, 3), (1, 0)])
    second = along(block, arriving(SECOND))
    near = along(block, [(1, 2), (2, 1)])
    last = far + near
    blocks = [block, beside]
    for own in (first, second, last):
        blocks += [own, swapped(own, "tp", 1)]
    return blocks


def line_scatter(parts):
    def joined(place):
        other = swapped(parts[2 * place + 1], "tp", 1)
        return parts[2 * place].astype(jnp.float32) + other.astype(jnp.float32)

    last = joined(0).astype(jnp.bfloat16)
    far = along(last, [(0, 1), (3, 2)])
    near = along(last, [(1, 2), (2, 1)])
    second = along(joined(1).astype(jnp.bfloat16), towards(SECOND))
    first = joined(2) + far.astype(jnp.float32)
    first = along(first.astype(jnp.bfloat16), towards(FIRST))
    own = joined(3) + near.astype(jnp.float32)
    return own, second, first


def line_total(own, second, first):
    return own + second.astype(jnp.float32) + first.astype(jnp.float32)


def line_stitch_kernel(packs, rank_ref, token_ref, weight_ref, *refs):
    blocks, out_refs = refs[:8], refs[8 : 8 + packs]
    rows, product, sems = refs[8 + packs :]
    block = rows.shape[0] // 8
    fetches = [
        pltpu.make_async_copy(blocks[i], rows.at[pl.ds(i * block, block)], sems.at[i])
        for i in range(8)
    ]
    for fetch in fetches:
        fetch.start()
    for half in range(2):
        here = pl.ds(half * 4 * block, 4 * block)
        for fetch in fetches[half * 4 : half * 4 + 4]:
            fetch.wait()
        product[here, :] = dot_f32(rows[here, :], weight_ref[...]).astype(jnp.bfloat16)
    pack_len = out_refs[0].shape[0]
    place = token_ref[...] - lax.broadcasted_iota(jnp.int32, (pack_len, product.shape[0]), 0)
    for distance in range(packs):
        first = (rank_ref[0] ^ distance) * pack_len
        chosen = (place == first).astype(jnp.float32).astype(jnp.bfloat16)
        out_refs[distance][...] = dot_f32(chosen, product[...]).astype(jnp.bfloat16)


def line_stitched(packs, pack_len, rank, token_row, blocks, weight):
    block, features = blocks[0].shape
    cols = weight.shape[1]
    whole, far = pl.BlockSpec(memory_space=pltpu.VMEM), pl.BlockSpec(memory_space=pl.ANY)
    return pl.pallas_call(
        functools.partial(line_stitch_kernel, packs),
        in_specs=[pl.BlockSpec(memory_space=pltpu.SMEM), whole, whole] + [far] * 8,
        out_specs=[whole] * packs,
        out_shape=[jax.ShapeDtypeStruct((pack_len, cols), jnp.bfloat16)] * packs,
        scratch_shapes=[
            pltpu.VMEM((8 * block, features), jnp.bfloat16),
            pltpu.VMEM((8 * block, cols), jnp.bfloat16),
            pltpu.SemaphoreType.DMA((8,)),
        ],
        compiler_params=pltpu.CompilerParams(vmem_limit_bytes=VMEM_LIMIT),
    )(rank.reshape(1), token_row, weight, *blocks)


def line_grad_kernel(ranks_ref, weight_ref, *refs):
    blocks, out_ref, features, total, sems = refs[:8], *refs[8:]
    step = pl.program_id(0)

    @pl.when(step == 0)
    def _():
        for i in range(8):
            pltpu.make_async_copy(blocks[i], features.at[i], sems.at[i]).start()
        total[...] = jnp.zeros_like(total)

    pltpu.make_async_copy(blocks[0], features.at[step], sems.at[step]).wait()
    total[...] += dot_f32(features[step], weight_ref[...], ROWS_BY_ROWS)

    @pl.when(step == 7)
    def _():
        out_ref[...] = total[...].astype(out_ref.dtype)


def line_grad_context(ranks, blocks, weight):
    rows, cols = blocks[0].shape
    heads_cols = weight.shape[0]
    far = pl.BlockSpec(memory_space=pl.ANY)
    return pl.pallas_call(
        line_grad_kernel,
        grid_spec=pltpu.PrefetchScalarGridSpec(
            num_scalar_prefetch=1,
            grid=(8,),
            in_specs=[pl.BlockSpec((heads_cols, cols), lambda i, ranks: (0, ranks[i]))] + [far] * 8,
            out_specs=pl.BlockSpec((rows, heads_cols), lambda i, ranks: (0, 0)),
            scratch_shapes=[
                pltpu.VMEM((8, rows, cols), jnp.bfloat16),
                pltpu.VMEM((rows, heads_cols), jnp.float32),
                pltpu.SemaphoreType.DMA((8,)),
            ],
        ),
        out_shape=jax.ShapeDtypeStruct((rows, heads_cols), jnp.bfloat16),
        compiler_params=pltpu.CompilerParams(vmem_limit_bytes=VMEM_LIMIT),
    )(ranks, weight, *blocks)


def line_attended_kernel(ranks_ref, context_ref, weight_ref, *out_refs):
    step = pl.program_id(0)
    product = dot_f32(context_ref[...], weight_ref[...]).astype(jnp.bfloat16)
    for i in range(8):

        @pl.when(step == i)
        def _(i=i):
            out_refs[i][...] = product


def line_attended(ranks, context, weight):
    rows, heads_cols = context.shape
    cols = weight.shape[1] // 8
    return pl.pallas_call(
        line_attended_kernel,
        grid_spec=pltpu.PrefetchScalarGridSpec(
            num_scalar_prefetch=1,
            grid=(8,),
            in_specs=[
                pl.BlockSpec((rows, heads_cols), lambda i, ranks: (0, 0)),
                pl.BlockSpec((heads_cols, cols), lambda i, ranks: (0, ranks[i])),
            ],
            out_specs=[pl.BlockSpec((rows, cols), lambda i, ranks: (0, 0))] * 8,
        ),
        out_shape=[jax.ShapeDtypeStruct((rows, cols), jnp.bfloat16)] * 8,
        compiler_params=pltpu.CompilerParams(vmem_limit_bytes=VMEM_LIMIT),
    )(ranks, context, weight)


def line_middle_kernel(
    repeat, from_ref, to_ref, gain_ref, cos_ref, sin_ref, seg_row_ref, seg_col_ref, grad_ref,
    q_weight_ref, kv_weight_ref, *refs,
):
    blocks, (context_ref, aligned_ref, scale_ref), out_refs = refs[:8], refs[8:11], refs[11:19]
    hidden, q_weight, kv_weight, out, query_sum, pair_sum, query_grad, sems, out_sems = refs[19:]
    width = q_weight.shape[0]
    rows, step = blocks[0].shape

    def part(rank):
        return pl.ds(pl.multiple_of(rank * step, step), step)

    def fetches(place):
        span = part(from_ref[place])
        return (
            pltpu.make_async_copy(q_weight_ref.at[span], q_weight.at[span], sems.at[1, place]),
            pltpu.make_async_copy(kv_weight_ref.at[span], kv_weight.at[span], sems.at[2, place]),
        )

    for place in range(8):
        pltpu.make_async_copy(blocks[place], hidden.at[place], sems.at[0, place]).start()
        for fetch in fetches(place):
            fetch.start()

    query_sum[...] = jnp.zeros_like(query_sum)
    pair_sum[...] = jnp.zeros_like(pair_sum)

    def project(place, squares):
        pltpu.make_async_copy(blocks[0], hidden.at[place], sems.at[0, place]).wait()
        for fetch in fetches(place):
            fetch.wait()
        span = part(from_ref[place])
        features = hidden[place].astype(jnp.float32)
        gained = (features * gain_ref[:, span]).astype(jnp.bfloat16)
        query_sum[...] += dot_f32(gained, q_weight[span, :])
        pair_sum[...] += dot_f32(gained, kv_weight[span, :])
        return squares + jnp.sum(features * features, axis=1, keepdims=True)

    squares = lax.fori_loop(0, 8, project, jnp.zeros((rows, 1), jnp.float32))
    row_scale = lax.rsqrt(squares / width + epsilon)
    scale_ref[...] = row_scale
    cosines, sines = cos_ref[...], sin_ref[...]
    groups = kv_weight.shape[1] // (2 * HD)
    pair_plain = pair_sum[...] * row_scale
    halves = [pair_plain[:, i * HD : (i + 1) * HD] for i in range(2 * groups)]
    aligned, key_parts, value_parts = attend(
        repeat, lambda own: query_sum[:, own] * row_scale, cosines, sines, seg_row_ref[...],
        seg_col_ref[...], [turn(half, cosines, sines).astype(jnp.bfloat16) for half in halves[::2]],
        [half.astype(jnp.bfloat16) for half in halves[1::2]], grad_ref, context_ref, query_grad,
    )
    pair_grads = []
    for key_part, value_part in zip(key_parts, value_parts):
        pair_grads.append(turn(key_part, cosines, -sines).astype(jnp.bfloat16))
        pair_grads.append(value_part.astype(jnp.bfloat16))
    for half, pair_grad in zip(halves, pair_grads):
        aligned += half * pair_grad.astype(jnp.float32)
    aligned_ref[...] = jnp.sum(aligned, axis=1, keepdims=True)
    pair_grad = jnp.concatenate(pair_grads, axis=1)

    @pl.loop(0, 8)
    def _(place):
        span = part(to_ref[place])
        out[place] = (
            dot_f32(query_grad[...], q_weight[span, :], ROWS_BY_ROWS)
            + dot_f32(pair_grad, kv_weight[span, :], ROWS_BY_ROWS)
        ).astype(out.dtype)
        for i in range(8):

            @pl.when(place == i)
            def _(i=i):
                pltpu.make_async_copy(out.at[i], out_refs[i], out_sems.at[i]).start()

    for i in range(8):
        pltpu.make_async_copy(out.at[i], out_refs[i], out_sems.at[i]).wait()


def line_middle(
    repeat, sources, targets, blocks, gain, q_weight, kv_weight, cosines, sines, seg_row,
    context_grad,
):
    rows, step = blocks[0].shape
    heads_cols, kv_cols = q_weight.shape[1], kv_weight.shape[1]
    whole, far = pl.BlockSpec(memory_space=pltpu.VMEM), pl.BlockSpec(memory_space=pl.ANY)
    scalars = pl.BlockSpec(memory_space=pltpu.SMEM)
    results = pl.pallas_call(
        functools.partial(line_middle_kernel, repeat),
        in_specs=[scalars] * 2 + [whole] * 6 + [far] * 10,
        out_specs=[whole] * 3 + [far] * 8,
        out_shape=[
            jax.ShapeDtypeStruct((rows, heads_cols), jnp.bfloat16),
            jax.ShapeDtypeStruct((rows, 1), jnp.float32),
            jax.ShapeDtypeStruct((rows, 1), jnp.float32),
        ]
        + [jax.ShapeDtypeStruct((rows, step), jnp.bfloat16)] * 8,
        scratch_shapes=[
            pltpu.VMEM((8, rows, step), jnp.bfloat16),
            pltpu.VMEM(q_weight.shape, jnp.bfloat16),
            pltpu.VMEM(kv_weight.shape, jnp.bfloat16),
            pltpu.VMEM((8, rows, step), jnp.bfloat16),
            pltpu.VMEM((rows, heads_cols), jnp.float32),
            pltpu.VMEM((rows, kv_cols), jnp.float32),
            pltpu.VMEM((rows, heads_cols), jnp.bfloat16),
            pltpu.SemaphoreType.DMA((3, 8)),
            pltpu.SemaphoreType.DMA((8,)),
        ],
        compiler_params=pltpu.CompilerParams(vmem_limit_bytes=VMEM_LIMIT),
    )(
        sources, targets, gain[None, :], cosines, sines, seg_row[None, :], seg_row[:, None],
        context_grad, q_weight, kv_weight, *blocks,
    )
    return results[0], results[1], results[2], results[3:]


def line_body(
    source, row_token, seg_ids, stitch_weight, norm_gain, q_weight, kv_weight, o_weight, out_grad
):
    tok_rank = lax.axis_index("tok")
    tp_rank = lax.axis_index("tp")
    packs = lax.axis_size("tok")
    pack_len = seg_ids.shape[1]
    width = q_weight.shape[0]
    own_cols = stitch_weight.shape[1]
    repeat = (q_weight.shape[1] // HD) // (kv_weight.shape[1] // (2 * HD))
    own_gain = lax.dynamic_slice_in_dim(norm_gain, tp_rank * own_cols, own_cols)
    chip, core = tp_rank // 2, tp_rank % 2

    def ranks(tables):
        chips = jnp.array(tables, jnp.int32)[:, chip]
        return jnp.stack([2 * chips + core, 2 * chips + 1 - core], axis=1).reshape(-1)

    stay = (0, 1, 2, 3)
    sources, targets = ranks((stay, FIRST, SECOND, LAST)), ranks((LAST, SECOND, FIRST, stay))

    within = jnp.arange(pack_len, dtype=jnp.int32)
    seg_row = seg_ids[0]
    earlier = jnp.sum((seg_row[None, :] < seg_row[:, None]).astype(jnp.int32), axis=1)
    angles = (within - earlier).astype(jnp.float32)[:, None] * frequencies()[None, :]
    cosine, sine = jnp.cos(angles), jnp.sin(angles)
    cosines = jnp.concatenate([cosine, cosine], axis=1)
    sines = jnp.concatenate([-sine, sine], axis=1)

    gathered = line_gather(source)
    token_row = row_token.reshape(8, -1)[sources].reshape(1, -1)
    late_grad, gathered[-2] = after(out_grad, gathered[-2])
    grad_blocks = line_gather(late_grad)
    placed = line_stitched(packs, pack_len, tok_rank, token_row, gathered, stitch_weight)
    hidden = placed[0].astype(jnp.float32)
    for distance in range(1, packs):
        hidden += swapped(placed[distance], "tok", distance).astype(jnp.float32)
    hidden_bf = hidden.astype(jnp.bfloat16)
    hidden_f = hidden_bf.astype(jnp.float32)
    hidden_blocks = line_gather(hidden_bf)
    grad_context = line_grad_context(sources, grad_blocks, o_weight)

    context, aligned, inv_rms, grad_parts = line_middle(
        repeat, sources, targets, hidden_blocks, norm_gain, q_weight, kv_weight, cosines, sines,
        seg_row, grad_context,
    )
    grad_own, grad_second, grad_first = line_scatter(grad_parts)
    aligned = summed(aligned[:, 0], "tp")
    context, aligned = after(context, aligned)
    attended_parts = line_attended(targets, context, o_weight)
    grad_sum = line_total(grad_own, grad_second, grad_first)
    attended_parts, grad_sum = after(attended_parts, grad_sum)
    grad_hidden = (
        out_grad.astype(jnp.float32)
        + inv_rms * own_gain * grad_sum
        - hidden_f * (inv_rms * inv_rms * aligned[:, None] / width)
    ).astype(jnp.bfloat16)
    every_pack = [grad_hidden] + [
        swapped(grad_hidden, "tok", distance) for distance in range(1, packs)
    ]
    token_order = (
        (tok_rank ^ jnp.arange(packs, dtype=jnp.int32))[:, None] * pack_len + within[None, :]
    ).reshape(-1)
    order = (token_row.reshape(-1, 1) == token_order[None, :]).astype(jnp.bfloat16)
    tokens_last = dot_f32(jnp.concatenate(gathered, axis=0), order, COLS_BY_COLS).astype(
        jnp.bfloat16
    )
    attended = line_scatter(attended_parts)
    late_hidden, *every_pack = lax.optimization_barrier((hidden_bf, *every_pack))
    stitch_grad = outer_summed(tokens_last, every_pack)
    attended = line_total(*attended)
    layer_out = (late_hidden.astype(jnp.float32) + attended).astype(jnp.bfloat16)
    return (layer_out, stitch_grad)


def body(
    source, row_token, seg_ids, stitch_weight, norm_gain, q_weight, kv_weight, o_weight, out_grad
):
    tok_rank = lax.axis_index("tok")
    tp_rank = lax.axis_index("tp")
    packs = lax.axis_size("tok")
    pack_len = seg_ids.shape[1]
    width = q_weight.shape[0]
    own_cols = stitch_weight.shape[1]
    own_gain = lax.dynamic_slice_in_dim(norm_gain, tp_rank * own_cols, own_cols)

    gathered = lax.all_gather(source, "tp", axis=0, tiled=True)
    placed = stitched(packs, pack_len, tok_rank, row_token, gathered, stitch_weight)
    within = jnp.arange(pack_len, dtype=jnp.int32)
    hidden = placed[0].astype(jnp.float32)
    for distance in range(1, packs):
        hidden += swapped(placed[distance], "tok", distance).astype(jnp.float32)
    hidden_bf = hidden.astype(jnp.bfloat16)
    hidden_f = hidden_bf.astype(jnp.float32)
    square_sum = summed(jnp.sum(hidden_f * hidden_f, axis=1), "tp")
    inv_rms = lax.rsqrt(square_sum / width + epsilon)[:, None]
    gained = lax.all_gather((hidden_f * own_gain).astype(jnp.bfloat16), "tp", axis=1, tiled=True)

    token_order = (
        (tok_rank ^ jnp.arange(packs, dtype=jnp.int32))[:, None] * pack_len + within[None, :]
    ).reshape(-1)
    order = (row_token[:, None] == token_order[None, :]).astype(jnp.bfloat16)
    tokens_last = dot_f32(gathered, order, COLS_BY_COLS).astype(jnp.bfloat16)

    seg_row = seg_ids[0]
    earlier = jnp.sum((seg_row[None, :] < seg_row[:, None]).astype(jnp.int32), axis=1)
    angles = (within - earlier).astype(jnp.float32)[:, None] * frequencies()[None, :]
    cosine, sine = jnp.cos(angles), jnp.sin(angles)
    cosines = jnp.concatenate([cosine, cosine], axis=1)
    sines = jnp.concatenate([-sine, sine], axis=1)
    local_heads = q_weight.shape[1] // HD
    kv_cols = kv_weight.shape[1]
    paired = kv_cols == HD
    kv_local = 1 if paired else kv_cols // (2 * HD)
    repeat = local_heads // kv_local
    every_grad = lax.all_gather(out_grad, "tp", axis=1, tiled=True)
    grad_context = lax.dot_general(
        every_grad, o_weight, (((1,), (1,)), ((), ())), preferred_element_type=jnp.float32
    ).astype(jnp.bfloat16)
    if paired:
        query_pre = jnp.dot(gained, q_weight, preferred_element_type=jnp.float32)
        projected = jnp.dot(gained, kv_weight, preferred_element_type=jnp.float32) * inv_rms
        is_key = tp_rank % 2 == 0
        own_part = jnp.where(is_key, rotate(projected, cosine, sine), projected).astype(
            jnp.bfloat16
        )
        partner = swapped(own_part, "tp", 1)
        keys = jnp.where(is_key, own_part, partner)
        values = jnp.where(is_key, partner, own_part)
        context, grad_queries, key_part, value_part, aligned = attention_parts(
            repeat, query_pre, inv_rms, cosines, sines, seg_row, keys, values, grad_context
        )
        outgoing = jnp.where(is_key, value_part, key_part)
        incoming = swapped(outgoing.astype(jnp.bfloat16), "tp", 1).astype(outgoing.dtype)
        own_sum = jnp.where(is_key, key_part, value_part) + incoming
        grad_pairs = jnp.where(is_key, unrotate(own_sum, cosine, sine), own_sum).astype(
            jnp.bfloat16
        )
        aligned += jnp.sum(grad_pairs.astype(jnp.float32) * projected, axis=1, keepdims=True)
        grad_normed = back_projected(grad_queries, grad_pairs, q_weight, kv_weight)
    else:
        context, aligned, grad_normed = middle(
            repeat, gained, q_weight, kv_weight, inv_rms, cosines, sines, seg_row, grad_context
        )
    aligned = summed(aligned[:, 0], "tp")[:, None]
    grad_sum = lax.psum_scatter(grad_normed, "tp", scatter_dimension=1, tiled=True)
    attended = jnp.dot(context, o_weight, preferred_element_type=jnp.float32).astype(jnp.bfloat16)
    attended, grad_sum = lax.optimization_barrier((attended, grad_sum))
    grad_hidden = (
        out_grad.astype(jnp.float32)
        + inv_rms * own_gain * grad_sum.astype(jnp.float32)
        - hidden_f * (inv_rms * inv_rms * aligned / width)
    ).astype(jnp.bfloat16)
    every_pack = [grad_hidden] + [
        swapped(grad_hidden, "tok", distance) for distance in range(1, packs)
    ]
    late_hidden, *every_pack = lax.optimization_barrier((hidden_bf, *every_pack))
    stitch_grad = outer_summed(tokens_last, every_pack)

    attended = lax.psum_scatter(attended, "tp", scatter_dimension=1, tiled=True)
    layer_out = (late_hidden.astype(jnp.float32) + attended.astype(jnp.float32)).astype(
        jnp.bfloat16
    )
    return (layer_out, stitch_grad)


def solution(mesh):
    placed = (
        P("tp", "tok"),
        P(),
        P("tok", None),
        P("tok", "tp"),
        P(),
        P(None, "tp"),
        P(None, "tp"),
        P("tp", None),
        P("tok", "tp"),
    )
    on_line = mesh.shape["tp"] == 8
    return jax.shard_map(
        line_body if on_line else body,
        mesh=mesh,
        in_specs=placed,
        out_specs=(P("tok", "tp"), P("tok", "tp")),
        check_vma=False,
    )
```

```python
import functools
import math

import jax
import jax.numpy as jnp
from jax import lax
from jax.experimental import pallas as pl
from jax.experimental.pallas import tpu as pltpu
from jax.sharding import PartitionSpec as P

HD = 128


epsilon = 1e-05


def swapped(value, axis, mask):
    pairs = [(source, source ^ mask) for source in range(lax.axis_size(axis))]
    return lax.ppermute(value, axis, pairs)


def summed(value, axis):
    mask = 1
    while mask < lax.axis_size(axis):
        value = value + swapped(value, axis, mask)
        mask *= 2
    return value


def frequencies():
    exponent = jnp.arange(0, HD, 2).astype(jnp.float32) / HD
    plain_rate = 500000.0 ** (-exponent)
    wavelength = 2.0 * math.pi / plain_rate
    smoothing = (8192.0 / wavelength - 1.0) / 3.0
    blended = (1.0 - smoothing) * plain_rate / 8.0 + smoothing * plain_rate
    return jnp.where(
        wavelength < 2048.0, plain_rate, jnp.where(wavelength > 8192.0, plain_rate / 8.0, blended)
    )


def rotate(vector_in, cosine_table, sine_table):
    half_size = vector_in.shape[-1] // 2
    first_half = vector_in[..., :half_size]
    second = vector_in[..., half_size:]
    return jnp.concatenate(
        [
            first_half * cosine_table - second * sine_table,
            second * cosine_table + first_half * sine_table,
        ],
        axis=-1,
    )


def unrotate(vector_in, cosine_table, sine_table):
    return rotate(vector_in, cosine_table, -sine_table)


VMEM_LIMIT = 56 * 2**20
ROWS_BY_ROWS = (((1,), (1,)), ((), ()))
COLS_BY_COLS = (((0,), (0,)), ((), ()))


def dot_f32(left, right, dims=(((1,), (0,)), ((), ()))):
    return lax.dot_general(left, right, dims, preferred_element_type=jnp.float32)


def attend(
    repeat, read_query, cosines, sines, seg_row, seg_col, keys, values, grad_ref, context_ref,
    query_grad_ref,
):
    rows = cosines.shape[0]
    score_scale = 1.0 / math.sqrt(HD)
    later = lax.broadcasted_iota(jnp.int32, (rows, rows), 0)
    sooner = lax.broadcasted_iota(jnp.int32, (rows, rows), 1)
    allowed = (seg_col == seg_row) & (sooner <= later)
    aligned = jnp.zeros((rows, HD), jnp.float32)
    key_parts, value_parts = [], []
    for group in range(len(keys)):
        key_part = jnp.zeros((rows, HD), jnp.float32)
        value_part = jnp.zeros((rows, HD), jnp.float32)
        for member in range(repeat):
            own = pl.ds((group * repeat + member) * HD, HD)
            plain = read_query(own)
            query = turn(plain, cosines, sines).astype(jnp.bfloat16)
            scores = dot_f32(query, keys[group], ROWS_BY_ROWS) * score_scale
            scores = jnp.where(allowed, scores, -1e30)
            exponents = jnp.exp(scores - jnp.max(scores, axis=1, keepdims=True))
            attention = exponents / jnp.sum(exponents, axis=1, keepdims=True)
            attention_bf = attention.astype(jnp.bfloat16)
            context_ref[:, own] = dot_f32(attention_bf, values[group]).astype(jnp.bfloat16)
            context_grad = grad_ref[:, own]
            grad_probs = dot_f32(context_grad, values[group], ROWS_BY_ROWS)
            mean = jnp.sum(grad_probs * attention, axis=1, keepdims=True)
            score_grad = (attention * (grad_probs - mean) * score_scale).astype(jnp.bfloat16)
            query_grad = turn(dot_f32(score_grad, keys[group]), cosines, -sines).astype(
                jnp.bfloat16
            )
            query_grad_ref[:, own] = query_grad
            aligned += query_grad.astype(jnp.float32) * plain
            key_part += dot_f32(score_grad, query, COLS_BY_COLS)
            value_part += dot_f32(attention_bf, context_grad, COLS_BY_COLS)
        key_parts.append(key_part)
        value_parts.append(value_part)
    return aligned, key_parts, value_parts


def turn(vector_in, cosines, sines):
    return vector_in * cosines + pltpu.roll(vector_in, HD // 2, 1) * sines


def attention_kernel(
    repeat, query_ref, scale_ref, cos_ref, sin_ref, seg_row_ref, seg_col_ref, key_ref, value_ref,
    grad_ref, context_ref, query_grad_ref, key_part_ref, value_part_ref, aligned_ref,
):
    row_scale = scale_ref[...]
    groups = [pl.ds(group * HD, HD) for group in range(key_ref.shape[1] // HD)]
    aligned, key_parts, value_parts = attend(
        repeat, lambda own: query_ref[:, own] * row_scale, cos_ref[...], sin_ref[...],
        seg_row_ref[...], seg_col_ref[...], [key_ref[:, shared] for shared in groups],
        [value_ref[:, shared] for shared in groups], grad_ref, context_ref, query_grad_ref,
    )
    for shared, key_part, value_part in zip(groups, key_parts, value_parts):
        key_part_ref[:, shared] = key_part
        value_part_ref[:, shared] = value_part
    aligned_ref[...] = jnp.sum(aligned, axis=1, keepdims=True)


def attention_parts(repeat, query_pre, inv_rms, cosines, sines, seg_row, keys, values, context_grad):
    rows = query_pre.shape[0]
    whole = pl.BlockSpec(memory_space=pltpu.VMEM)
    return pl.pallas_call(
        functools.partial(attention_kernel, repeat),
        in_specs=[whole] * 9,
        out_specs=[whole] * 5,
        out_shape=[
            jax.ShapeDtypeStruct(query_pre.shape, jnp.bfloat16),
            jax.ShapeDtypeStruct(query_pre.shape, jnp.bfloat16),
            jax.ShapeDtypeStruct(keys.shape, jnp.float32),
            jax.ShapeDtypeStruct(keys.shape, jnp.float32),
            jax.ShapeDtypeStruct((rows, 1), jnp.float32),
        ],
        compiler_params=pltpu.CompilerParams(vmem_limit_bytes=VMEM_LIMIT),
    )(
        query_pre, inv_rms, cosines, sines, seg_row[None, :], seg_row[:, None], keys, values,
        context_grad,
    )


def middle_kernel(
    repeat, gained_ref, q_weight_ref, kv_weight_ref, scale_ref, cos_ref, sin_ref, seg_row_ref,
    seg_col_ref, grad_ref, context_ref, aligned_ref, out_ref, gained, q_weight, kv_weight, out,
    query_sum, pair_sum, query_grad, sems,
):
    width, heads_cols = q_weight.shape
    pieces = sems.shape[1]
    step = width // pieces

    def part(piece):
        return pl.ds(pl.multiple_of(piece * step, step), step)

    def fetches(piece):
        span = part(piece)
        return (
            pltpu.make_async_copy(
                gained_ref.at[:, span], gained.at[:, span], sems.at[0, piece]
            ),
            pltpu.make_async_copy(q_weight_ref.at[span], q_weight.at[span], sems.at[1, piece]),
            pltpu.make_async_copy(kv_weight_ref.at[span], kv_weight.at[span], sems.at[2, piece]),
        )

    def returned(piece):
        span = part(piece)
        return pltpu.make_async_copy(out.at[:, span], out_ref.at[:, span], sems.at[3, piece])

    @pl.loop(0, pieces)
    def _(piece):
        for fetch in fetches(piece):
            fetch.start()

    query_sum[...] = jnp.zeros_like(query_sum)
    pair_sum[...] = jnp.zeros_like(pair_sum)

    @pl.loop(0, pieces)
    def _(piece):
        for fetch in fetches(piece):
            fetch.wait()
        span = part(piece)
        features = gained[:, span]
        query_sum[...] += dot_f32(features, q_weight[span, :])
        pair_sum[...] += dot_f32(features, kv_weight[span, :])

    row_scale = scale_ref[...]
    cosines, sines = cos_ref[...], sin_ref[...]
    groups = kv_weight.shape[1] // (2 * HD)
    pair_plain = pair_sum[...] * row_scale
    halves = [pair_plain[:, i * HD : (i + 1) * HD] for i in range(2 * groups)]
    aligned, key_parts, value_parts = attend(
        repeat, lambda own: query_sum[:, own] * row_scale, cosines, sines, seg_row_ref[...],
        seg_col_ref[...], [turn(half, cosines, sines).astype(jnp.bfloat16) for half in halves[::2]],
        [half.astype(jnp.bfloat16) for half in halves[1::2]], grad_ref, context_ref, query_grad,
    )
    pair_grads = []
    for key_part, value_part in zip(key_parts, value_parts):
        pair_grads.append(turn(key_part, cosines, -sines).astype(jnp.bfloat16))
        pair_grads.append(value_part.astype(jnp.bfloat16))
    for half, pair_grad in zip(halves, pair_grads):
        aligned += half * pair_grad.astype(jnp.float32)
    aligned_ref[...] = jnp.sum(aligned, axis=1, keepdims=True)
    pair_grad = jnp.concatenate(pair_grads, axis=1)

    @pl.loop(0, pieces)
    def _(piece):
        span = part(piece)
        out[:, span] = (
            dot_f32(query_grad[...], q_weight[span, :], ROWS_BY_ROWS)
            + dot_f32(pair_grad, kv_weight[span, :], ROWS_BY_ROWS)
        ).astype(out.dtype)
        returned(piece).start()

    @pl.loop(0, pieces)
    def _(piece):
        returned(piece).wait()


def middle(
    repeat, gained, q_weight, kv_weight, inv_rms, cosines, sines, seg_row, context_grad
):
    rows, width = gained.shape
    heads_cols, kv_cols = q_weight.shape[1], kv_weight.shape[1]
    whole, far = pl.BlockSpec(memory_space=pltpu.VMEM), pl.BlockSpec(memory_space=pl.ANY)
    return pl.pallas_call(
        functools.partial(middle_kernel, repeat),
        in_specs=[far] * 3 + [whole] * 6,
        out_specs=[whole] * 2 + [far],
        out_shape=[
            jax.ShapeDtypeStruct((rows, heads_cols), jnp.bfloat16),
            jax.ShapeDtypeStruct((rows, 1), jnp.float32),
            jax.ShapeDtypeStruct((rows, width), jnp.bfloat16),
        ],
        scratch_shapes=[
            pltpu.VMEM(gained.shape, jnp.bfloat16),
            pltpu.VMEM(q_weight.shape, jnp.bfloat16),
            pltpu.VMEM(kv_weight.shape, jnp.bfloat16),
            pltpu.VMEM(gained.shape, jnp.bfloat16),
            pltpu.VMEM((rows, heads_cols), jnp.float32),
            pltpu.VMEM((rows, kv_cols), jnp.float32),
            pltpu.VMEM((rows, heads_cols), jnp.bfloat16),
            pltpu.SemaphoreType.DMA((4, 8)),
        ],
        compiler_params=pltpu.CompilerParams(vmem_limit_bytes=VMEM_LIMIT),
    )(
        gained, q_weight, kv_weight, inv_rms, cosines, sines, seg_row[None, :], seg_row[:, None],
        context_grad,
    )


def stitch_kernel(packs, rank_ref, token_ref, source_ref, weight_ref, *refs):
    out_refs, product = refs[:packs], refs[-1]
    block = source_ref.shape[0]
    step = pl.program_id(0)
    here = pl.ds(pl.multiple_of(step * block, block), block)
    product[here, :] = dot_f32(source_ref[...], weight_ref[...]).astype(jnp.bfloat16)

    @pl.when(step == pl.num_programs(0) - 1)
    def _():
        pack_len = out_refs[0].shape[0]
        shape = (pack_len, product.shape[0])
        place = token_ref[...] - lax.broadcasted_iota(jnp.int32, shape, 0)
        for distance in range(packs):
            first = (rank_ref[0] ^ distance) * pack_len
            rows = (place == first).astype(jnp.float32).astype(jnp.bfloat16)
            out_refs[distance][...] = dot_f32(rows, product[...]).astype(jnp.bfloat16)


def stitched(packs, pack_len, rank, row_token, source, weight):
    rows, features = source.shape
    cols = weight.shape[1]
    block = min(512, rows)
    fixed = lambda i: (0, 0)
    return pl.pallas_call(
        functools.partial(stitch_kernel, packs),
        grid=(rows // block,),
        in_specs=[
            pl.BlockSpec(memory_space=pltpu.SMEM),
            pl.BlockSpec((1, rows), fixed),
            pl.BlockSpec((block, features), lambda i: (i, 0)),
            pl.BlockSpec(weight.shape, fixed),
        ],
        out_specs=[pl.BlockSpec((pack_len, cols), fixed)] * packs,
        out_shape=[jax.ShapeDtypeStruct((pack_len, cols), jnp.bfloat16)] * packs,
        scratch_shapes=[pltpu.VMEM((rows, cols), jnp.bfloat16)],
        compiler_params=pltpu.CompilerParams(vmem_limit_bytes=VMEM_LIMIT),
    )(rank.reshape(1), row_token[None, :], source, weight)


def back_kernel(query_ref, pair_ref, q_weight_ref, kv_weight_ref, out_ref):
    out_ref[...] = (
        dot_f32(query_ref[...], q_weight_ref[...], ROWS_BY_ROWS)
        + dot_f32(pair_ref[...], kv_weight_ref[...], ROWS_BY_ROWS)
    ).astype(out_ref.dtype)


def back_projected(grad_queries, grad_pairs, q_weight, kv_weight):
    rows = grad_queries.shape[0]
    width = q_weight.shape[0]
    block = 2048
    fixed = lambda i: (0, 0)
    return pl.pallas_call(
        back_kernel,
        grid=(width // block,),
        in_specs=[
            pl.BlockSpec(grad_queries.shape, fixed),
            pl.BlockSpec(grad_pairs.shape, fixed),
            pl.BlockSpec((block, q_weight.shape[1]), lambda i: (i, 0)),
            pl.BlockSpec((block, kv_weight.shape[1]), lambda i: (i, 0)),
        ],
        out_specs=pl.BlockSpec((rows, block), lambda i: (0, i)),
        out_shape=jax.ShapeDtypeStruct((rows, width), jnp.bfloat16),
        compiler_params=pltpu.CompilerParams(vmem_limit_bytes=VMEM_LIMIT),
    )(grad_queries, grad_pairs, q_weight, kv_weight)


def outer_kernel(*refs):
    features_ref, out_ref = refs[0], refs[-1]
    total = None
    for place, grad_ref in enumerate(refs[1:-1]):
        rows = grad_ref.shape[0]
        term = dot_f32(features_ref[:, pl.ds(place * rows, rows)], grad_ref[...])
        total = term if total is None else total + term
    out_ref[...] = total


def outer_summed(features, grads):
    block = min(512, features.shape[0])
    cols = grads[0].shape[1]
    return pl.pallas_call(
        outer_kernel,
        grid=(features.shape[0] // block,),
        in_specs=[pl.BlockSpec((block, features.shape[1]), lambda i: (i, 0))]
        + [pl.BlockSpec(grad.shape, lambda i: (0, 0)) for grad in grads],
        out_specs=pl.BlockSpec((block, cols), lambda i: (i, 0)),
        out_shape=jax.ShapeDtypeStruct((features.shape[0], cols), jnp.float32),
        compiler_params=pltpu.CompilerParams(vmem_limit_bytes=VMEM_LIMIT),
    )(features, *grads)


STAY, FIRST, SECOND, LAST = (0, 1, 2, 3), (1, 3, 0, 2), (2, 0, 3, 1), (3, 2, 1, 0)


def along(value, pairs):
    both = [(2 * start + core, 2 * end + core) for start, end in pairs for core in range(2)]
    return lax.ppermute(value, "tp", both)


def towards(table):
    return [(start, end) for start, end in enumerate(table)]


def arriving(table):
    return [(start, end) for end, start in enumerate(table)]


def after(value, done):
    value, done = lax.optimization_barrier((value, done))
    return value, done


def gather_begun(block):
    return along(block, arriving(FIRST))


def gather_rest(block, first):
    far = along(first, [(2, 3), (1, 0)])
    second = along(block, arriving(SECOND))
    near = along(block, [(1, 2), (2, 1)])
    return far, second, near


def early_blocks(block, first):
    return [block, swapped(block, "tp", 1), first, swapped(first, "tp", 1)]


def late_blocks(rest):
    far, second, near = rest
    last = far + near
    return [second, swapped(second, "tp", 1), last, swapped(last, "tp", 1)]


def line_scatter(parts):
    def joined(place):
        other = swapped(parts[2 * place + 1], "tp", 1)
        return parts[2 * place].astype(jnp.float32) + other.astype(jnp.float32)

    last = joined(0).astype(jnp.bfloat16)
    far = along(last, [(0, 1), (3, 2)])
    near = along(last, [(1, 2), (2, 1)])
    second = along(joined(1).astype(jnp.bfloat16), towards(SECOND))
    first = joined(2) + far.astype(jnp.float32)
    first = along(first.astype(jnp.bfloat16), towards(FIRST))
    own = joined(3) + near.astype(jnp.float32)
    return own, second, first


def line_total(own, second, first):
    return own + second.astype(jnp.float32) + first.astype(jnp.float32)


def line_stitch_half(blocks, rows, rows_ref, weight_ref, product, here, sems, out_sem):
    block = blocks[0].shape[0]
    fetches = [
        pltpu.make_async_copy(blocks[i], rows.at[pl.ds(i * block, block)], sems.at[i])
        for i in range(4)
    ]
    for fetch in fetches:
        fetch.start()
    for fetch in fetches:
        fetch.wait()
    kept = pltpu.make_async_copy(rows, rows_ref, out_sem)
    kept.start()
    product[here, :] = dot_f32(rows[...], weight_ref[...]).astype(jnp.bfloat16)
    return kept


def line_stitch_early_kernel(weight_ref, *refs):
    blocks, (product_ref, rows_ref, rows, sems, out_sem) = refs[:4], refs[4:]
    everything = pl.ds(0, rows.shape[0])
    line_stitch_half(
        blocks, rows, rows_ref, weight_ref, product_ref, everything, sems, out_sem
    ).wait()


def line_stitch_kernel(packs, rank_ref, token_ref, weight_ref, early_ref, *refs):
    blocks, out_refs = refs[:4], refs[4 : 4 + packs]
    rows_ref, rows, product, sems, out_sem = refs[4 + packs :]
    half = rows.shape[0]
    kept = line_stitch_half(
        blocks, rows, rows_ref, weight_ref, product, pl.ds(half, half), sems, out_sem
    )
    product[pl.ds(0, half), :] = early_ref[...]
    pack_len = out_refs[0].shape[0]
    place = token_ref[...] - lax.broadcasted_iota(jnp.int32, (pack_len, product.shape[0]), 0)
    for distance in range(packs):
        first = (rank_ref[0] ^ distance) * pack_len
        chosen = (place == first).astype(jnp.float32).astype(jnp.bfloat16)
        out_refs[distance][...] = dot_f32(chosen, product[...]).astype(jnp.bfloat16)
    kept.wait()


def line_stitched_early(blocks, weight):
    block, features = blocks[0].shape
    cols = weight.shape[1]
    whole, far = pl.BlockSpec(memory_space=pltpu.VMEM), pl.BlockSpec(memory_space=pl.ANY)
    return pl.pallas_call(
        line_stitch_early_kernel,
        in_specs=[whole] + [far] * 4,
        out_specs=[whole, far],
        out_shape=[
            jax.ShapeDtypeStruct((4 * block, cols), jnp.bfloat16),
            jax.ShapeDtypeStruct((4 * block, features), jnp.bfloat16),
        ],
        scratch_shapes=[
            pltpu.VMEM((4 * block, features), jnp.bfloat16),
            pltpu.SemaphoreType.DMA((4,)),
            pltpu.SemaphoreType.DMA,
        ],
        compiler_params=pltpu.CompilerParams(vmem_limit_bytes=VMEM_LIMIT),
    )(weight, *blocks)


def line_stitched(packs, pack_len, rank, token_row, early, blocks, weight):
    block, features = blocks[0].shape
    cols = weight.shape[1]
    whole, far = pl.BlockSpec(memory_space=pltpu.VMEM), pl.BlockSpec(memory_space=pl.ANY)
    results = pl.pallas_call(
        functools.partial(line_stitch_kernel, packs),
        in_specs=[pl.BlockSpec(memory_space=pltpu.SMEM)] + [whole] * 3 + [far] * 4,
        out_specs=[whole] * packs + [far],
        out_shape=[jax.ShapeDtypeStruct((pack_len, cols), jnp.bfloat16)] * packs
        + [jax.ShapeDtypeStruct((4 * block, features), jnp.bfloat16)],
        scratch_shapes=[
            pltpu.VMEM((4 * block, features), jnp.bfloat16),
            pltpu.VMEM((8 * block, cols), jnp.bfloat16),
            pltpu.SemaphoreType.DMA((4,)),
            pltpu.SemaphoreType.DMA,
        ],
        compiler_params=pltpu.CompilerParams(vmem_limit_bytes=VMEM_LIMIT),
    )(rank.reshape(1), token_row, weight, early, *blocks)
    return results[:packs], results[packs]


def line_grad_kernel(chips_ref, core_ref, weight_ref, *refs):
    blocks, out_ref, features, total, sems = refs[:8], *refs[8:]
    step = pl.program_id(0)
    cols = blocks[0].shape[1]

    def fetch(place, half):
        core = core_ref[0] if half == 0 else 1 - core_ref[0]
        there = features.at[place, :, pl.ds(pl.multiple_of(core * cols, cols), cols)]
        return there, sems.at[place, half]

    @pl.when(step == 0)
    def _():
        for i in range(8):
            pltpu.make_async_copy(blocks[i], *fetch(i // 2, i % 2)).start()
        total[...] = jnp.zeros_like(total)

    for half in range(2):
        pltpu.make_async_copy(blocks[half], *fetch(step, half)).wait()
    total[...] += dot_f32(features[step], weight_ref[...], ROWS_BY_ROWS)

    @pl.when(step == 3)
    def _():
        out_ref[...] = total[...].astype(out_ref.dtype)


def line_grad_context(chips, core, blocks, weight):
    rows, cols = blocks[0].shape
    heads_cols = weight.shape[0]
    far = pl.BlockSpec(memory_space=pl.ANY)
    return pl.pallas_call(
        line_grad_kernel,
        grid_spec=pltpu.PrefetchScalarGridSpec(
            num_scalar_prefetch=2,
            grid=(4,),
            in_specs=[pl.BlockSpec((heads_cols, 2 * cols), lambda i, chips, core: (0, chips[i]))]
            + [far] * 8,
            out_specs=pl.BlockSpec((rows, heads_cols), lambda i, chips, core: (0, 0)),
            scratch_shapes=[
                pltpu.VMEM((4, rows, 2 * cols), jnp.bfloat16),
                pltpu.VMEM((rows, heads_cols), jnp.float32),
                pltpu.SemaphoreType.DMA((4, 2)),
            ],
        ),
        out_shape=jax.ShapeDtypeStruct((rows, heads_cols), jnp.bfloat16),
        compiler_params=pltpu.CompilerParams(vmem_limit_bytes=VMEM_LIMIT),
    )(chips, core.reshape(1), weight, *blocks)


def line_attended_kernel(chips_ref, core_ref, context_ref, weight_ref, *refs):
    out_refs, product = refs[:8], refs[8]
    step = pl.program_id(0)
    cols = out_refs[0].shape[1]
    product[...] = dot_f32(context_ref[...], weight_ref[...]).astype(jnp.bfloat16)
    for i in range(4):

        @pl.when(step == i)
        def _(i=i):
            for half in range(2):
                core = core_ref[0] if half == 0 else 1 - core_ref[0]
                here = pl.ds(pl.multiple_of(core * cols, cols), cols)
                out_refs[2 * i + half][...] = product[:, here]


def line_attended(chips, core, context, weight):
    rows, heads_cols = context.shape
    cols = weight.shape[1] // 8
    fixed = lambda i, chips, core: (0, 0)
    return pl.pallas_call(
        line_attended_kernel,
        grid_spec=pltpu.PrefetchScalarGridSpec(
            num_scalar_prefetch=2,
            grid=(4,),
            in_specs=[
                pl.BlockSpec((rows, heads_cols), fixed),
                pl.BlockSpec((heads_cols, 2 * cols), lambda i, chips, core: (0, chips[i])),
            ],
            out_specs=[pl.BlockSpec((rows, cols), fixed)] * 8,
            scratch_shapes=[pltpu.VMEM((rows, 2 * cols), jnp.bfloat16)],
        ),
        out_shape=[jax.ShapeDtypeStruct((rows, cols), jnp.bfloat16)] * 8,
        compiler_params=pltpu.CompilerParams(vmem_limit_bytes=VMEM_LIMIT),
    )(chips, core.reshape(1), context, weight)


def line_middle_kernel(
    repeat, from_ref, to_ref, gain_ref, cos_ref, sin_ref, seg_row_ref, seg_col_ref, grad_ref,
    q_weight_ref, kv_weight_ref, *refs,
):
    blocks, context_ref, out_refs = refs[:8], refs[8], refs[9:17]
    hidden, q_weight, kv_weight, out, query_sum, pair_sum, query_grad, sems, out_sems = refs[17:]
    width = q_weight.shape[0]
    rows, step = blocks[0].shape

    def part(rank):
        return pl.ds(pl.multiple_of(rank * step, step), step)

    def fetches(place):
        span = part(from_ref[place])
        return (
            pltpu.make_async_copy(q_weight_ref.at[span], q_weight.at[span], sems.at[1, place]),
            pltpu.make_async_copy(kv_weight_ref.at[span], kv_weight.at[span], sems.at[2, place]),
        )

    for place in range(8):
        pltpu.make_async_copy(blocks[place], hidden.at[place], sems.at[0, place]).start()
        for fetch in fetches(place):
            fetch.start()

    query_sum[...] = jnp.zeros_like(query_sum)
    pair_sum[...] = jnp.zeros_like(pair_sum)

    def project(place, squares):
        pltpu.make_async_copy(blocks[0], hidden.at[place], sems.at[0, place]).wait()
        for fetch in fetches(place):
            fetch.wait()
        span = part(from_ref[place])
        features = hidden[place].astype(jnp.float32)
        gained = (features * gain_ref[:, span]).astype(jnp.bfloat16)
        query_sum[...] += dot_f32(gained, q_weight[span, :])
        pair_sum[...] += dot_f32(gained, kv_weight[span, :])
        return squares + jnp.sum(features * features, axis=1, keepdims=True)

    squares = lax.fori_loop(0, 8, project, jnp.zeros((rows, 1), jnp.float32))
    row_scale = lax.rsqrt(squares / width + epsilon)
    cosines, sines = cos_ref[...], sin_ref[...]
    groups = kv_weight.shape[1] // (2 * HD)
    pair_plain = pair_sum[...] * row_scale
    halves = [pair_plain[:, i * HD : (i + 1) * HD] for i in range(2 * groups)]
    aligned, key_parts, value_parts = attend(
        repeat, lambda own: query_sum[:, own] * row_scale, cosines, sines, seg_row_ref[...],
        seg_col_ref[...], [turn(half, cosines, sines).astype(jnp.bfloat16) for half in halves[::2]],
        [half.astype(jnp.bfloat16) for half in halves[1::2]], grad_ref, context_ref, query_grad,
    )
    pair_grads = []
    for key_part, value_part in zip(key_parts, value_parts):
        pair_grads.append(turn(key_part, cosines, -sines).astype(jnp.bfloat16))
        pair_grads.append(value_part.astype(jnp.bfloat16))
    for half, pair_grad in zip(halves, pair_grads):
        aligned += half * pair_grad.astype(jnp.float32)
    aligned = jnp.sum(aligned, axis=1, keepdims=True) * (row_scale * row_scale / width)
    pair_grad = jnp.concatenate(pair_grads, axis=1)

    @pl.loop(0, 8)
    def _(place):
        span = part(to_ref[place])
        grad_normed = dot_f32(query_grad[...], q_weight[span, :], ROWS_BY_ROWS)
        grad_normed += dot_f32(pair_grad, kv_weight[span, :], ROWS_BY_ROWS)
        features = hidden[6 - 2 * (place // 2) + place % 2].astype(jnp.float32)
        out[place] = (
            grad_normed * (row_scale * gain_ref[:, span]) - features * aligned
        ).astype(out.dtype)
        for i in range(8):

            @pl.when(place == i)
            def _(i=i):
                pltpu.make_async_copy(out.at[i], out_refs[i], out_sems.at[i]).start()

    for i in range(8):
        pltpu.make_async_copy(out.at[i], out_refs[i], out_sems.at[i]).wait()


def line_middle(
    repeat, sources, targets, blocks, gain, q_weight, kv_weight, cosines, sines, seg_row,
    context_grad,
):
    rows, step = blocks[0].shape
    heads_cols, kv_cols = q_weight.shape[1], kv_weight.shape[1]
    whole, far = pl.BlockSpec(memory_space=pltpu.VMEM), pl.BlockSpec(memory_space=pl.ANY)
    scalars = pl.BlockSpec(memory_space=pltpu.SMEM)
    results = pl.pallas_call(
        functools.partial(line_middle_kernel, repeat),
        in_specs=[scalars] * 2 + [whole] * 6 + [far] * 10,
        out_specs=[whole] + [far] * 8,
        out_shape=[jax.ShapeDtypeStruct((rows, heads_cols), jnp.bfloat16)]
        + [jax.ShapeDtypeStruct((rows, step), jnp.bfloat16)] * 8,
        scratch_shapes=[
            pltpu.VMEM((8, rows, step), jnp.bfloat16),
            pltpu.VMEM(q_weight.shape, jnp.bfloat16),
            pltpu.VMEM(kv_weight.shape, jnp.bfloat16),
            pltpu.VMEM((8, rows, step), jnp.bfloat16),
            pltpu.VMEM((rows, heads_cols), jnp.float32),
            pltpu.VMEM((rows, kv_cols), jnp.float32),
            pltpu.VMEM((rows, heads_cols), jnp.bfloat16),
            pltpu.SemaphoreType.DMA((3, 8)),
            pltpu.SemaphoreType.DMA((8,)),
        ],
        compiler_params=pltpu.CompilerParams(vmem_limit_bytes=VMEM_LIMIT),
    )(
        sources, targets, gain[None, :], cosines, sines, seg_row[None, :], seg_row[:, None],
        context_grad, q_weight, kv_weight, *blocks,
    )
    return results[0], results[1:]


def line_body(
    source, row_token, seg_ids, stitch_weight, norm_gain, q_weight, kv_weight, o_weight, out_grad
):
    tok_rank = lax.axis_index("tok")
    tp_rank = lax.axis_index("tp")
    packs = lax.axis_size("tok")
    pack_len = seg_ids.shape[1]
    width = q_weight.shape[0]
    own_cols = stitch_weight.shape[1]
    repeat = (q_weight.shape[1] // HD) // (kv_weight.shape[1] // (2 * HD))
    chip, core = tp_rank // 2, tp_rank % 2

    def chips(tables):
        return jnp.array(tables, jnp.int32)[:, chip]

    def ranks(tables):
        pairs = 2 * chips(tables)
        return jnp.stack([pairs + core, pairs + 1 - core], axis=1).reshape(-1)

    arrival, departure = (STAY, FIRST, SECOND, LAST), (LAST, SECOND, FIRST, STAY)
    sources, targets = ranks(arrival), ranks(departure)

    within = jnp.arange(pack_len, dtype=jnp.int32)
    seg_row = seg_ids[0]
    earlier = jnp.sum((seg_row[None, :] < seg_row[:, None]).astype(jnp.int32), axis=1)
    angles = (within - earlier).astype(jnp.float32)[:, None] * frequencies()[None, :]
    cosine, sine = jnp.cos(angles), jnp.sin(angles)
    cosines = jnp.concatenate([cosine, cosine], axis=1)
    sines = jnp.concatenate([-sine, sine], axis=1)

    token_row = row_token.reshape(8, -1)[sources].reshape(1, -1)
    first = gather_begun(source)
    source, (first, token_row) = after(source, (first, token_row))
    rest = gather_rest(source, first)
    early_source = early_blocks(source, first)
    early_product, early_rows = line_stitched_early(early_source, stitch_weight)
    out_grad, (rest, early_product) = after(out_grad, (rest, early_product))
    late_source = late_blocks(rest)
    grad_first = gather_begun(out_grad)
    placed, late_rows = line_stitched(
        packs, pack_len, tok_rank, token_row, early_product, late_source, stitch_weight
    )
    received = [swapped(placed[distance], "tok", distance) for distance in range(1, packs)]
    received[0], grad_first = after(received[0], grad_first)
    grad_rest = gather_rest(out_grad, grad_first)
    hidden = placed[0].astype(jnp.float32)
    for part in received:
        hidden += part.astype(jnp.float32)
    hidden_bf = hidden.astype(jnp.bfloat16)
    hidden_first = gather_begun(hidden_bf)
    (hidden_bf, hidden_first), grad_rest = after((hidden_bf, hidden_first), grad_rest)
    hidden_rest = gather_rest(hidden_bf, hidden_first)
    grad_blocks = early_blocks(out_grad, grad_first) + late_blocks(grad_rest)
    grad_context = line_grad_context(chips(arrival), core, grad_blocks, o_weight)
    hidden_rest, grad_context = after(hidden_rest, grad_context)
    hidden_blocks = early_blocks(hidden_bf, hidden_first) + late_blocks(hidden_rest)

    context, grad_parts = line_middle(
        repeat, sources, targets, hidden_blocks, norm_gain, q_weight, kv_weight, cosines, sines,
        seg_row, grad_context,
    )
    grad_own, grad_second, grad_first = line_scatter(grad_parts)
    attended_parts = line_attended(chips(departure), core, context, o_weight)
    attended_parts, grad_second = after(attended_parts, grad_second)
    grad_hidden = (
        out_grad.astype(jnp.float32) + line_total(grad_own, grad_second, grad_first)
    ).astype(jnp.bfloat16)
    every_pack = [grad_hidden] + [
        swapped(grad_hidden, "tok", distance) for distance in range(1, packs)
    ]
    token_order = (
        (tok_rank ^ jnp.arange(packs, dtype=jnp.int32))[:, None] * pack_len + within[None, :]
    ).reshape(-1)
    order = (token_row.reshape(-1, 1) == token_order[None, :]).astype(jnp.bfloat16)
    half = early_rows.shape[0]
    tokens_last = (
        dot_f32(early_rows, order[:half], COLS_BY_COLS)
        + dot_f32(late_rows, order[half:], COLS_BY_COLS)
    ).astype(jnp.bfloat16)
    attended = line_scatter(attended_parts)
    late_hidden, *every_pack = lax.optimization_barrier((hidden_bf, *every_pack))
    stitch_grad = outer_summed(tokens_last, every_pack)
    attended = line_total(*attended)
    layer_out = (late_hidden.astype(jnp.float32) + attended).astype(jnp.bfloat16)
    return (layer_out, stitch_grad)


def body(
    source, row_token, seg_ids, stitch_weight, norm_gain, q_weight, kv_weight, o_weight, out_grad
):
    tok_rank = lax.axis_index("tok")
    tp_rank = lax.axis_index("tp")
    packs = lax.axis_size("tok")
    pack_len = seg_ids.shape[1]
    width = q_weight.shape[0]
    own_cols = stitch_weight.shape[1]
    own_gain = lax.dynamic_slice_in_dim(norm_gain, tp_rank * own_cols, own_cols)

    gathered = lax.all_gather(source, "tp", axis=0, tiled=True)
    placed = stitched(packs, pack_len, tok_rank, row_token, gathered, stitch_weight)
    within = jnp.arange(pack_len, dtype=jnp.int32)
    hidden = placed[0].astype(jnp.float32)
    for distance in range(1, packs):
        hidden += swapped(placed[distance], "tok", distance).astype(jnp.float32)
    hidden_bf = hidden.astype(jnp.bfloat16)
    hidden_f = hidden_bf.astype(jnp.float32)
    square_sum = summed(jnp.sum(hidden_f * hidden_f, axis=1), "tp")
    inv_rms = lax.rsqrt(square_sum / width + epsilon)[:, None]
    gained = lax.all_gather((hidden_f * own_gain).astype(jnp.bfloat16), "tp", axis=1, tiled=True)

    token_order = (
        (tok_rank ^ jnp.arange(packs, dtype=jnp.int32))[:, None] * pack_len + within[None, :]
    ).reshape(-1)
    order = (row_token[:, None] == token_order[None, :]).astype(jnp.bfloat16)
    tokens_last = dot_f32(gathered, order, COLS_BY_COLS).astype(jnp.bfloat16)

    seg_row = seg_ids[0]
    earlier = jnp.sum((seg_row[None, :] < seg_row[:, None]).astype(jnp.int32), axis=1)
    angles = (within - earlier).astype(jnp.float32)[:, None] * frequencies()[None, :]
    cosine, sine = jnp.cos(angles), jnp.sin(angles)
    cosines = jnp.concatenate([cosine, cosine], axis=1)
    sines = jnp.concatenate([-sine, sine], axis=1)
    local_heads = q_weight.shape[1] // HD
    kv_cols = kv_weight.shape[1]
    paired = kv_cols == HD
    kv_local = 1 if paired else kv_cols // (2 * HD)
    repeat = local_heads // kv_local
    every_grad = lax.all_gather(out_grad, "tp", axis=1, tiled=True)
    grad_context = lax.dot_general(
        every_grad, o_weight, (((1,), (1,)), ((), ())), preferred_element_type=jnp.float32
    ).astype(jnp.bfloat16)
    if paired:
        query_pre = jnp.dot(gained, q_weight, preferred_element_type=jnp.float32)
        projected = jnp.dot(gained, kv_weight, preferred_element_type=jnp.float32) * inv_rms
        is_key = tp_rank % 2 == 0
        own_part = jnp.where(is_key, rotate(projected, cosine, sine), projected).astype(
            jnp.bfloat16
        )
        partner = swapped(own_part, "tp", 1)
        keys = jnp.where(is_key, own_part, partner)
        values = jnp.where(is_key, partner, own_part)
        context, grad_queries, key_part, value_part, aligned = attention_parts(
            repeat, query_pre, inv_rms, cosines, sines, seg_row, keys, values, grad_context
        )
        outgoing = jnp.where(is_key, value_part, key_part)
        incoming = swapped(outgoing.astype(jnp.bfloat16), "tp", 1).astype(outgoing.dtype)
        own_sum = jnp.where(is_key, key_part, value_part) + incoming
        grad_pairs = jnp.where(is_key, unrotate(own_sum, cosine, sine), own_sum).astype(
            jnp.bfloat16
        )
        aligned += jnp.sum(grad_pairs.astype(jnp.float32) * projected, axis=1, keepdims=True)
        grad_normed = back_projected(grad_queries, grad_pairs, q_weight, kv_weight)
    else:
        context, aligned, grad_normed = middle(
            repeat, gained, q_weight, kv_weight, inv_rms, cosines, sines, seg_row, grad_context
        )
    aligned = summed(aligned[:, 0], "tp")[:, None]
    grad_sum = lax.psum_scatter(grad_normed, "tp", scatter_dimension=1, tiled=True)
    attended = jnp.dot(context, o_weight, preferred_element_type=jnp.float32).astype(jnp.bfloat16)
    attended, grad_sum = lax.optimization_barrier((attended, grad_sum))
    grad_hidden = (
        out_grad.astype(jnp.float32)
        + inv_rms * own_gain * grad_sum.astype(jnp.float32)
        - hidden_f * (inv_rms * inv_rms * aligned / width)
    ).astype(jnp.bfloat16)
    every_pack = [grad_hidden] + [
        swapped(grad_hidden, "tok", distance) for distance in range(1, packs)
    ]
    late_hidden, *every_pack = lax.optimization_barrier((hidden_bf, *every_pack))
    stitch_grad = outer_summed(tokens_last, every_pack)

    attended = lax.psum_scatter(attended, "tp", scatter_dimension=1, tiled=True)
    layer_out = (late_hidden.astype(jnp.float32) + attended.astype(jnp.float32)).astype(
        jnp.bfloat16
    )
    return (layer_out, stitch_grad)


def solution(mesh):
    placed = (
        P("tp", "tok"),
        P(),
        P("tok", None),
        P("tok", "tp"),
        P(),
        P(None, "tp"),
        P(None, "tp"),
        P("tp", None),
        P("tok", "tp"),
    )
    on_line = mesh.shape["tp"] == 8
    return jax.shard_map(
        line_body if on_line else body,
        mesh=mesh,
        in_specs=placed,
        out_specs=(P("tok", "tp"), P("tok", "tp")),
        check_vma=False,
    )
```

```python
import functools
import math

import jax
import jax.numpy as jnp
from jax import lax
from jax.experimental import pallas as pl
from jax.experimental.pallas import tpu as pltpu
from jax.sharding import PartitionSpec as P

HD = 128


epsilon = 1e-05


def swapped(value, axis, mask):
    pairs = [(source, source ^ mask) for source in range(lax.axis_size(axis))]
    return lax.ppermute(value, axis, pairs)


def summed(value, axis):
    mask = 1
    while mask < lax.axis_size(axis):
        value = value + swapped(value, axis, mask)
        mask *= 2
    return value


def frequencies():
    exponent = jnp.arange(0, HD, 2).astype(jnp.float32) / HD
    plain_rate = 500000.0 ** (-exponent)
    wavelength = 2.0 * math.pi / plain_rate
    smoothing = (8192.0 / wavelength - 1.0) / 3.0
    blended = (1.0 - smoothing) * plain_rate / 8.0 + smoothing * plain_rate
    return jnp.where(
        wavelength < 2048.0, plain_rate, jnp.where(wavelength > 8192.0, plain_rate / 8.0, blended)
    )


def rotate(vector_in, cosine_table, sine_table):
    half_size = vector_in.shape[-1] // 2
    first_half = vector_in[..., :half_size]
    second = vector_in[..., half_size:]
    return jnp.concatenate(
        [
            first_half * cosine_table - second * sine_table,
            second * cosine_table + first_half * sine_table,
        ],
        axis=-1,
    )


def unrotate(vector_in, cosine_table, sine_table):
    return rotate(vector_in, cosine_table, -sine_table)


VMEM_LIMIT = 56 * 2**20
ROWS_BY_ROWS = (((1,), (1,)), ((), ()))
COLS_BY_COLS = (((0,), (0,)), ((), ()))


def dot_f32(left, right, dims=(((1,), (0,)), ((), ()))):
    return lax.dot_general(left, right, dims, preferred_element_type=jnp.float32)


def attend(
    repeat, read_query, cosines, sines, seg_row, seg_col, keys, values, grad_ref, context_ref,
    query_grad_ref,
):
    rows = cosines.shape[0]
    score_scale = 1.0 / math.sqrt(HD)
    later = lax.broadcasted_iota(jnp.int32, (rows, rows), 0)
    sooner = lax.broadcasted_iota(jnp.int32, (rows, rows), 1)
    allowed = (seg_col == seg_row) & (sooner <= later)
    aligned = jnp.zeros((rows, HD), jnp.float32)
    key_parts, value_parts = [], []
    for group in range(len(keys)):
        key_part = jnp.zeros((rows, HD), jnp.float32)
        value_part = jnp.zeros((rows, HD), jnp.float32)
        for member in range(repeat):
            own = pl.ds((group * repeat + member) * HD, HD)
            plain = read_query(own)
            query = turn(plain, cosines, sines).astype(jnp.bfloat16)
            scores = dot_f32(query, keys[group], ROWS_BY_ROWS) * score_scale
            scores = jnp.where(allowed, scores, -1e30)
            exponents = jnp.exp(scores - jnp.max(scores, axis=1, keepdims=True))
            attention = exponents / jnp.sum(exponents, axis=1, keepdims=True)
            attention_bf = attention.astype(jnp.bfloat16)
            context_ref[:, own] = dot_f32(attention_bf, values[group]).astype(jnp.bfloat16)
            context_grad = grad_ref[:, own]
            grad_probs = dot_f32(context_grad, values[group], ROWS_BY_ROWS)
            mean = jnp.sum(grad_probs * attention, axis=1, keepdims=True)
            score_grad = (attention * (grad_probs - mean) * score_scale).astype(jnp.bfloat16)
            query_grad = turn(dot_f32(score_grad, keys[group]), cosines, -sines).astype(
                jnp.bfloat16
            )
            query_grad_ref[:, own] = query_grad
            aligned += query_grad.astype(jnp.float32) * plain
            key_part += dot_f32(score_grad, query, COLS_BY_COLS)
            value_part += dot_f32(attention_bf, context_grad, COLS_BY_COLS)
        key_parts.append(key_part)
        value_parts.append(value_part)
    return aligned, key_parts, value_parts


def turn(vector_in, cosines, sines):
    return vector_in * cosines + pltpu.roll(vector_in, HD // 2, 1) * sines


def attention_kernel(
    repeat, query_ref, scale_ref, cos_ref, sin_ref, seg_row_ref, seg_col_ref, key_ref, value_ref,
    grad_ref, context_ref, query_grad_ref, key_part_ref, value_part_ref, aligned_ref,
):
    row_scale = scale_ref[...]
    groups = [pl.ds(group * HD, HD) for group in range(key_ref.shape[1] // HD)]
    aligned, key_parts, value_parts = attend(
        repeat, lambda own: query_ref[:, own] * row_scale, cos_ref[...], sin_ref[...],
        seg_row_ref[...], seg_col_ref[...], [key_ref[:, shared] for shared in groups],
        [value_ref[:, shared] for shared in groups], grad_ref, context_ref, query_grad_ref,
    )
    for shared, key_part, value_part in zip(groups, key_parts, value_parts):
        key_part_ref[:, shared] = key_part
        value_part_ref[:, shared] = value_part
    aligned_ref[...] = jnp.sum(aligned, axis=1, keepdims=True)


def attention_parts(repeat, query_pre, inv_rms, cosines, sines, seg_row, keys, values, context_grad):
    rows = query_pre.shape[0]
    whole = pl.BlockSpec(memory_space=pltpu.VMEM)
    return pl.pallas_call(
        functools.partial(attention_kernel, repeat),
        in_specs=[whole] * 9,
        out_specs=[whole] * 5,
        out_shape=[
            jax.ShapeDtypeStruct(query_pre.shape, jnp.bfloat16),
            jax.ShapeDtypeStruct(query_pre.shape, jnp.bfloat16),
            jax.ShapeDtypeStruct(keys.shape, jnp.float32),
            jax.ShapeDtypeStruct(keys.shape, jnp.float32),
            jax.ShapeDtypeStruct((rows, 1), jnp.float32),
        ],
        compiler_params=pltpu.CompilerParams(vmem_limit_bytes=VMEM_LIMIT),
    )(
        query_pre, inv_rms, cosines, sines, seg_row[None, :], seg_row[:, None], keys, values,
        context_grad,
    )


def middle_kernel(
    repeat, gained_ref, q_weight_ref, kv_weight_ref, scale_ref, cos_ref, sin_ref, seg_row_ref,
    seg_col_ref, grad_ref, context_ref, aligned_ref, out_ref, gained, q_weight, kv_weight, out,
    query_sum, pair_sum, query_grad, sems,
):
    width, heads_cols = q_weight.shape
    pieces = sems.shape[1]
    step = width // pieces

    def part(piece):
        return pl.ds(pl.multiple_of(piece * step, step), step)

    def fetches(piece):
        span = part(piece)
        return (
            pltpu.make_async_copy(
                gained_ref.at[:, span], gained.at[:, span], sems.at[0, piece]
            ),
            pltpu.make_async_copy(q_weight_ref.at[span], q_weight.at[span], sems.at[1, piece]),
            pltpu.make_async_copy(kv_weight_ref.at[span], kv_weight.at[span], sems.at[2, piece]),
        )

    def returned(piece):
        span = part(piece)
        return pltpu.make_async_copy(out.at[:, span], out_ref.at[:, span], sems.at[3, piece])

    @pl.loop(0, pieces)
    def _(piece):
        for fetch in fetches(piece):
            fetch.start()

    query_sum[...] = jnp.zeros_like(query_sum)
    pair_sum[...] = jnp.zeros_like(pair_sum)

    @pl.loop(0, pieces)
    def _(piece):
        for fetch in fetches(piece):
            fetch.wait()
        span = part(piece)
        features = gained[:, span]
        query_sum[...] += dot_f32(features, q_weight[span, :])
        pair_sum[...] += dot_f32(features, kv_weight[span, :])

    row_scale = scale_ref[...]
    cosines, sines = cos_ref[...], sin_ref[...]
    groups = kv_weight.shape[1] // (2 * HD)
    pair_plain = pair_sum[...] * row_scale
    halves = [pair_plain[:, i * HD : (i + 1) * HD] for i in range(2 * groups)]
    aligned, key_parts, value_parts = attend(
        repeat, lambda own: query_sum[:, own] * row_scale, cosines, sines, seg_row_ref[...],
        seg_col_ref[...], [turn(half, cosines, sines).astype(jnp.bfloat16) for half in halves[::2]],
        [half.astype(jnp.bfloat16) for half in halves[1::2]], grad_ref, context_ref, query_grad,
    )
    pair_grads = []
    for key_part, value_part in zip(key_parts, value_parts):
        pair_grads.append(turn(key_part, cosines, -sines).astype(jnp.bfloat16))
        pair_grads.append(value_part.astype(jnp.bfloat16))
    for half, pair_grad in zip(halves, pair_grads):
        aligned += half * pair_grad.astype(jnp.float32)
    aligned_ref[...] = jnp.sum(aligned, axis=1, keepdims=True)
    pair_grad = jnp.concatenate(pair_grads, axis=1)

    @pl.loop(0, pieces)
    def _(piece):
        span = part(piece)
        out[:, span] = (
            dot_f32(query_grad[...], q_weight[span, :], ROWS_BY_ROWS)
            + dot_f32(pair_grad, kv_weight[span, :], ROWS_BY_ROWS)
        ).astype(out.dtype)
        returned(piece).start()

    @pl.loop(0, pieces)
    def _(piece):
        returned(piece).wait()


def middle(
    repeat, gained, q_weight, kv_weight, inv_rms, cosines, sines, seg_row, context_grad
):
    rows, width = gained.shape
    heads_cols, kv_cols = q_weight.shape[1], kv_weight.shape[1]
    whole, far = pl.BlockSpec(memory_space=pltpu.VMEM), pl.BlockSpec(memory_space=pl.ANY)
    return pl.pallas_call(
        functools.partial(middle_kernel, repeat),
        in_specs=[far] * 3 + [whole] * 6,
        out_specs=[whole] * 2 + [far],
        out_shape=[
            jax.ShapeDtypeStruct((rows, heads_cols), jnp.bfloat16),
            jax.ShapeDtypeStruct((rows, 1), jnp.float32),
            jax.ShapeDtypeStruct((rows, width), jnp.bfloat16),
        ],
        scratch_shapes=[
            pltpu.VMEM(gained.shape, jnp.bfloat16),
            pltpu.VMEM(q_weight.shape, jnp.bfloat16),
            pltpu.VMEM(kv_weight.shape, jnp.bfloat16),
            pltpu.VMEM(gained.shape, jnp.bfloat16),
            pltpu.VMEM((rows, heads_cols), jnp.float32),
            pltpu.VMEM((rows, kv_cols), jnp.float32),
            pltpu.VMEM((rows, heads_cols), jnp.bfloat16),
            pltpu.SemaphoreType.DMA((4, 8)),
        ],
        compiler_params=pltpu.CompilerParams(vmem_limit_bytes=VMEM_LIMIT),
    )(
        gained, q_weight, kv_weight, inv_rms, cosines, sines, seg_row[None, :], seg_row[:, None],
        context_grad,
    )


def stitch_kernel(packs, rank_ref, token_ref, source_ref, weight_ref, *refs):
    out_refs, product = refs[:packs], refs[-1]
    block = source_ref.shape[0]
    step = pl.program_id(0)
    here = pl.ds(pl.multiple_of(step * block, block), block)
    product[here, :] = dot_f32(source_ref[...], weight_ref[...]).astype(jnp.bfloat16)

    @pl.when(step == pl.num_programs(0) - 1)
    def _():
        pack_len = out_refs[0].shape[0]
        shape = (pack_len, product.shape[0])
        place = token_ref[...] - lax.broadcasted_iota(jnp.int32, shape, 0)
        for distance in range(packs):
            first = (rank_ref[0] ^ distance) * pack_len
            rows = (place == first).astype(jnp.float32).astype(jnp.bfloat16)
            out_refs[distance][...] = dot_f32(rows, product[...]).astype(jnp.bfloat16)


def stitched(packs, pack_len, rank, row_token, source, weight):
    rows, features = source.shape
    cols = weight.shape[1]
    block = min(512, rows)
    fixed = lambda i: (0, 0)
    return pl.pallas_call(
        functools.partial(stitch_kernel, packs),
        grid=(rows // block,),
        in_specs=[
            pl.BlockSpec(memory_space=pltpu.SMEM),
            pl.BlockSpec((1, rows), fixed),
            pl.BlockSpec((block, features), lambda i: (i, 0)),
            pl.BlockSpec(weight.shape, fixed),
        ],
        out_specs=[pl.BlockSpec((pack_len, cols), fixed)] * packs,
        out_shape=[jax.ShapeDtypeStruct((pack_len, cols), jnp.bfloat16)] * packs,
        scratch_shapes=[pltpu.VMEM((rows, cols), jnp.bfloat16)],
        compiler_params=pltpu.CompilerParams(vmem_limit_bytes=VMEM_LIMIT),
    )(rank.reshape(1), row_token[None, :], source, weight)


def back_kernel(query_ref, pair_ref, q_weight_ref, kv_weight_ref, out_ref):
    out_ref[...] = (
        dot_f32(query_ref[...], q_weight_ref[...], ROWS_BY_ROWS)
        + dot_f32(pair_ref[...], kv_weight_ref[...], ROWS_BY_ROWS)
    ).astype(out_ref.dtype)


def back_projected(grad_queries, grad_pairs, q_weight, kv_weight):
    rows = grad_queries.shape[0]
    width = q_weight.shape[0]
    block = 2048
    fixed = lambda i: (0, 0)
    return pl.pallas_call(
        back_kernel,
        grid=(width // block,),
        in_specs=[
            pl.BlockSpec(grad_queries.shape, fixed),
            pl.BlockSpec(grad_pairs.shape, fixed),
            pl.BlockSpec((block, q_weight.shape[1]), lambda i: (i, 0)),
            pl.BlockSpec((block, kv_weight.shape[1]), lambda i: (i, 0)),
        ],
        out_specs=pl.BlockSpec((rows, block), lambda i: (0, i)),
        out_shape=jax.ShapeDtypeStruct((rows, width), jnp.bfloat16),
        compiler_params=pltpu.CompilerParams(vmem_limit_bytes=VMEM_LIMIT),
    )(grad_queries, grad_pairs, q_weight, kv_weight)


def outer_kernel(*refs):
    features_ref, out_ref = refs[0], refs[-1]
    total = None
    for place, grad_ref in enumerate(refs[1:-1]):
        rows = grad_ref.shape[0]
        term = dot_f32(features_ref[:, pl.ds(place * rows, rows)], grad_ref[...])
        total = term if total is None else total + term
    out_ref[...] = total


def outer_summed(features, grads):
    block = min(512, features.shape[0])
    cols = grads[0].shape[1]
    return pl.pallas_call(
        outer_kernel,
        grid=(features.shape[0] // block,),
        in_specs=[pl.BlockSpec((block, features.shape[1]), lambda i: (i, 0))]
        + [pl.BlockSpec(grad.shape, lambda i: (0, 0)) for grad in grads],
        out_specs=pl.BlockSpec((block, cols), lambda i: (i, 0)),
        out_shape=jax.ShapeDtypeStruct((features.shape[0], cols), jnp.float32),
        compiler_params=pltpu.CompilerParams(vmem_limit_bytes=VMEM_LIMIT),
    )(features, *grads)


STAY, FIRST, SECOND, LAST = (0, 1, 2, 3), (1, 3, 0, 2), (2, 0, 3, 1), (3, 2, 1, 0)


OUTWARD = [(0, 1), (1, 0), (2, 3), (3, 2)]
INSIDE = [(0, 1), (1, 0), (2, 4), (3, 5), (4, 2), (5, 3), (6, 7), (7, 6)]


def is_inner():
    chip = lax.axis_index("tp") // 2
    return (chip == 1) | (chip == 2)


def along(value, pairs):
    both = [(2 * start + core, 2 * end + core) for start, end in pairs for core in range(2)]
    return lax.ppermute(value, "tp", both)


def towards(table):
    return [(start, end) for start, end in enumerate(table)]


def arriving(table):
    return [(start, end) for end, start in enumerate(table)]


def after(value, done):
    value, done = lax.optimization_barrier((value, done))
    return value, done


def gather_begun(block):
    return along(block, arriving(FIRST))


def gather_second(block):
    return along(block, arriving(SECOND))


def gather_last(block, first):
    return along(first, OUTWARD), lax.ppermute(block, "tp", INSIDE)


def early_blocks(block, first):
    return [block, swapped(block, "tp", 1), first, swapped(first, "tp", 1)]


def late_blocks(second, last):
    far, near = last
    last = jnp.where(is_inner(), near, far)
    return [second, swapped(second, "tp", 1), last, swapped(last, "tp", 1)]


def both_cores(parts, place):
    other = swapped(parts[2 * place + 1], "tp", 1)
    return parts[2 * place].astype(jnp.float32) + other.astype(jnp.float32)


def scatter_begun(parts):
    last = both_cores(parts, 0).astype(jnp.bfloat16)
    return last, along(last, OUTWARD), lax.ppermute(last, "tp", INSIDE)


def scatter_second(parts):
    return along(both_cores(parts, 1).astype(jnp.bfloat16), towards(SECOND))


def scatter_first(parts, far):
    first = both_cores(parts, 2)
    first += jnp.where(is_inner(), far.astype(jnp.float32), 0.0)
    return along(first.astype(jnp.bfloat16), towards(FIRST))


def scatter_total(parts, near, second, first):
    total = both_cores(parts, 3) + jnp.where(is_inner(), near.astype(jnp.float32), 0.0)
    return total + second.astype(jnp.float32) + first.astype(jnp.float32)


def line_stitch_half(blocks, rows, rows_ref, weight_ref, product, here, sems, out_sem):
    block = blocks[0].shape[0]
    fetches = [
        pltpu.make_async_copy(blocks[i], rows.at[pl.ds(i * block, block)], sems.at[i])
        for i in range(4)
    ]
    for fetch in fetches:
        fetch.start()
    for fetch in fetches:
        fetch.wait()
    kept = pltpu.make_async_copy(rows, rows_ref, out_sem)
    kept.start()
    product[here, :] = dot_f32(rows[...], weight_ref[...]).astype(jnp.bfloat16)
    return kept


def line_stitch_early_kernel(weight_ref, *refs):
    blocks, (product_ref, rows_ref, rows, sems, out_sem) = refs[:4], refs[4:]
    everything = pl.ds(0, rows.shape[0])
    line_stitch_half(
        blocks, rows, rows_ref, weight_ref, product_ref, everything, sems, out_sem
    ).wait()


def line_stitch_kernel(packs, rank_ref, token_ref, weight_ref, early_ref, *refs):
    blocks, out_refs = refs[:4], refs[4 : 4 + packs]
    rows_ref, rows, product, sems, out_sem = refs[4 + packs :]
    half = rows.shape[0]
    kept = line_stitch_half(
        blocks, rows, rows_ref, weight_ref, product, pl.ds(half, half), sems, out_sem
    )
    product[pl.ds(0, half), :] = early_ref[...]
    pack_len = out_refs[0].shape[0]
    place = token_ref[...] - lax.broadcasted_iota(jnp.int32, (pack_len, product.shape[0]), 0)
    for distance in range(packs):
        first = (rank_ref[0] ^ distance) * pack_len
        chosen = (place == first).astype(jnp.float32).astype(jnp.bfloat16)
        out_refs[distance][...] = dot_f32(chosen, product[...]).astype(jnp.bfloat16)
    kept.wait()


def line_stitched_early(blocks, weight):
    block, features = blocks[0].shape
    cols = weight.shape[1]
    whole, far = pl.BlockSpec(memory_space=pltpu.VMEM), pl.BlockSpec(memory_space=pl.ANY)
    return pl.pallas_call(
        line_stitch_early_kernel,
        in_specs=[whole] + [far] * 4,
        out_specs=[whole, far],
        out_shape=[
            jax.ShapeDtypeStruct((4 * block, cols), jnp.bfloat16),
            jax.ShapeDtypeStruct((4 * block, features), jnp.bfloat16),
        ],
        scratch_shapes=[
            pltpu.VMEM((4 * block, features), jnp.bfloat16),
            pltpu.SemaphoreType.DMA((4,)),
            pltpu.SemaphoreType.DMA,
        ],
        compiler_params=pltpu.CompilerParams(vmem_limit_bytes=VMEM_LIMIT),
    )(weight, *blocks)


def line_stitched(packs, pack_len, rank, token_row, early, blocks, weight):
    block, features = blocks[0].shape
    cols = weight.shape[1]
    whole, far = pl.BlockSpec(memory_space=pltpu.VMEM), pl.BlockSpec(memory_space=pl.ANY)
    results = pl.pallas_call(
        functools.partial(line_stitch_kernel, packs),
        in_specs=[pl.BlockSpec(memory_space=pltpu.SMEM)] + [whole] * 3 + [far] * 4,
        out_specs=[whole] * packs + [far],
        out_shape=[jax.ShapeDtypeStruct((pack_len, cols), jnp.bfloat16)] * packs
        + [jax.ShapeDtypeStruct((4 * block, features), jnp.bfloat16)],
        scratch_shapes=[
            pltpu.VMEM((4 * block, features), jnp.bfloat16),
            pltpu.VMEM((8 * block, cols), jnp.bfloat16),
            pltpu.SemaphoreType.DMA((4,)),
            pltpu.SemaphoreType.DMA,
        ],
        compiler_params=pltpu.CompilerParams(vmem_limit_bytes=VMEM_LIMIT),
    )(rank.reshape(1), token_row, weight, early, *blocks)
    return results[:packs], results[packs]


def line_grad_kernel(chips_ref, core_ref, weight_ref, *refs):
    blocks, out_ref, features, total, sems = refs[:8], *refs[8:]
    step = pl.program_id(0)
    cols = blocks[0].shape[1]

    def fetch(place, half):
        core = core_ref[0] if half == 0 else 1 - core_ref[0]
        there = features.at[place, :, pl.ds(pl.multiple_of(core * cols, cols), cols)]
        return there, sems.at[place, half]

    @pl.when(step == 0)
    def _():
        for i in range(8):
            pltpu.make_async_copy(blocks[i], *fetch(i // 2, i % 2)).start()
        total[...] = jnp.zeros_like(total)

    for half in range(2):
        pltpu.make_async_copy(blocks[half], *fetch(step, half)).wait()
    total[...] += dot_f32(features[step], weight_ref[...], ROWS_BY_ROWS)

    @pl.when(step == 3)
    def _():
        out_ref[...] = total[...].astype(out_ref.dtype)


def line_grad_context(chips, core, blocks, weight):
    rows, cols = blocks[0].shape
    heads_cols = weight.shape[0]
    far = pl.BlockSpec(memory_space=pl.ANY)
    return pl.pallas_call(
        line_grad_kernel,
        grid_spec=pltpu.PrefetchScalarGridSpec(
            num_scalar_prefetch=2,
            grid=(4,),
            in_specs=[pl.BlockSpec((heads_cols, 2 * cols), lambda i, chips, core: (0, chips[i]))]
            + [far] * 8,
            out_specs=pl.BlockSpec((rows, heads_cols), lambda i, chips, core: (0, 0)),
            scratch_shapes=[
                pltpu.VMEM((4, rows, 2 * cols), jnp.bfloat16),
                pltpu.VMEM((rows, heads_cols), jnp.float32),
                pltpu.SemaphoreType.DMA((4, 2)),
            ],
        ),
        out_shape=jax.ShapeDtypeStruct((rows, heads_cols), jnp.bfloat16),
        compiler_params=pltpu.CompilerParams(vmem_limit_bytes=VMEM_LIMIT),
    )(chips, core.reshape(1), weight, *blocks)


def line_attended_kernel(chips_ref, core_ref, context_ref, weight_ref, *refs):
    out_refs, product = refs[:8], refs[8]
    step = pl.program_id(0)
    cols = out_refs[0].shape[1]
    product[...] = dot_f32(context_ref[...], weight_ref[...]).astype(jnp.bfloat16)
    for i in range(4):

        @pl.when(step == i)
        def _(i=i):
            for half in range(2):
                core = core_ref[0] if half == 0 else 1 - core_ref[0]
                here = pl.ds(pl.multiple_of(core * cols, cols), cols)
                out_refs[2 * i + half][...] = product[:, here]


def line_attended(chips, core, context, weight):
    rows, heads_cols = context.shape
    cols = weight.shape[1] // 8
    fixed = lambda i, chips, core: (0, 0)
    return pl.pallas_call(
        line_attended_kernel,
        grid_spec=pltpu.PrefetchScalarGridSpec(
            num_scalar_prefetch=2,
            grid=(4,),
            in_specs=[
                pl.BlockSpec((rows, heads_cols), fixed),
                pl.BlockSpec((heads_cols, 2 * cols), lambda i, chips, core: (0, chips[i])),
            ],
            out_specs=[pl.BlockSpec((rows, cols), fixed)] * 8,
            scratch_shapes=[pltpu.VMEM((rows, 2 * cols), jnp.bfloat16)],
        ),
        out_shape=[jax.ShapeDtypeStruct((rows, cols), jnp.bfloat16)] * 8,
        compiler_params=pltpu.CompilerParams(vmem_limit_bytes=VMEM_LIMIT),
    )(chips, core.reshape(1), context, weight)


def line_project(
    places, from_ref, gain_ref, q_weight_ref, kv_weight_ref, blocks, hidden, q_weight, kv_weight,
    sems, query_sum, pair_sum, squares,
):
    rows, step = blocks[0].shape

    def part(place):
        return pl.ds(pl.multiple_of(from_ref[place] * step, step), step)

    def fetches(place):
        span = part(place)
        return (
            pltpu.make_async_copy(q_weight_ref.at[span], q_weight.at[span], sems.at[1, place]),
            pltpu.make_async_copy(kv_weight_ref.at[span], kv_weight.at[span], sems.at[2, place]),
        )

    def features(place):
        return pltpu.make_async_copy(blocks[0], hidden.at[place], sems.at[0, place])

    later = [place for place in range(len(blocks)) if place not in places]
    for place in [*places, *later]:
        pltpu.make_async_copy(blocks[place], hidden.at[place], sems.at[0, place]).start()
        for fetch in fetches(place):
            fetch.start()

    def project(place, squares):
        features(place).wait()
        for fetch in fetches(place):
            fetch.wait()
        span = part(place)
        wide = hidden[place].astype(jnp.float32)
        gained = (wide * gain_ref[:, span]).astype(jnp.bfloat16)
        query_sum[...] += dot_f32(gained, q_weight[span, :])
        pair_sum[...] += dot_f32(gained, kv_weight[span, :])
        return squares + jnp.sum(wide * wide, axis=1, keepdims=True)

    squares = lax.fori_loop(places[0], places[-1] + 1, project, squares)

    def finish():
        for place in later:
            features(place).wait()
            for fetch in fetches(place):
                fetch.wait()

    return squares, finish


def line_projected_kernel(
    from_ref, gain_ref, q_weight_ref, kv_weight_ref, *refs,
):
    blocks, (query_sum, pair_sum, squares_ref) = refs[:4], refs[4:7]
    hidden, q_weight, kv_weight, sems = refs[7:]
    query_sum[...] = jnp.zeros_like(query_sum)
    pair_sum[...] = jnp.zeros_like(pair_sum)
    squares, _ = line_project(
        range(4), from_ref, gain_ref, q_weight_ref, kv_weight_ref, blocks, hidden, q_weight,
        kv_weight, sems, query_sum, pair_sum, jnp.zeros(squares_ref.shape, jnp.float32),
    )
    squares_ref[...] = squares


def line_projected(sources, blocks, gain, q_weight, kv_weight):
    rows, step = blocks[0].shape
    heads_cols, kv_cols = q_weight.shape[1], kv_weight.shape[1]
    whole, far = pl.BlockSpec(memory_space=pltpu.VMEM), pl.BlockSpec(memory_space=pl.ANY)
    return pl.pallas_call(
        line_projected_kernel,
        in_specs=[pl.BlockSpec(memory_space=pltpu.SMEM), whole] + [far] * 6,
        out_specs=[whole] * 3,
        out_shape=[
            jax.ShapeDtypeStruct((rows, heads_cols), jnp.float32),
            jax.ShapeDtypeStruct((rows, kv_cols), jnp.float32),
            jax.ShapeDtypeStruct((rows, 1), jnp.float32),
        ],
        scratch_shapes=[
            pltpu.VMEM((4, rows, step), jnp.bfloat16),
            pltpu.VMEM(q_weight.shape, jnp.bfloat16),
            pltpu.VMEM(kv_weight.shape, jnp.bfloat16),
            pltpu.SemaphoreType.DMA((3, 4)),
        ],
        compiler_params=pltpu.CompilerParams(vmem_limit_bytes=VMEM_LIMIT),
    )(sources, gain[None, :], q_weight, kv_weight, *blocks)


def line_tokens_kernel(token_ref, order_ref, early_ref, late_ref, out_ref):
    half = early_ref.shape[0]
    total = None
    for place, rows_ref in enumerate((early_ref, late_ref)):
        tokens = token_ref[pl.ds(place * half, half), :]
        chosen = (tokens == order_ref[...]).astype(jnp.float32).astype(jnp.bfloat16)
        term = dot_f32(rows_ref[...], chosen, COLS_BY_COLS)
        total = term if total is None else total + term
    out_ref[...] = total.astype(out_ref.dtype)


def line_tokens_last(token_col, token_order, early_rows, late_rows):
    half, features = early_rows.shape
    tokens = token_order.shape[1]
    block = min(1024, features)
    fixed = lambda i: (0, 0)
    return pl.pallas_call(
        line_tokens_kernel,
        grid=(features // block,),
        in_specs=[
            pl.BlockSpec((2 * half, 1), fixed),
            pl.BlockSpec((1, tokens), fixed),
            pl.BlockSpec((half, block), lambda i: (0, i)),
            pl.BlockSpec((half, block), lambda i: (0, i)),
        ],
        out_specs=pl.BlockSpec((block, tokens), lambda i: (i, 0)),
        out_shape=jax.ShapeDtypeStruct((features, tokens), jnp.bfloat16),
        compiler_params=pltpu.CompilerParams(vmem_limit_bytes=VMEM_LIMIT),
    )(token_col, token_order, early_rows, late_rows)


def line_middle_kernel(
    repeat, from_ref, to_ref, gain_ref, cos_ref, sin_ref, seg_row_ref, seg_col_ref, grad_ref,
    early_query_ref, early_pair_ref, early_squares_ref, q_weight_ref, kv_weight_ref, *refs,
):
    blocks, context_ref, out_refs = refs[:8], refs[8], refs[9:17]
    hidden, q_weight, kv_weight, out, query_sum, pair_sum, query_grad, sems, out_sems = refs[17:]
    width = q_weight.shape[0]
    rows, step = blocks[0].shape

    def part(rank):
        return pl.ds(pl.multiple_of(rank * step, step), step)

    query_sum[...] = early_query_ref[...]
    pair_sum[...] = early_pair_ref[...]
    squares, finish = line_project(
        range(4, 8), from_ref, gain_ref, q_weight_ref, kv_weight_ref, blocks, hidden, q_weight,
        kv_weight, sems, query_sum, pair_sum, early_squares_ref[...],
    )
    row_scale = lax.rsqrt(squares / width + epsilon)
    cosines, sines = cos_ref[...], sin_ref[...]
    groups = kv_weight.shape[1] // (2 * HD)
    pair_plain = pair_sum[...] * row_scale
    halves = [pair_plain[:, i * HD : (i + 1) * HD] for i in range(2 * groups)]
    aligned, key_parts, value_parts = attend(
        repeat, lambda own: query_sum[:, own] * row_scale, cosines, sines, seg_row_ref[...],
        seg_col_ref[...], [turn(half, cosines, sines).astype(jnp.bfloat16) for half in halves[::2]],
        [half.astype(jnp.bfloat16) for half in halves[1::2]], grad_ref, context_ref, query_grad,
    )
    pair_grads = []
    for key_part, value_part in zip(key_parts, value_parts):
        pair_grads.append(turn(key_part, cosines, -sines).astype(jnp.bfloat16))
        pair_grads.append(value_part.astype(jnp.bfloat16))
    for half, pair_grad in zip(halves, pair_grads):
        aligned += half * pair_grad.astype(jnp.float32)
    aligned = jnp.sum(aligned, axis=1, keepdims=True) * (row_scale * row_scale / width)
    pair_grad = jnp.concatenate(pair_grads, axis=1)
    finish()

    @pl.loop(0, 8)
    def _(place):
        span = part(to_ref[place])
        grad_normed = dot_f32(query_grad[...], q_weight[span, :], ROWS_BY_ROWS)
        grad_normed += dot_f32(pair_grad, kv_weight[span, :], ROWS_BY_ROWS)
        features = hidden[6 - 2 * (place // 2) + place % 2].astype(jnp.float32)
        out[place] = (
            grad_normed * (row_scale * gain_ref[:, span]) - features * aligned
        ).astype(out.dtype)
        for i in range(8):

            @pl.when(place == i)
            def _(i=i):
                pltpu.make_async_copy(out.at[i], out_refs[i], out_sems.at[i]).start()

    for i in range(8):
        pltpu.make_async_copy(out.at[i], out_refs[i], out_sems.at[i]).wait()


def line_middle(
    repeat, sources, targets, blocks, early_sums, gain, q_weight, kv_weight, cosines, sines, seg_row,
    seg_col, context_grad,
):
    rows, step = blocks[0].shape
    heads_cols, kv_cols = q_weight.shape[1], kv_weight.shape[1]
    whole, far = pl.BlockSpec(memory_space=pltpu.VMEM), pl.BlockSpec(memory_space=pl.ANY)
    scalars = pl.BlockSpec(memory_space=pltpu.SMEM)
    results = pl.pallas_call(
        functools.partial(line_middle_kernel, repeat),
        in_specs=[scalars] * 2 + [whole] * 9 + [far] * 10,
        out_specs=[whole] + [far] * 8,
        out_shape=[jax.ShapeDtypeStruct((rows, heads_cols), jnp.bfloat16)]
        + [jax.ShapeDtypeStruct((rows, step), jnp.bfloat16)] * 8,
        scratch_shapes=[
            pltpu.VMEM((8, rows, step), jnp.bfloat16),
            pltpu.VMEM(q_weight.shape, jnp.bfloat16),
            pltpu.VMEM(kv_weight.shape, jnp.bfloat16),
            pltpu.VMEM((8, rows, step), jnp.bfloat16),
            pltpu.VMEM((rows, heads_cols), jnp.float32),
            pltpu.VMEM((rows, kv_cols), jnp.float32),
            pltpu.VMEM((rows, heads_cols), jnp.bfloat16),
            pltpu.SemaphoreType.DMA((3, 8)),
            pltpu.SemaphoreType.DMA((8,)),
        ],
        compiler_params=pltpu.CompilerParams(vmem_limit_bytes=VMEM_LIMIT),
    )(
        sources, targets, gain[None, :], cosines, sines, seg_row[None, :], seg_col,
        context_grad, *early_sums, q_weight, kv_weight, *blocks,
    )
    return results[0], results[1:]


def line_body(
    source, row_token, seg_ids, stitch_weight, norm_gain, q_weight, kv_weight, o_weight, out_grad
):
    tok_rank = lax.axis_index("tok")
    tp_rank = lax.axis_index("tp")
    packs = lax.axis_size("tok")
    pack_len = seg_ids.shape[1]
    width = q_weight.shape[0]
    own_cols = stitch_weight.shape[1]
    repeat = (q_weight.shape[1] // HD) // (kv_weight.shape[1] // (2 * HD))
    chip, core = tp_rank // 2, tp_rank % 2

    def chips(tables):
        return jnp.array(tables, jnp.int32)[:, chip]

    def ranks(tables):
        pairs = 2 * chips(tables)
        return jnp.stack([pairs + core, pairs + 1 - core], axis=1).reshape(-1)

    arrival, departure = (STAY, FIRST, SECOND, LAST), (LAST, SECOND, FIRST, STAY)
    sources, targets = ranks(arrival), ranks(departure)

    within = jnp.arange(pack_len, dtype=jnp.int32)
    seg_row = seg_ids[0]
    earlier = jnp.sum((seg_row[None, :] < seg_row[:, None]).astype(jnp.int32), axis=1)
    angles = (within - earlier).astype(jnp.float32)[:, None] * frequencies()[None, :]
    cosine, sine = jnp.cos(angles), jnp.sin(angles)
    cosines = jnp.concatenate([cosine, cosine], axis=1)
    sines = jnp.concatenate([-sine, sine], axis=1)

    token_row = row_token.reshape(8, -1)[sources].reshape(1, -1)
    first = gather_begun(source)
    seg_col, token_col = seg_row[:, None], token_row.reshape(-1, 1)
    arrivals, departures = chips(arrival), chips(departure)
    small = (token_row, token_col, seg_col, cosines, sines, sources, targets, arrivals, departures)
    source, (first, small) = after(source, (first, small))
    token_row, token_col, seg_col, cosines, sines, sources, targets, arrivals, departures = small
    second, last = gather_second(source), gather_last(source, first)
    early_source = early_blocks(source, first)
    early_product, early_rows = line_stitched_early(early_source, stitch_weight)
    out_grad, (second, last, early_product) = after(out_grad, (second, last, early_product))
    late_source = late_blocks(second, last)
    og_first = gather_begun(out_grad)
    placed, late_rows = line_stitched(
        packs, pack_len, tok_rank, token_row, early_product, late_source, stitch_weight
    )
    received = [swapped(placed[distance], "tok", distance) for distance in range(1, packs)]
    received[0], og_first = after(received[0], og_first)
    og_second, og_last = gather_second(out_grad), gather_last(out_grad, og_first)
    hidden = placed[0].astype(jnp.float32)
    for part in received:
        hidden += part.astype(jnp.float32)
    hidden_bf = hidden.astype(jnp.bfloat16)
    hidden_first = gather_begun(hidden_bf)
    early_rows, hidden_bf = after(early_rows, hidden_bf)
    token_order = (
        (tok_rank ^ jnp.arange(packs, dtype=jnp.int32))[:, None] * pack_len + within[None, :]
    ).reshape(-1)
    tokens_last = line_tokens_last(token_col, token_order[None, :], early_rows, late_rows)
    (hidden_bf, hidden_first), (og_second, og_last, tokens_last) = after(
        (hidden_bf, hidden_first), (og_second, og_last, tokens_last)
    )
    hidden_second, hidden_last = gather_second(hidden_bf), gather_last(hidden_bf, hidden_first)
    og_blocks = early_blocks(out_grad, og_first) + late_blocks(og_second, og_last)
    grad_context = line_grad_context(arrivals, core, og_blocks, o_weight)
    early_hidden = early_blocks(hidden_bf, hidden_first)
    early_sums = line_projected(sources, early_hidden, norm_gain, q_weight, kv_weight)
    hidden_last, (hidden_second, grad_context, early_sums) = after(
        hidden_last, (hidden_second, grad_context, early_sums)
    )
    hidden_blocks = early_hidden + late_blocks(hidden_second, hidden_last)

    context, grad_parts = line_middle(
        repeat, sources, targets, hidden_blocks, early_sums, norm_gain, q_weight, kv_weight,
        cosines, sines, seg_row, seg_col, grad_context,
    )
    last, far, near = scatter_begun(grad_parts)
    context, last = after(context, last)
    attended_parts = line_attended(departures, core, context, o_weight)
    second = scatter_second(grad_parts)
    far, (near, attended_parts) = after(far, (near, attended_parts))
    first = scatter_first(grad_parts, far)
    attended_parts, second = after(attended_parts, second)
    grad_sum = scatter_total(grad_parts, near, second, first)
    grad_hidden = (out_grad.astype(jnp.float32) + grad_sum).astype(jnp.bfloat16)
    every_pack = [grad_hidden] + [
        swapped(grad_hidden, "tok", distance) for distance in range(1, packs)
    ]
    _, far, near = scatter_begun(attended_parts)
    second = scatter_second(attended_parts)
    far, near = after(far, near)
    first = scatter_first(attended_parts, far)
    late_hidden, *every_pack = lax.optimization_barrier((hidden_bf, *every_pack))
    stitch_grad = outer_summed(tokens_last, every_pack)
    attended = scatter_total(attended_parts, near, second, first)
    layer_out = (late_hidden.astype(jnp.float32) + attended).astype(jnp.bfloat16)
    return (layer_out, stitch_grad)


def body(
    source, row_token, seg_ids, stitch_weight, norm_gain, q_weight, kv_weight, o_weight, out_grad
):
    tok_rank = lax.axis_index("tok")
    tp_rank = lax.axis_index("tp")
    packs = lax.axis_size("tok")
    pack_len = seg_ids.shape[1]
    width = q_weight.shape[0]
    own_cols = stitch_weight.shape[1]
    own_gain = lax.dynamic_slice_in_dim(norm_gain, tp_rank * own_cols, own_cols)

    gathered = lax.all_gather(source, "tp", axis=0, tiled=True)
    placed = stitched(packs, pack_len, tok_rank, row_token, gathered, stitch_weight)
    within = jnp.arange(pack_len, dtype=jnp.int32)
    hidden = placed[0].astype(jnp.float32)
    for distance in range(1, packs):
        hidden += swapped(placed[distance], "tok", distance).astype(jnp.float32)
    hidden_bf = hidden.astype(jnp.bfloat16)
    hidden_f = hidden_bf.astype(jnp.float32)
    square_sum = summed(jnp.sum(hidden_f * hidden_f, axis=1), "tp")
    inv_rms = lax.rsqrt(square_sum / width + epsilon)[:, None]
    gained = lax.all_gather((hidden_f * own_gain).astype(jnp.bfloat16), "tp", axis=1, tiled=True)

    token_order = (
        (tok_rank ^ jnp.arange(packs, dtype=jnp.int32))[:, None] * pack_len + within[None, :]
    ).reshape(-1)
    order = (row_token[:, None] == token_order[None, :]).astype(jnp.bfloat16)
    tokens_last = dot_f32(gathered, order, COLS_BY_COLS).astype(jnp.bfloat16)

    seg_row = seg_ids[0]
    earlier = jnp.sum((seg_row[None, :] < seg_row[:, None]).astype(jnp.int32), axis=1)
    angles = (within - earlier).astype(jnp.float32)[:, None] * frequencies()[None, :]
    cosine, sine = jnp.cos(angles), jnp.sin(angles)
    cosines = jnp.concatenate([cosine, cosine], axis=1)
    sines = jnp.concatenate([-sine, sine], axis=1)
    local_heads = q_weight.shape[1] // HD
    kv_cols = kv_weight.shape[1]
    paired = kv_cols == HD
    kv_local = 1 if paired else kv_cols // (2 * HD)
    repeat = local_heads // kv_local
    every_grad = lax.all_gather(out_grad, "tp", axis=1, tiled=True)
    grad_context = lax.dot_general(
        every_grad, o_weight, (((1,), (1,)), ((), ())), preferred_element_type=jnp.float32
    ).astype(jnp.bfloat16)
    if paired:
        query_pre = jnp.dot(gained, q_weight, preferred_element_type=jnp.float32)
        projected = jnp.dot(gained, kv_weight, preferred_element_type=jnp.float32) * inv_rms
        is_key = tp_rank % 2 == 0
        own_part = jnp.where(is_key, rotate(projected, cosine, sine), projected).astype(
            jnp.bfloat16
        )
        partner = swapped(own_part, "tp", 1)
        keys = jnp.where(is_key, own_part, partner)
        values = jnp.where(is_key, partner, own_part)
        context, grad_queries, key_part, value_part, aligned = attention_parts(
            repeat, query_pre, inv_rms, cosines, sines, seg_row, keys, values, grad_context
        )
        outgoing = jnp.where(is_key, value_part, key_part)
        incoming = swapped(outgoing.astype(jnp.bfloat16), "tp", 1).astype(outgoing.dtype)
        own_sum = jnp.where(is_key, key_part, value_part) + incoming
        grad_pairs = jnp.where(is_key, unrotate(own_sum, cosine, sine), own_sum).astype(
            jnp.bfloat16
        )
        aligned += jnp.sum(grad_pairs.astype(jnp.float32) * projected, axis=1, keepdims=True)
        grad_normed = back_projected(grad_queries, grad_pairs, q_weight, kv_weight)
    else:
        context, aligned, grad_normed = middle(
            repeat, gained, q_weight, kv_weight, inv_rms, cosines, sines, seg_row, grad_context
        )
    aligned = summed(aligned[:, 0], "tp")[:, None]
    grad_sum = lax.psum_scatter(grad_normed, "tp", scatter_dimension=1, tiled=True)
    attended = jnp.dot(context, o_weight, preferred_element_type=jnp.float32).astype(jnp.bfloat16)
    attended, grad_sum = lax.optimization_barrier((attended, grad_sum))
    grad_hidden = (
        out_grad.astype(jnp.float32)
        + inv_rms * own_gain * grad_sum.astype(jnp.float32)
        - hidden_f * (inv_rms * inv_rms * aligned / width)
    ).astype(jnp.bfloat16)
    every_pack = [grad_hidden] + [
        swapped(grad_hidden, "tok", distance) for distance in range(1, packs)
    ]
    late_hidden, *every_pack = lax.optimization_barrier((hidden_bf, *every_pack))
    stitch_grad = outer_summed(tokens_last, every_pack)

    attended = lax.psum_scatter(attended, "tp", scatter_dimension=1, tiled=True)
    layer_out = (late_hidden.astype(jnp.float32) + attended.astype(jnp.float32)).astype(
        jnp.bfloat16
    )
    return (layer_out, stitch_grad)


def solution(mesh):
    placed = (
        P("tp", "tok"),
        P(),
        P("tok", None),
        P("tok", "tp"),
        P(),
        P(None, "tp"),
        P(None, "tp"),
        P("tp", None),
        P("tok", "tp"),
    )
    on_line = mesh.shape["tp"] == 8
    return jax.shard_map(
        line_body if on_line else body,
        mesh=mesh,
        in_specs=placed,
        out_specs=(P("tok", "tp"), P("tok", "tp")),
        check_vma=False,
    )
```

```python
import functools
import math

import jax
import jax.numpy as jnp
from jax import lax
from jax.experimental import pallas as pl
from jax.experimental.pallas import tpu as pltpu
from jax.sharding import PartitionSpec as P

HD = 128


epsilon = 1e-05


def swapped(value, axis, mask):
    pairs = [(source, source ^ mask) for source in range(lax.axis_size(axis))]
    return lax.ppermute(value, axis, pairs)


def summed(value, axis):
    mask = 1
    while mask < lax.axis_size(axis):
        value = value + swapped(value, axis, mask)
        mask *= 2
    return value


def frequencies():
    exponent = jnp.arange(0, HD, 2).astype(jnp.float32) / HD
    plain_rate = 500000.0 ** (-exponent)
    wavelength = 2.0 * math.pi / plain_rate
    smoothing = (8192.0 / wavelength - 1.0) / 3.0
    blended = (1.0 - smoothing) * plain_rate / 8.0 + smoothing * plain_rate
    return jnp.where(
        wavelength < 2048.0, plain_rate, jnp.where(wavelength > 8192.0, plain_rate / 8.0, blended)
    )


def rotate(vector_in, cosine_table, sine_table):
    half_size = vector_in.shape[-1] // 2
    first_half = vector_in[..., :half_size]
    second = vector_in[..., half_size:]
    return jnp.concatenate(
        [
            first_half * cosine_table - second * sine_table,
            second * cosine_table + first_half * sine_table,
        ],
        axis=-1,
    )


def unrotate(vector_in, cosine_table, sine_table):
    return rotate(vector_in, cosine_table, -sine_table)


VMEM_LIMIT = 56 * 2**20
ROWS_BY_ROWS = (((1,), (1,)), ((), ()))
COLS_BY_COLS = (((0,), (0,)), ((), ()))


def dot_f32(left, right, dims=(((1,), (0,)), ((), ()))):
    return lax.dot_general(left, right, dims, preferred_element_type=jnp.float32)


def attend(
    repeat, read_query, cosines, sines, seg_row, seg_col, keys, values, grad_ref, context_ref,
    query_grad_ref,
):
    rows = cosines.shape[0]
    score_scale = 1.0 / math.sqrt(HD)
    later = lax.broadcasted_iota(jnp.int32, (rows, rows), 0)
    sooner = lax.broadcasted_iota(jnp.int32, (rows, rows), 1)
    allowed = (seg_col == seg_row) & (sooner <= later)
    aligned = jnp.zeros((rows, HD), jnp.float32)
    key_parts, value_parts = [], []
    for group in range(len(keys)):
        key_part = jnp.zeros((rows, HD), jnp.float32)
        value_part = jnp.zeros((rows, HD), jnp.float32)
        for member in range(repeat):
            own = pl.ds((group * repeat + member) * HD, HD)
            plain = read_query(own)
            query = turn(plain, cosines, sines).astype(jnp.bfloat16)
            scores = dot_f32(query, keys[group], ROWS_BY_ROWS) * score_scale
            scores = jnp.where(allowed, scores, -1e30)
            exponents = jnp.exp(scores - jnp.max(scores, axis=1, keepdims=True))
            attention = exponents / jnp.sum(exponents, axis=1, keepdims=True)
            attention_bf = attention.astype(jnp.bfloat16)
            context_ref[:, own] = dot_f32(attention_bf, values[group]).astype(jnp.bfloat16)
            context_grad = grad_ref[:, own]
            grad_probs = dot_f32(context_grad, values[group], ROWS_BY_ROWS)
            mean = jnp.sum(grad_probs * attention, axis=1, keepdims=True)
            score_grad = (attention * (grad_probs - mean) * score_scale).astype(jnp.bfloat16)
            query_grad = turn(dot_f32(score_grad, keys[group]), cosines, -sines).astype(
                jnp.bfloat16
            )
            query_grad_ref[:, own] = query_grad
            aligned += query_grad.astype(jnp.float32) * plain
            key_part += dot_f32(score_grad, query, COLS_BY_COLS)
            value_part += dot_f32(attention_bf, context_grad, COLS_BY_COLS)
        key_parts.append(key_part)
        value_parts.append(value_part)
    return aligned, key_parts, value_parts


def turn(vector_in, cosines, sines):
    return vector_in * cosines + pltpu.roll(vector_in, HD // 2, 1) * sines


def attention_kernel(
    repeat, query_ref, scale_ref, cos_ref, sin_ref, seg_row_ref, seg_col_ref, key_ref, value_ref,
    grad_ref, context_ref, query_grad_ref, key_part_ref, value_part_ref, aligned_ref,
):
    row_scale = scale_ref[...]
    groups = [pl.ds(group * HD, HD) for group in range(key_ref.shape[1] // HD)]
    aligned, key_parts, value_parts = attend(
        repeat, lambda own: query_ref[:, own] * row_scale, cos_ref[...], sin_ref[...],
        seg_row_ref[...], seg_col_ref[...], [key_ref[:, shared] for shared in groups],
        [value_ref[:, shared] for shared in groups], grad_ref, context_ref, query_grad_ref,
    )
    for shared, key_part, value_part in zip(groups, key_parts, value_parts):
        key_part_ref[:, shared] = key_part
        value_part_ref[:, shared] = value_part
    aligned_ref[...] = jnp.sum(aligned, axis=1, keepdims=True)


def attention_parts(repeat, query_pre, inv_rms, cosines, sines, seg_row, keys, values, context_grad):
    rows = query_pre.shape[0]
    whole = pl.BlockSpec(memory_space=pltpu.VMEM)
    return pl.pallas_call(
        functools.partial(attention_kernel, repeat),
        in_specs=[whole] * 9,
        out_specs=[whole] * 5,
        out_shape=[
            jax.ShapeDtypeStruct(query_pre.shape, jnp.bfloat16),
            jax.ShapeDtypeStruct(query_pre.shape, jnp.bfloat16),
            jax.ShapeDtypeStruct(keys.shape, jnp.float32),
            jax.ShapeDtypeStruct(keys.shape, jnp.float32),
            jax.ShapeDtypeStruct((rows, 1), jnp.float32),
        ],
        compiler_params=pltpu.CompilerParams(vmem_limit_bytes=VMEM_LIMIT),
    )(
        query_pre, inv_rms, cosines, sines, seg_row[None, :], seg_row[:, None], keys, values,
        context_grad,
    )


def middle_kernel(
    repeat, gained_ref, q_weight_ref, kv_weight_ref, scale_ref, cos_ref, sin_ref, seg_row_ref,
    seg_col_ref, grad_ref, context_ref, aligned_ref, out_ref, gained, q_weight, kv_weight, out,
    query_sum, pair_sum, query_grad, sems,
):
    width, heads_cols = q_weight.shape
    pieces = sems.shape[1]
    step = width // pieces

    def part(piece):
        return pl.ds(pl.multiple_of(piece * step, step), step)

    def fetches(piece):
        span = part(piece)
        return (
            pltpu.make_async_copy(
                gained_ref.at[:, span], gained.at[:, span], sems.at[0, piece]
            ),
            pltpu.make_async_copy(q_weight_ref.at[span], q_weight.at[span], sems.at[1, piece]),
            pltpu.make_async_copy(kv_weight_ref.at[span], kv_weight.at[span], sems.at[2, piece]),
        )

    def returned(piece):
        span = part(piece)
        return pltpu.make_async_copy(out.at[:, span], out_ref.at[:, span], sems.at[3, piece])

    @pl.loop(0, pieces)
    def _(piece):
        for fetch in fetches(piece):
            fetch.start()

    query_sum[...] = jnp.zeros_like(query_sum)
    pair_sum[...] = jnp.zeros_like(pair_sum)

    @pl.loop(0, pieces)
    def _(piece):
        for fetch in fetches(piece):
            fetch.wait()
        span = part(piece)
        features = gained[:, span]
        query_sum[...] += dot_f32(features, q_weight[span, :])
        pair_sum[...] += dot_f32(features, kv_weight[span, :])

    row_scale = scale_ref[...]
    cosines, sines = cos_ref[...], sin_ref[...]
    groups = kv_weight.shape[1] // (2 * HD)
    pair_plain = pair_sum[...] * row_scale
    halves = [pair_plain[:, i * HD : (i + 1) * HD] for i in range(2 * groups)]
    aligned, key_parts, value_parts = attend(
        repeat, lambda own: query_sum[:, own] * row_scale, cosines, sines, seg_row_ref[...],
        seg_col_ref[...], [turn(half, cosines, sines).astype(jnp.bfloat16) for half in halves[::2]],
        [half.astype(jnp.bfloat16) for half in halves[1::2]], grad_ref, context_ref, query_grad,
    )
    pair_grads = []
    for key_part, value_part in zip(key_parts, value_parts):
        pair_grads.append(turn(key_part, cosines, -sines).astype(jnp.bfloat16))
        pair_grads.append(value_part.astype(jnp.bfloat16))
    for half, pair_grad in zip(halves, pair_grads):
        aligned += half * pair_grad.astype(jnp.float32)
    aligned_ref[...] = jnp.sum(aligned, axis=1, keepdims=True)
    pair_grad = jnp.concatenate(pair_grads, axis=1)

    @pl.loop(0, pieces)
    def _(piece):
        span = part(piece)
        out[:, span] = (
            dot_f32(query_grad[...], q_weight[span, :], ROWS_BY_ROWS)
            + dot_f32(pair_grad, kv_weight[span, :], ROWS_BY_ROWS)
        ).astype(out.dtype)
        returned(piece).start()

    @pl.loop(0, pieces)
    def _(piece):
        returned(piece).wait()


def middle(
    repeat, gained, q_weight, kv_weight, inv_rms, cosines, sines, seg_row, context_grad
):
    rows, width = gained.shape
    heads_cols, kv_cols = q_weight.shape[1], kv_weight.shape[1]
    whole, far = pl.BlockSpec(memory_space=pltpu.VMEM), pl.BlockSpec(memory_space=pl.ANY)
    return pl.pallas_call(
        functools.partial(middle_kernel, repeat),
        in_specs=[far] * 3 + [whole] * 6,
        out_specs=[whole] * 2 + [far],
        out_shape=[
            jax.ShapeDtypeStruct((rows, heads_cols), jnp.bfloat16),
            jax.ShapeDtypeStruct((rows, 1), jnp.float32),
            jax.ShapeDtypeStruct((rows, width), jnp.bfloat16),
        ],
        scratch_shapes=[
            pltpu.VMEM(gained.shape, jnp.bfloat16),
            pltpu.VMEM(q_weight.shape, jnp.bfloat16),
            pltpu.VMEM(kv_weight.shape, jnp.bfloat16),
            pltpu.VMEM(gained.shape, jnp.bfloat16),
            pltpu.VMEM((rows, heads_cols), jnp.float32),
            pltpu.VMEM((rows, kv_cols), jnp.float32),
            pltpu.VMEM((rows, heads_cols), jnp.bfloat16),
            pltpu.SemaphoreType.DMA((4, 8)),
        ],
        compiler_params=pltpu.CompilerParams(vmem_limit_bytes=VMEM_LIMIT),
    )(
        gained, q_weight, kv_weight, inv_rms, cosines, sines, seg_row[None, :], seg_row[:, None],
        context_grad,
    )


def stitch_kernel(packs, rank_ref, token_ref, source_ref, weight_ref, *refs):
    out_refs, product = refs[:packs], refs[-1]
    block = source_ref.shape[0]
    step = pl.program_id(0)
    here = pl.ds(pl.multiple_of(step * block, block), block)
    product[here, :] = dot_f32(source_ref[...], weight_ref[...]).astype(jnp.bfloat16)

    @pl.when(step == pl.num_programs(0) - 1)
    def _():
        pack_len = out_refs[0].shape[0]
        shape = (pack_len, product.shape[0])
        place = token_ref[...] - lax.broadcasted_iota(jnp.int32, shape, 0)
        for distance in range(packs):
            first = (rank_ref[0] ^ distance) * pack_len
            rows = (place == first).astype(jnp.float32).astype(jnp.bfloat16)
            out_refs[distance][...] = dot_f32(rows, product[...]).astype(jnp.bfloat16)


def stitched(packs, pack_len, rank, row_token, source, weight):
    rows, features = source.shape
    cols = weight.shape[1]
    block = min(512, rows)
    fixed = lambda i: (0, 0)
    return pl.pallas_call(
        functools.partial(stitch_kernel, packs),
        grid=(rows // block,),
        in_specs=[
            pl.BlockSpec(memory_space=pltpu.SMEM),
            pl.BlockSpec((1, rows), fixed),
            pl.BlockSpec((block, features), lambda i: (i, 0)),
            pl.BlockSpec(weight.shape, fixed),
        ],
        out_specs=[pl.BlockSpec((pack_len, cols), fixed)] * packs,
        out_shape=[jax.ShapeDtypeStruct((pack_len, cols), jnp.bfloat16)] * packs,
        scratch_shapes=[pltpu.VMEM((rows, cols), jnp.bfloat16)],
        compiler_params=pltpu.CompilerParams(vmem_limit_bytes=VMEM_LIMIT),
    )(rank.reshape(1), row_token[None, :], source, weight)


def back_kernel(query_ref, pair_ref, q_weight_ref, kv_weight_ref, out_ref):
    out_ref[...] = (
        dot_f32(query_ref[...], q_weight_ref[...], ROWS_BY_ROWS)
        + dot_f32(pair_ref[...], kv_weight_ref[...], ROWS_BY_ROWS)
    ).astype(out_ref.dtype)


def back_projected(grad_queries, grad_pairs, q_weight, kv_weight):
    rows = grad_queries.shape[0]
    width = q_weight.shape[0]
    block = 2048
    fixed = lambda i: (0, 0)
    return pl.pallas_call(
        back_kernel,
        grid=(width // block,),
        in_specs=[
            pl.BlockSpec(grad_queries.shape, fixed),
            pl.BlockSpec(grad_pairs.shape, fixed),
            pl.BlockSpec((block, q_weight.shape[1]), lambda i: (i, 0)),
            pl.BlockSpec((block, kv_weight.shape[1]), lambda i: (i, 0)),
        ],
        out_specs=pl.BlockSpec((rows, block), lambda i: (0, i)),
        out_shape=jax.ShapeDtypeStruct((rows, width), jnp.bfloat16),
        compiler_params=pltpu.CompilerParams(vmem_limit_bytes=VMEM_LIMIT),
    )(grad_queries, grad_pairs, q_weight, kv_weight)


def outer_kernel(*refs):
    features_ref, out_ref = refs[0], refs[-1]
    total = None
    for place, grad_ref in enumerate(refs[1:-1]):
        rows = grad_ref.shape[0]
        term = dot_f32(features_ref[:, pl.ds(place * rows, rows)], grad_ref[...])
        total = term if total is None else total + term
    out_ref[...] = total


def outer_summed(features, grads):
    block = min(512, features.shape[0])
    cols = grads[0].shape[1]
    return pl.pallas_call(
        outer_kernel,
        grid=(features.shape[0] // block,),
        in_specs=[pl.BlockSpec((block, features.shape[1]), lambda i: (i, 0))]
        + [pl.BlockSpec(grad.shape, lambda i: (0, 0)) for grad in grads],
        out_specs=pl.BlockSpec((block, cols), lambda i: (i, 0)),
        out_shape=jax.ShapeDtypeStruct((features.shape[0], cols), jnp.float32),
        compiler_params=pltpu.CompilerParams(vmem_limit_bytes=20 * 2**20),
    )(features, *grads)


STAY, FIRST, SECOND, LAST = (0, 1, 2, 3), (1, 3, 0, 2), (2, 0, 3, 1), (3, 2, 1, 0)


OUTWARD = [(0, 1), (1, 0), (2, 3), (3, 2)]
INSIDE = [(0, 1), (1, 0), (2, 4), (3, 5), (4, 2), (5, 3), (6, 7), (7, 6)]


def is_inner():
    chip = lax.axis_index("tp") // 2
    return (chip == 1) | (chip == 2)


def along(value, pairs):
    both = [(2 * start + core, 2 * end + core) for start, end in pairs for core in range(2)]
    return lax.ppermute(value, "tp", both)


def towards(table):
    return [(start, end) for start, end in enumerate(table)]


def arriving(table):
    return [(start, end) for end, start in enumerate(table)]


def after(value, done):
    value, done = lax.optimization_barrier((value, done))
    return value, done


def gather_begun(block):
    return along(block, arriving(FIRST))


def gather_second(block):
    return along(block, arriving(SECOND))


def gather_last(block, first):
    return along(first, OUTWARD), lax.ppermute(block, "tp", INSIDE)


def early_blocks(block, first):
    return [block, swapped(block, "tp", 1), first, swapped(first, "tp", 1)]


def late_blocks(second, last):
    far, near = last
    last = jnp.where(is_inner(), near, far)
    return [second, swapped(second, "tp", 1), last, swapped(last, "tp", 1)]


def both_cores(parts, place):
    other = swapped(parts[2 * place + 1], "tp", 1)
    return parts[2 * place].astype(jnp.float32) + other.astype(jnp.float32)


def scatter_begun(parts):
    last = both_cores(parts, 0).astype(jnp.bfloat16)
    return last, along(last, OUTWARD), lax.ppermute(last, "tp", INSIDE)


def scatter_second(parts):
    return along(both_cores(parts, 1).astype(jnp.bfloat16), towards(SECOND))


def scatter_first(parts, far):
    first = both_cores(parts, 2)
    first += jnp.where(is_inner(), far.astype(jnp.float32), 0.0)
    return along(first.astype(jnp.bfloat16), towards(FIRST))


def scatter_total(parts, near, second, first):
    total = both_cores(parts, 3) + jnp.where(is_inner(), near.astype(jnp.float32), 0.0)
    return total + second.astype(jnp.float32) + first.astype(jnp.float32)


def line_stitch_half(blocks, rows, rows_ref, weight_ref, product, here, sems, out_sem):
    block = blocks[0].shape[0]
    fetches = [
        pltpu.make_async_copy(blocks[i], rows.at[pl.ds(i * block, block)], sems.at[i])
        for i in range(4)
    ]
    for fetch in fetches:
        fetch.start()
    for fetch in fetches:
        fetch.wait()
    kept = pltpu.make_async_copy(rows, rows_ref, out_sem)
    kept.start()
    product[here, :] = dot_f32(rows[...], weight_ref[...]).astype(jnp.bfloat16)
    return kept


def line_stitch_early_kernel(weight_ref, *refs):
    blocks, (product_ref, rows_ref, rows, sems, out_sem) = refs[:4], refs[4:]
    everything = pl.ds(0, rows.shape[0])
    line_stitch_half(
        blocks, rows, rows_ref, weight_ref, product_ref, everything, sems, out_sem
    ).wait()


def line_stitch_kernel(packs, rank_ref, token_ref, weight_ref, early_ref, *refs):
    blocks, out_refs = refs[:4], refs[4 : 4 + packs]
    rows_ref, rows, product, sems, out_sem = refs[4 + packs :]
    half = rows.shape[0]
    kept = line_stitch_half(
        blocks, rows, rows_ref, weight_ref, product, pl.ds(half, half), sems, out_sem
    )
    product[pl.ds(0, half), :] = early_ref[...]
    pack_len = out_refs[0].shape[0]
    place = token_ref[...] - lax.broadcasted_iota(jnp.int32, (pack_len, product.shape[0]), 0)
    for distance in range(packs):
        first = (rank_ref[0] ^ distance) * pack_len
        chosen = (place == first).astype(jnp.float32).astype(jnp.bfloat16)
        out_refs[distance][...] = dot_f32(chosen, product[...]).astype(jnp.bfloat16)
    kept.wait()


def line_stitched_early(blocks, weight):
    block, features = blocks[0].shape
    cols = weight.shape[1]
    whole, far = pl.BlockSpec(memory_space=pltpu.VMEM), pl.BlockSpec(memory_space=pl.ANY)
    return pl.pallas_call(
        line_stitch_early_kernel,
        in_specs=[whole] + [far] * 4,
        out_specs=[whole, far],
        out_shape=[
            jax.ShapeDtypeStruct((4 * block, cols), jnp.bfloat16),
            jax.ShapeDtypeStruct((4 * block, features), jnp.bfloat16),
        ],
        scratch_shapes=[
            pltpu.VMEM((4 * block, features), jnp.bfloat16),
            pltpu.SemaphoreType.DMA((4,)),
            pltpu.SemaphoreType.DMA,
        ],
        compiler_params=pltpu.CompilerParams(vmem_limit_bytes=20 * 2**20),
    )(weight, *blocks)


def line_stitched(packs, pack_len, rank, token_row, early, blocks, weight):
    block, features = blocks[0].shape
    cols = weight.shape[1]
    whole, far = pl.BlockSpec(memory_space=pltpu.VMEM), pl.BlockSpec(memory_space=pl.ANY)
    results = pl.pallas_call(
        functools.partial(line_stitch_kernel, packs),
        in_specs=[pl.BlockSpec(memory_space=pltpu.SMEM)] + [whole] * 3 + [far] * 4,
        out_specs=[whole] * packs + [far],
        out_shape=[jax.ShapeDtypeStruct((pack_len, cols), jnp.bfloat16)] * packs
        + [jax.ShapeDtypeStruct((4 * block, features), jnp.bfloat16)],
        scratch_shapes=[
            pltpu.VMEM((4 * block, features), jnp.bfloat16),
            pltpu.VMEM((8 * block, cols), jnp.bfloat16),
            pltpu.SemaphoreType.DMA((4,)),
            pltpu.SemaphoreType.DMA,
        ],
        compiler_params=pltpu.CompilerParams(vmem_limit_bytes=24 * 2**20),
    )(rank.reshape(1), token_row, weight, early, *blocks)
    return results[:packs], results[packs]


def line_grad_kernel(chips_ref, core_ref, weight_ref, *refs):
    blocks, out_ref, features, total, sems = refs[:8], *refs[8:]
    step = pl.program_id(0)
    cols = blocks[0].shape[1]

    def fetch(place, half):
        core = core_ref[0] if half == 0 else 1 - core_ref[0]
        there = features.at[place, :, pl.ds(pl.multiple_of(core * cols, cols), cols)]
        return there, sems.at[place, half]

    @pl.when(step == 0)
    def _():
        for i in range(8):
            pltpu.make_async_copy(blocks[i], *fetch(i // 2, i % 2)).start()
        total[...] = jnp.zeros_like(total)

    for half in range(2):
        pltpu.make_async_copy(blocks[half], *fetch(step, half)).wait()
    total[...] += dot_f32(features[step], weight_ref[...], ROWS_BY_ROWS)

    @pl.when(step == 3)
    def _():
        out_ref[...] = total[...].astype(out_ref.dtype)


def line_grad_context(chips, core, blocks, weight):
    rows, cols = blocks[0].shape
    heads_cols = weight.shape[0]
    far = pl.BlockSpec(memory_space=pl.ANY)
    return pl.pallas_call(
        line_grad_kernel,
        grid_spec=pltpu.PrefetchScalarGridSpec(
            num_scalar_prefetch=2,
            grid=(4,),
            in_specs=[pl.BlockSpec((heads_cols, 2 * cols), lambda i, chips, core: (0, chips[i]))]
            + [far] * 8,
            out_specs=pl.BlockSpec((rows, heads_cols), lambda i, chips, core: (0, 0)),
            scratch_shapes=[
                pltpu.VMEM((4, rows, 2 * cols), jnp.bfloat16),
                pltpu.VMEM((rows, heads_cols), jnp.float32),
                pltpu.SemaphoreType.DMA((4, 2)),
            ],
        ),
        out_shape=jax.ShapeDtypeStruct((rows, heads_cols), jnp.bfloat16),
        compiler_params=pltpu.CompilerParams(vmem_limit_bytes=VMEM_LIMIT),
    )(chips, core.reshape(1), weight, *blocks)


def line_attended_kernel(chips_ref, core_ref, context_ref, weight_ref, *refs):
    out_refs, product = refs[:8], refs[8]
    step = pl.program_id(0)
    cols = out_refs[0].shape[1]
    product[...] = dot_f32(context_ref[...], weight_ref[...]).astype(jnp.bfloat16)
    for i in range(4):

        @pl.when(step == i)
        def _(i=i):
            for half in range(2):
                core = core_ref[0] if half == 0 else 1 - core_ref[0]
                here = pl.ds(pl.multiple_of(core * cols, cols), cols)
                out_refs[2 * i + half][...] = product[:, here]


def line_attended(chips, core, context, weight):
    rows, heads_cols = context.shape
    cols = weight.shape[1] // 8
    fixed = lambda i, chips, core: (0, 0)
    return pl.pallas_call(
        line_attended_kernel,
        grid_spec=pltpu.PrefetchScalarGridSpec(
            num_scalar_prefetch=2,
            grid=(4,),
            in_specs=[
                pl.BlockSpec((rows, heads_cols), fixed),
                pl.BlockSpec((heads_cols, 2 * cols), lambda i, chips, core: (0, chips[i])),
            ],
            out_specs=[pl.BlockSpec((rows, cols), fixed)] * 8,
            scratch_shapes=[pltpu.VMEM((rows, 2 * cols), jnp.bfloat16)],
        ),
        out_shape=[jax.ShapeDtypeStruct((rows, cols), jnp.bfloat16)] * 8,
        compiler_params=pltpu.CompilerParams(vmem_limit_bytes=VMEM_LIMIT),
    )(chips, core.reshape(1), context, weight)


def line_project(
    places, from_ref, gain_ref, q_weight_ref, kv_weight_ref, blocks, hidden, q_weight, kv_weight,
    sems, query_sum, pair_sum, squares,
):
    rows, step = blocks[0].shape

    def part(place):
        return pl.ds(pl.multiple_of(from_ref[place] * step, step), step)

    def fetches(place):
        span = part(place)
        return (
            pltpu.make_async_copy(q_weight_ref.at[span], q_weight.at[span], sems.at[1, place]),
            pltpu.make_async_copy(kv_weight_ref.at[span], kv_weight.at[span], sems.at[2, place]),
        )

    def features(place):
        return pltpu.make_async_copy(blocks[0], hidden.at[place], sems.at[0, place])

    later = [place for place in range(len(blocks)) if place not in places]
    for place in [*places, *later]:
        pltpu.make_async_copy(blocks[place], hidden.at[place], sems.at[0, place]).start()
        for fetch in fetches(place):
            fetch.start()

    def project(place, squares):
        features(place).wait()
        for fetch in fetches(place):
            fetch.wait()
        span = part(place)
        wide = hidden[place].astype(jnp.float32)
        gained = (wide * gain_ref[:, span]).astype(jnp.bfloat16)
        query_sum[...] += dot_f32(gained, q_weight[span, :])
        pair_sum[...] += dot_f32(gained, kv_weight[span, :])
        return squares + jnp.sum(wide * wide, axis=1, keepdims=True)

    squares = lax.fori_loop(places[0], places[-1] + 1, project, squares)

    def finish():
        for place in later:
            features(place).wait()
            for fetch in fetches(place):
                fetch.wait()

    return squares, finish


def line_projected_kernel(
    from_ref, gain_ref, q_weight_ref, kv_weight_ref, *refs,
):
    blocks, (query_sum, pair_sum, squares_ref) = refs[:4], refs[4:7]
    hidden, q_weight, kv_weight, sems = refs[7:]
    query_sum[...] = jnp.zeros_like(query_sum)
    pair_sum[...] = jnp.zeros_like(pair_sum)
    squares, _ = line_project(
        range(4), from_ref, gain_ref, q_weight_ref, kv_weight_ref, blocks, hidden, q_weight,
        kv_weight, sems, query_sum, pair_sum, jnp.zeros(squares_ref.shape, jnp.float32),
    )
    squares_ref[...] = squares


def line_projected(sources, blocks, gain, q_weight, kv_weight):
    rows, step = blocks[0].shape
    heads_cols, kv_cols = q_weight.shape[1], kv_weight.shape[1]
    whole, far = pl.BlockSpec(memory_space=pltpu.VMEM), pl.BlockSpec(memory_space=pl.ANY)
    return pl.pallas_call(
        line_projected_kernel,
        in_specs=[pl.BlockSpec(memory_space=pltpu.SMEM), whole] + [far] * 6,
        out_specs=[whole] * 3,
        out_shape=[
            jax.ShapeDtypeStruct((rows, heads_cols), jnp.float32),
            jax.ShapeDtypeStruct((rows, kv_cols), jnp.float32),
            jax.ShapeDtypeStruct((rows, 1), jnp.float32),
        ],
        scratch_shapes=[
            pltpu.VMEM((4, rows, step), jnp.bfloat16),
            pltpu.VMEM(q_weight.shape, jnp.bfloat16),
            pltpu.VMEM(kv_weight.shape, jnp.bfloat16),
            pltpu.SemaphoreType.DMA((3, 4)),
        ],
        compiler_params=pltpu.CompilerParams(vmem_limit_bytes=VMEM_LIMIT),
    )(sources, gain[None, :], q_weight, kv_weight, *blocks)


def line_tokens_kernel(token_ref, order_ref, early_ref, late_ref, out_ref):
    half = early_ref.shape[0]
    total = None
    for place, rows_ref in enumerate((early_ref, late_ref)):
        tokens = token_ref[pl.ds(place * half, half), :]
        chosen = (tokens == order_ref[...]).astype(jnp.float32).astype(jnp.bfloat16)
        term = dot_f32(rows_ref[...], chosen, COLS_BY_COLS)
        total = term if total is None else total + term
    out_ref[...] = total.astype(out_ref.dtype)


def line_tokens_last(token_col, token_order, early_rows, late_rows):
    half, features = early_rows.shape
    tokens = token_order.shape[1]
    block = min(1024, features)
    fixed = lambda i: (0, 0)
    return pl.pallas_call(
        line_tokens_kernel,
        grid=(features // block,),
        in_specs=[
            pl.BlockSpec((2 * half, 1), fixed),
            pl.BlockSpec((1, tokens), fixed),
            pl.BlockSpec((half, block), lambda i: (0, i)),
            pl.BlockSpec((half, block), lambda i: (0, i)),
        ],
        out_specs=pl.BlockSpec((block, tokens), lambda i: (i, 0)),
        out_shape=jax.ShapeDtypeStruct((features, tokens), jnp.bfloat16),
        compiler_params=pltpu.CompilerParams(vmem_limit_bytes=VMEM_LIMIT),
    )(token_col, token_order, early_rows, late_rows)


def line_middle_kernel(
    repeat, from_ref, to_ref, gain_ref, cos_ref, sin_ref, seg_row_ref, seg_col_ref, grad_ref,
    early_query_ref, early_pair_ref, early_squares_ref, q_weight_ref, kv_weight_ref, *refs,
):
    blocks, context_ref, out_refs = refs[:8], refs[8], refs[9:17]
    hidden, q_weight, kv_weight, out, query_sum, pair_sum, query_grad, sems, out_sems = refs[17:]
    width = q_weight.shape[0]
    rows, step = blocks[0].shape

    def part(rank):
        return pl.ds(pl.multiple_of(rank * step, step), step)

    query_sum[...] = early_query_ref[...]
    pair_sum[...] = early_pair_ref[...]
    squares, finish = line_project(
        range(4, 8), from_ref, gain_ref, q_weight_ref, kv_weight_ref, blocks, hidden, q_weight,
        kv_weight, sems, query_sum, pair_sum, early_squares_ref[...],
    )
    row_scale = lax.rsqrt(squares / width + epsilon)
    cosines, sines = cos_ref[...], sin_ref[...]
    groups = kv_weight.shape[1] // (2 * HD)
    pair_plain = pair_sum[...] * row_scale
    halves = [pair_plain[:, i * HD : (i + 1) * HD] for i in range(2 * groups)]
    aligned, key_parts, value_parts = attend(
        repeat, lambda own: query_sum[:, own] * row_scale, cosines, sines, seg_row_ref[...],
        seg_col_ref[...], [turn(half, cosines, sines).astype(jnp.bfloat16) for half in halves[::2]],
        [half.astype(jnp.bfloat16) for half in halves[1::2]], grad_ref, context_ref, query_grad,
    )
    pair_grads = []
    for key_part, value_part in zip(key_parts, value_parts):
        pair_grads.append(turn(key_part, cosines, -sines).astype(jnp.bfloat16))
        pair_grads.append(value_part.astype(jnp.bfloat16))
    for half, pair_grad in zip(halves, pair_grads):
        aligned += half * pair_grad.astype(jnp.float32)
    aligned = jnp.sum(aligned, axis=1, keepdims=True) * (row_scale * row_scale / width)
    pair_grad = jnp.concatenate(pair_grads, axis=1)
    finish()

    @pl.loop(0, 8)
    def _(place):
        span = part(to_ref[place])
        grad_normed = dot_f32(query_grad[...], q_weight[span, :], ROWS_BY_ROWS)
        grad_normed += dot_f32(pair_grad, kv_weight[span, :], ROWS_BY_ROWS)
        features = hidden[6 - 2 * (place // 2) + place % 2].astype(jnp.float32)
        out[place] = (
            grad_normed * (row_scale * gain_ref[:, span]) - features * aligned
        ).astype(out.dtype)
        for i in range(8):

            @pl.when(place == i)
            def _(i=i):
                pltpu.make_async_copy(out.at[i], out_refs[i], out_sems.at[i]).start()

    for i in range(8):
        pltpu.make_async_copy(out.at[i], out_refs[i], out_sems.at[i]).wait()


def line_middle(
    repeat, sources, targets, blocks, early_sums, gain, q_weight, kv_weight, cosines, sines, seg_row,
    seg_col, context_grad,
):
    rows, step = blocks[0].shape
    heads_cols, kv_cols = q_weight.shape[1], kv_weight.shape[1]
    whole, far = pl.BlockSpec(memory_space=pltpu.VMEM), pl.BlockSpec(memory_space=pl.ANY)
    scalars = pl.BlockSpec(memory_space=pltpu.SMEM)
    results = pl.pallas_call(
        functools.partial(line_middle_kernel, repeat),
        in_specs=[scalars] * 2 + [whole] * 9 + [far] * 10,
        out_specs=[whole] + [far] * 8,
        out_shape=[jax.ShapeDtypeStruct((rows, heads_cols), jnp.bfloat16)]
        + [jax.ShapeDtypeStruct((rows, step), jnp.bfloat16)] * 8,
        scratch_shapes=[
            pltpu.VMEM((8, rows, step), jnp.bfloat16),
            pltpu.VMEM(q_weight.shape, jnp.bfloat16),
            pltpu.VMEM(kv_weight.shape, jnp.bfloat16),
            pltpu.VMEM((8, rows, step), jnp.bfloat16),
            pltpu.VMEM((rows, heads_cols), jnp.float32),
            pltpu.VMEM((rows, kv_cols), jnp.float32),
            pltpu.VMEM((rows, heads_cols), jnp.bfloat16),
            pltpu.SemaphoreType.DMA((3, 8)),
            pltpu.SemaphoreType.DMA((8,)),
        ],
        compiler_params=pltpu.CompilerParams(vmem_limit_bytes=VMEM_LIMIT),
    )(
        sources, targets, gain[None, :], cosines, sines, seg_row[None, :], seg_col,
        context_grad, *early_sums, q_weight, kv_weight, *blocks,
    )
    return results[0], results[1:]


def line_body(
    source, row_token, seg_ids, stitch_weight, norm_gain, q_weight, kv_weight, o_weight, out_grad
):
    tok_rank = lax.axis_index("tok")
    tp_rank = lax.axis_index("tp")
    packs = lax.axis_size("tok")
    pack_len = seg_ids.shape[1]
    width = q_weight.shape[0]
    own_cols = stitch_weight.shape[1]
    repeat = (q_weight.shape[1] // HD) // (kv_weight.shape[1] // (2 * HD))
    chip, core = tp_rank // 2, tp_rank % 2

    def chips(tables):
        return jnp.array(tables, jnp.int32)[:, chip]

    def ranks(tables):
        pairs = 2 * chips(tables)
        return jnp.stack([pairs + core, pairs + 1 - core], axis=1).reshape(-1)

    arrival, departure = (STAY, FIRST, SECOND, LAST), (LAST, SECOND, FIRST, STAY)
    sources, targets = ranks(arrival), ranks(departure)

    within = jnp.arange(pack_len, dtype=jnp.int32)
    seg_row = seg_ids[0]
    earlier = jnp.sum((seg_row[None, :] < seg_row[:, None]).astype(jnp.int32), axis=1)
    angles = (within - earlier).astype(jnp.float32)[:, None] * frequencies()[None, :]
    cosine, sine = jnp.cos(angles), jnp.sin(angles)
    cosines = jnp.concatenate([cosine, cosine], axis=1)
    sines = jnp.concatenate([-sine, sine], axis=1)

    token_row = row_token.reshape(8, -1)[sources].reshape(1, -1)
    first = gather_begun(source)
    seg_col, token_col = seg_row[:, None], token_row.reshape(-1, 1)
    arrivals, departures = chips(arrival), chips(departure)
    small = (token_row, token_col, seg_col, cosines, sines, sources, targets, arrivals, departures)
    source, (first, small) = after(source, (first, small))
    token_row, token_col, seg_col, cosines, sines, sources, targets, arrivals, departures = small
    second, last = gather_second(source), gather_last(source, first)
    early_source = early_blocks(source, first)
    early_product, early_rows = line_stitched_early(early_source, stitch_weight)
    out_grad, (second, last, early_product) = after(out_grad, (second, last, early_product))
    late_source = late_blocks(second, last)
    og_first = gather_begun(out_grad)
    placed, late_rows = line_stitched(
        packs, pack_len, tok_rank, token_row, early_product, late_source, stitch_weight
    )
    received = [swapped(placed[distance], "tok", distance) for distance in range(1, packs)]
    received[0], og_first = after(received[0], og_first)
    og_second, og_last = gather_second(out_grad), gather_last(out_grad, og_first)
    hidden = placed[0].astype(jnp.float32)
    for part in received:
        hidden += part.astype(jnp.float32)
    hidden_bf = hidden.astype(jnp.bfloat16)
    hidden_first = gather_begun(hidden_bf)
    early_rows, hidden_bf = after(early_rows, hidden_bf)
    token_order = (
        (tok_rank ^ jnp.arange(packs, dtype=jnp.int32))[:, None] * pack_len + within[None, :]
    ).reshape(-1)
    tokens_last = line_tokens_last(token_col, token_order[None, :], early_rows, late_rows)
    (hidden_bf, hidden_first), (og_second, og_last, tokens_last) = after(
        (hidden_bf, hidden_first), (og_second, og_last, tokens_last)
    )
    hidden_second, hidden_last = gather_second(hidden_bf), gather_last(hidden_bf, hidden_first)
    og_blocks = early_blocks(out_grad, og_first) + late_blocks(og_second, og_last)
    grad_context = line_grad_context(arrivals, core, og_blocks, o_weight)
    early_hidden = early_blocks(hidden_bf, hidden_first)
    early_sums = line_projected(sources, early_hidden, norm_gain, q_weight, kv_weight)
    hidden_last, (hidden_second, grad_context, early_sums) = after(
        hidden_last, (hidden_second, grad_context, early_sums)
    )
    hidden_blocks = early_hidden + late_blocks(hidden_second, hidden_last)

    context, grad_parts = line_middle(
        repeat, sources, targets, hidden_blocks, early_sums, norm_gain, q_weight, kv_weight,
        cosines, sines, seg_row, seg_col, grad_context,
    )
    last, far, near = scatter_begun(grad_parts)
    context, last = after(context, last)
    attended_parts = line_attended(departures, core, context, o_weight)
    second = scatter_second(grad_parts)
    far, (near, attended_parts) = after(far, (near, attended_parts))
    first = scatter_first(grad_parts, far)
    grad_sum = scatter_total(grad_parts, near, second, first)
    grad_hidden = (out_grad.astype(jnp.float32) + grad_sum).astype(jnp.bfloat16)
    every_pack = [grad_hidden] + [
        swapped(grad_hidden, "tok", distance) for distance in range(1, packs)
    ]
    _, far, near = scatter_begun(attended_parts)
    second = scatter_second(attended_parts)
    far, near = after(far, near)
    first = scatter_first(attended_parts, far)
    late_hidden, *every_pack = lax.optimization_barrier((hidden_bf, *every_pack))
    stitch_grad = outer_summed(tokens_last, every_pack)
    attended = scatter_total(attended_parts, near, second, first)
    layer_out = (late_hidden.astype(jnp.float32) + attended).astype(jnp.bfloat16)
    return (layer_out, stitch_grad)


def body(
    source, row_token, seg_ids, stitch_weight, norm_gain, q_weight, kv_weight, o_weight, out_grad
):
    tok_rank = lax.axis_index("tok")
    tp_rank = lax.axis_index("tp")
    packs = lax.axis_size("tok")
    pack_len = seg_ids.shape[1]
    width = q_weight.shape[0]
    own_cols = stitch_weight.shape[1]
    own_gain = lax.dynamic_slice_in_dim(norm_gain, tp_rank * own_cols, own_cols)

    gathered = lax.all_gather(source, "tp", axis=0, tiled=True)
    placed = stitched(packs, pack_len, tok_rank, row_token, gathered, stitch_weight)
    within = jnp.arange(pack_len, dtype=jnp.int32)
    hidden = placed[0].astype(jnp.float32)
    for distance in range(1, packs):
        hidden += swapped(placed[distance], "tok", distance).astype(jnp.float32)
    hidden_bf = hidden.astype(jnp.bfloat16)
    hidden_f = hidden_bf.astype(jnp.float32)
    square_sum = summed(jnp.sum(hidden_f * hidden_f, axis=1), "tp")
    inv_rms = lax.rsqrt(square_sum / width + epsilon)[:, None]
    gained = lax.all_gather((hidden_f * own_gain).astype(jnp.bfloat16), "tp", axis=1, tiled=True)

    token_order = (
        (tok_rank ^ jnp.arange(packs, dtype=jnp.int32))[:, None] * pack_len + within[None, :]
    ).reshape(-1)
    order = (row_token[:, None] == token_order[None, :]).astype(jnp.bfloat16)
    tokens_last = dot_f32(gathered, order, COLS_BY_COLS).astype(jnp.bfloat16)

    seg_row = seg_ids[0]
    earlier = jnp.sum((seg_row[None, :] < seg_row[:, None]).astype(jnp.int32), axis=1)
    angles = (within - earlier).astype(jnp.float32)[:, None] * frequencies()[None, :]
    cosine, sine = jnp.cos(angles), jnp.sin(angles)
    cosines = jnp.concatenate([cosine, cosine], axis=1)
    sines = jnp.concatenate([-sine, sine], axis=1)
    local_heads = q_weight.shape[1] // HD
    kv_cols = kv_weight.shape[1]
    paired = kv_cols == HD
    kv_local = 1 if paired else kv_cols // (2 * HD)
    repeat = local_heads // kv_local
    every_grad = lax.all_gather(out_grad, "tp", axis=1, tiled=True)
    grad_context = lax.dot_general(
        every_grad, o_weight, (((1,), (1,)), ((), ())), preferred_element_type=jnp.float32
    ).astype(jnp.bfloat16)
    if paired:
        query_pre = jnp.dot(gained, q_weight, preferred_element_type=jnp.float32)
        projected = jnp.dot(gained, kv_weight, preferred_element_type=jnp.float32) * inv_rms
        is_key = tp_rank % 2 == 0
        own_part = jnp.where(is_key, rotate(projected, cosine, sine), projected).astype(
            jnp.bfloat16
        )
        partner = swapped(own_part, "tp", 1)
        keys = jnp.where(is_key, own_part, partner)
        values = jnp.where(is_key, partner, own_part)
        context, grad_queries, key_part, value_part, aligned = attention_parts(
            repeat, query_pre, inv_rms, cosines, sines, seg_row, keys, values, grad_context
        )
        outgoing = jnp.where(is_key, value_part, key_part)
        incoming = swapped(outgoing.astype(jnp.bfloat16), "tp", 1).astype(outgoing.dtype)
        own_sum = jnp.where(is_key, key_part, value_part) + incoming
        grad_pairs = jnp.where(is_key, unrotate(own_sum, cosine, sine), own_sum).astype(
            jnp.bfloat16
        )
        aligned += jnp.sum(grad_pairs.astype(jnp.float32) * projected, axis=1, keepdims=True)
        grad_normed = back_projected(grad_queries, grad_pairs, q_weight, kv_weight)
    else:
        context, aligned, grad_normed = middle(
            repeat, gained, q_weight, kv_weight, inv_rms, cosines, sines, seg_row, grad_context
        )
    aligned = summed(aligned[:, 0], "tp")[:, None]
    grad_sum = lax.psum_scatter(grad_normed, "tp", scatter_dimension=1, tiled=True)
    attended = jnp.dot(context, o_weight, preferred_element_type=jnp.float32).astype(jnp.bfloat16)
    attended, grad_sum = lax.optimization_barrier((attended, grad_sum))
    grad_hidden = (
        out_grad.astype(jnp.float32)
        + inv_rms * own_gain * grad_sum.astype(jnp.float32)
        - hidden_f * (inv_rms * inv_rms * aligned / width)
    ).astype(jnp.bfloat16)
    every_pack = [grad_hidden] + [
        swapped(grad_hidden, "tok", distance) for distance in range(1, packs)
    ]
    late_hidden, *every_pack = lax.optimization_barrier((hidden_bf, *every_pack))
    stitch_grad = outer_summed(tokens_last, every_pack)

    attended = lax.psum_scatter(attended, "tp", scatter_dimension=1, tiled=True)
    layer_out = (late_hidden.astype(jnp.float32) + attended.astype(jnp.float32)).astype(
        jnp.bfloat16
    )
    return (layer_out, stitch_grad)


def solution(mesh):
    placed = (
        P("tp", "tok"),
        P(),
        P("tok", None),
        P("tok", "tp"),
        P(),
        P(None, "tp"),
        P(None, "tp"),
        P("tp", None),
        P("tok", "tp"),
    )
    on_line = mesh.shape["tp"] == 8
    return jax.shard_map(
        line_body if on_line else body,
        mesh=mesh,
        in_specs=placed,
        out_specs=(P("tok", "tp"), P("tok", "tp")),
        check_vma=False,
    )
```

```python
import functools
import math

import jax
import jax.numpy as jnp
from jax import lax
from jax.experimental import pallas as pl
from jax.experimental.pallas import tpu as pltpu
from jax.sharding import PartitionSpec as P

HD = 128


epsilon = 1e-05


def swapped(value, axis, mask):
    pairs = [(source, source ^ mask) for source in range(lax.axis_size(axis))]
    return lax.ppermute(value, axis, pairs)


def summed(value, axis):
    mask = 1
    while mask < lax.axis_size(axis):
        value = value + swapped(value, axis, mask)
        mask *= 2
    return value


def frequencies():
    exponent = jnp.arange(0, HD, 2).astype(jnp.float32) / HD
    plain_rate = 500000.0 ** (-exponent)
    wavelength = 2.0 * math.pi / plain_rate
    smoothing = (8192.0 / wavelength - 1.0) / 3.0
    blended = (1.0 - smoothing) * plain_rate / 8.0 + smoothing * plain_rate
    return jnp.where(
        wavelength < 2048.0, plain_rate, jnp.where(wavelength > 8192.0, plain_rate / 8.0, blended)
    )


def rotate(vector_in, cosine_table, sine_table):
    half_size = vector_in.shape[-1] // 2
    first_half = vector_in[..., :half_size]
    second = vector_in[..., half_size:]
    return jnp.concatenate(
        [
            first_half * cosine_table - second * sine_table,
            second * cosine_table + first_half * sine_table,
        ],
        axis=-1,
    )


def unrotate(vector_in, cosine_table, sine_table):
    return rotate(vector_in, cosine_table, -sine_table)


VMEM_LIMIT = 56 * 2**20
ROWS_BY_ROWS = (((1,), (1,)), ((), ()))
COLS_BY_COLS = (((0,), (0,)), ((), ()))


def dot_f32(left, right, dims=(((1,), (0,)), ((), ()))):
    return lax.dot_general(left, right, dims, preferred_element_type=jnp.float32)


def attend(
    repeat, read_query, cosines, sines, seg_row, seg_col, keys, values, grad_ref, context_ref,
    query_grad_ref,
):
    rows = cosines.shape[0]
    score_scale = 1.0 / math.sqrt(HD)
    later = lax.broadcasted_iota(jnp.int32, (rows, rows), 0)
    sooner = lax.broadcasted_iota(jnp.int32, (rows, rows), 1)
    allowed = (seg_col == seg_row) & (sooner <= later)
    aligned = jnp.zeros((rows, HD), jnp.float32)
    key_parts, value_parts = [], []
    for group in range(len(keys)):
        key_part = jnp.zeros((rows, HD), jnp.float32)
        value_part = jnp.zeros((rows, HD), jnp.float32)
        for member in range(repeat):
            own = pl.ds((group * repeat + member) * HD, HD)
            plain = read_query(own)
            query = turn(plain, cosines, sines).astype(jnp.bfloat16)
            scores = dot_f32(query, keys[group], ROWS_BY_ROWS) * score_scale
            scores = jnp.where(allowed, scores, -1e30)
            exponents = jnp.exp(scores - jnp.max(scores, axis=1, keepdims=True))
            attention = exponents / jnp.sum(exponents, axis=1, keepdims=True)
            attention_bf = attention.astype(jnp.bfloat16)
            context_ref[:, own] = dot_f32(attention_bf, values[group]).astype(jnp.bfloat16)
            context_grad = grad_ref[:, own]
            grad_probs = dot_f32(context_grad, values[group], ROWS_BY_ROWS)
            mean = jnp.sum(grad_probs * attention, axis=1, keepdims=True)
            score_grad = (attention * (grad_probs - mean) * score_scale).astype(jnp.bfloat16)
            query_grad = turn(dot_f32(score_grad, keys[group]), cosines, -sines).astype(
                jnp.bfloat16
            )
            query_grad_ref[:, own] = query_grad
            aligned += query_grad.astype(jnp.float32) * plain
            key_part += dot_f32(score_grad, query, COLS_BY_COLS)
            value_part += dot_f32(attention_bf, context_grad, COLS_BY_COLS)
        key_parts.append(key_part)
        value_parts.append(value_part)
    return aligned, key_parts, value_parts


def turn(vector_in, cosines, sines):
    return vector_in * cosines + pltpu.roll(vector_in, HD // 2, 1) * sines


def attention_kernel(
    repeat, query_ref, scale_ref, cos_ref, sin_ref, seg_row_ref, seg_col_ref, key_ref, value_ref,
    grad_ref, context_ref, query_grad_ref, key_part_ref, value_part_ref, aligned_ref,
):
    row_scale = scale_ref[...]
    groups = [pl.ds(group * HD, HD) for group in range(key_ref.shape[1] // HD)]
    aligned, key_parts, value_parts = attend(
        repeat, lambda own: query_ref[:, own] * row_scale, cos_ref[...], sin_ref[...],
        seg_row_ref[...], seg_col_ref[...], [key_ref[:, shared] for shared in groups],
        [value_ref[:, shared] for shared in groups], grad_ref, context_ref, query_grad_ref,
    )
    for shared, key_part, value_part in zip(groups, key_parts, value_parts):
        key_part_ref[:, shared] = key_part
        value_part_ref[:, shared] = value_part
    aligned_ref[...] = jnp.sum(aligned, axis=1, keepdims=True)


def attention_parts(repeat, query_pre, inv_rms, cosines, sines, seg_row, keys, values, context_grad):
    rows = query_pre.shape[0]
    whole = pl.BlockSpec(memory_space=pltpu.VMEM)
    return pl.pallas_call(
        functools.partial(attention_kernel, repeat),
        in_specs=[whole] * 9,
        out_specs=[whole] * 5,
        out_shape=[
            jax.ShapeDtypeStruct(query_pre.shape, jnp.bfloat16),
            jax.ShapeDtypeStruct(query_pre.shape, jnp.bfloat16),
            jax.ShapeDtypeStruct(keys.shape, jnp.float32),
            jax.ShapeDtypeStruct(keys.shape, jnp.float32),
            jax.ShapeDtypeStruct((rows, 1), jnp.float32),
        ],
        compiler_params=pltpu.CompilerParams(vmem_limit_bytes=VMEM_LIMIT),
    )(
        query_pre, inv_rms, cosines, sines, seg_row[None, :], seg_row[:, None], keys, values,
        context_grad,
    )


def middle_kernel(
    repeat, gained_ref, q_weight_ref, kv_weight_ref, scale_ref, cos_ref, sin_ref, seg_row_ref,
    seg_col_ref, grad_ref, context_ref, aligned_ref, out_ref, gained, q_weight, kv_weight, out,
    query_sum, pair_sum, query_grad, sems,
):
    width, heads_cols = q_weight.shape
    pieces = sems.shape[1]
    step = width // pieces

    def part(piece):
        return pl.ds(pl.multiple_of(piece * step, step), step)

    def fetches(piece):
        span = part(piece)
        return (
            pltpu.make_async_copy(
                gained_ref.at[:, span], gained.at[:, span], sems.at[0, piece]
            ),
            pltpu.make_async_copy(q_weight_ref.at[span], q_weight.at[span], sems.at[1, piece]),
            pltpu.make_async_copy(kv_weight_ref.at[span], kv_weight.at[span], sems.at[2, piece]),
        )

    def returned(piece):
        span = part(piece)
        return pltpu.make_async_copy(out.at[:, span], out_ref.at[:, span], sems.at[3, piece])

    @pl.loop(0, pieces)
    def _(piece):
        for fetch in fetches(piece):
            fetch.start()

    query_sum[...] = jnp.zeros_like(query_sum)
    pair_sum[...] = jnp.zeros_like(pair_sum)

    @pl.loop(0, pieces)
    def _(piece):
        for fetch in fetches(piece):
            fetch.wait()
        span = part(piece)
        features = gained[:, span]
        query_sum[...] += dot_f32(features, q_weight[span, :])
        pair_sum[...] += dot_f32(features, kv_weight[span, :])

    row_scale = scale_ref[...]
    cosines, sines = cos_ref[...], sin_ref[...]
    groups = kv_weight.shape[1] // (2 * HD)
    pair_plain = pair_sum[...] * row_scale
    halves = [pair_plain[:, i * HD : (i + 1) * HD] for i in range(2 * groups)]
    aligned, key_parts, value_parts = attend(
        repeat, lambda own: query_sum[:, own] * row_scale, cosines, sines, seg_row_ref[...],
        seg_col_ref[...], [turn(half, cosines, sines).astype(jnp.bfloat16) for half in halves[::2]],
        [half.astype(jnp.bfloat16) for half in halves[1::2]], grad_ref, context_ref, query_grad,
    )
    pair_grads = []
    for key_part, value_part in zip(key_parts, value_parts):
        pair_grads.append(turn(key_part, cosines, -sines).astype(jnp.bfloat16))
        pair_grads.append(value_part.astype(jnp.bfloat16))
    for half, pair_grad in zip(halves, pair_grads):
        aligned += half * pair_grad.astype(jnp.float32)
    aligned_ref[...] = jnp.sum(aligned, axis=1, keepdims=True)
    pair_grad = jnp.concatenate(pair_grads, axis=1)

    @pl.loop(0, pieces)
    def _(piece):
        span = part(piece)
        out[:, span] = (
            dot_f32(query_grad[...], q_weight[span, :], ROWS_BY_ROWS)
            + dot_f32(pair_grad, kv_weight[span, :], ROWS_BY_ROWS)
        ).astype(out.dtype)
        returned(piece).start()

    @pl.loop(0, pieces)
    def _(piece):
        returned(piece).wait()


def middle(
    repeat, gained, q_weight, kv_weight, inv_rms, cosines, sines, seg_row, context_grad
):
    rows, width = gained.shape
    heads_cols, kv_cols = q_weight.shape[1], kv_weight.shape[1]
    whole, far = pl.BlockSpec(memory_space=pltpu.VMEM), pl.BlockSpec(memory_space=pl.ANY)
    return pl.pallas_call(
        functools.partial(middle_kernel, repeat),
        in_specs=[far] * 3 + [whole] * 6,
        out_specs=[whole] * 2 + [far],
        out_shape=[
            jax.ShapeDtypeStruct((rows, heads_cols), jnp.bfloat16),
            jax.ShapeDtypeStruct((rows, 1), jnp.float32),
            jax.ShapeDtypeStruct((rows, width), jnp.bfloat16),
        ],
        scratch_shapes=[
            pltpu.VMEM(gained.shape, jnp.bfloat16),
            pltpu.VMEM(q_weight.shape, jnp.bfloat16),
            pltpu.VMEM(kv_weight.shape, jnp.bfloat16),
            pltpu.VMEM(gained.shape, jnp.bfloat16),
            pltpu.VMEM((rows, heads_cols), jnp.float32),
            pltpu.VMEM((rows, kv_cols), jnp.float32),
            pltpu.VMEM((rows, heads_cols), jnp.bfloat16),
            pltpu.SemaphoreType.DMA((4, 8)),
        ],
        compiler_params=pltpu.CompilerParams(vmem_limit_bytes=VMEM_LIMIT),
    )(
        gained, q_weight, kv_weight, inv_rms, cosines, sines, seg_row[None, :], seg_row[:, None],
        context_grad,
    )


def stitch_kernel(packs, rank_ref, token_ref, source_ref, weight_ref, *refs):
    out_refs, product = refs[:packs], refs[-1]
    block = source_ref.shape[0]
    step = pl.program_id(0)
    here = pl.ds(pl.multiple_of(step * block, block), block)
    product[here, :] = dot_f32(source_ref[...], weight_ref[...]).astype(jnp.bfloat16)

    @pl.when(step == pl.num_programs(0) - 1)
    def _():
        pack_len = out_refs[0].shape[0]
        shape = (pack_len, product.shape[0])
        place = token_ref[...] - lax.broadcasted_iota(jnp.int32, shape, 0)
        for distance in range(packs):
            first = (rank_ref[0] ^ distance) * pack_len
            rows = (place == first).astype(jnp.float32).astype(jnp.bfloat16)
            out_refs[distance][...] = dot_f32(rows, product[...]).astype(jnp.bfloat16)


def stitched(packs, pack_len, rank, row_token, source, weight):
    rows, features = source.shape
    cols = weight.shape[1]
    block = min(512, rows)
    fixed = lambda i: (0, 0)
    return pl.pallas_call(
        functools.partial(stitch_kernel, packs),
        grid=(rows // block,),
        in_specs=[
            pl.BlockSpec(memory_space=pltpu.SMEM),
            pl.BlockSpec((1, rows), fixed),
            pl.BlockSpec((block, features), lambda i: (i, 0)),
            pl.BlockSpec(weight.shape, fixed),
        ],
        out_specs=[pl.BlockSpec((pack_len, cols), fixed)] * packs,
        out_shape=[jax.ShapeDtypeStruct((pack_len, cols), jnp.bfloat16)] * packs,
        scratch_shapes=[pltpu.VMEM((rows, cols), jnp.bfloat16)],
        compiler_params=pltpu.CompilerParams(vmem_limit_bytes=VMEM_LIMIT),
    )(rank.reshape(1), row_token[None, :], source, weight)


def back_kernel(query_ref, pair_ref, q_weight_ref, kv_weight_ref, out_ref):
    out_ref[...] = (
        dot_f32(query_ref[...], q_weight_ref[...], ROWS_BY_ROWS)
        + dot_f32(pair_ref[...], kv_weight_ref[...], ROWS_BY_ROWS)
    ).astype(out_ref.dtype)


def back_projected(grad_queries, grad_pairs, q_weight, kv_weight):
    rows = grad_queries.shape[0]
    width = q_weight.shape[0]
    block = 2048
    fixed = lambda i: (0, 0)
    return pl.pallas_call(
        back_kernel,
        grid=(width // block,),
        in_specs=[
            pl.BlockSpec(grad_queries.shape, fixed),
            pl.BlockSpec(grad_pairs.shape, fixed),
            pl.BlockSpec((block, q_weight.shape[1]), lambda i: (i, 0)),
            pl.BlockSpec((block, kv_weight.shape[1]), lambda i: (i, 0)),
        ],
        out_specs=pl.BlockSpec((rows, block), lambda i: (0, i)),
        out_shape=jax.ShapeDtypeStruct((rows, width), jnp.bfloat16),
        compiler_params=pltpu.CompilerParams(vmem_limit_bytes=VMEM_LIMIT),
    )(grad_queries, grad_pairs, q_weight, kv_weight)


def outer_kernel(*refs):
    features_ref, out_ref = refs[0], refs[-1]
    total = None
    for place, grad_ref in enumerate(refs[1:-1]):
        rows = grad_ref.shape[0]
        term = dot_f32(features_ref[:, pl.ds(place * rows, rows)], grad_ref[...])
        total = term if total is None else total + term
    out_ref[...] = total


def outer_summed(features, grads):
    block = min(512, features.shape[0])
    cols = grads[0].shape[1]
    return pl.pallas_call(
        outer_kernel,
        grid=(features.shape[0] // block,),
        in_specs=[pl.BlockSpec((block, features.shape[1]), lambda i: (i, 0))]
        + [pl.BlockSpec(grad.shape, lambda i: (0, 0)) for grad in grads],
        out_specs=pl.BlockSpec((block, cols), lambda i: (i, 0)),
        out_shape=jax.ShapeDtypeStruct((features.shape[0], cols), jnp.float32),
        compiler_params=pltpu.CompilerParams(vmem_limit_bytes=20 * 2**20),
    )(features, *grads)


STAY, FIRST, SECOND, LAST = (0, 1, 2, 3), (1, 3, 0, 2), (2, 0, 3, 1), (3, 2, 1, 0)


OUTWARD = [(0, 1), (1, 0), (2, 3), (3, 2)]
INSIDE = [(0, 1), (1, 0), (2, 4), (3, 5), (4, 2), (5, 3), (6, 7), (7, 6)]


def is_inner():
    chip = lax.axis_index("tp") // 2
    return (chip == 1) | (chip == 2)


def along(value, pairs):
    both = [(2 * start + core, 2 * end + core) for start, end in pairs for core in range(2)]
    return lax.ppermute(value, "tp", both)


def towards(table):
    return [(start, end) for start, end in enumerate(table)]


def arriving(table):
    return [(start, end) for end, start in enumerate(table)]


def after(value, done):
    value, done = lax.optimization_barrier((value, done))
    return value, done


def gather_begun(block):
    return along(block, arriving(FIRST))


def gather_second(block):
    return along(block, arriving(SECOND))


def gather_last(block, first):
    return along(first, OUTWARD), lax.ppermute(block, "tp", INSIDE)


def early_blocks(block, first):
    return [block, swapped(block, "tp", 1), first, swapped(first, "tp", 1)]


def late_blocks(second, last):
    far, near = last
    last = jnp.where(is_inner(), near, far)
    return [second, swapped(second, "tp", 1), last, swapped(last, "tp", 1)]


def both_cores(parts, place):
    other = swapped(parts[2 * place + 1], "tp", 1)
    return parts[2 * place].astype(jnp.float32) + other.astype(jnp.float32)


def scatter_begun(parts):
    last = both_cores(parts, 0).astype(jnp.bfloat16)
    return last, along(last, OUTWARD), lax.ppermute(last, "tp", INSIDE)


def scatter_second(parts):
    return along(both_cores(parts, 1).astype(jnp.bfloat16), towards(SECOND))


def scatter_first(parts, far):
    first = both_cores(parts, 2)
    first += jnp.where(is_inner(), far.astype(jnp.float32), 0.0)
    return along(first.astype(jnp.bfloat16), towards(FIRST))


def scatter_total(parts, near, second, first):
    total = both_cores(parts, 3) + jnp.where(is_inner(), near.astype(jnp.float32), 0.0)
    return total + second.astype(jnp.float32) + first.astype(jnp.float32)


def line_stitch_half(blocks, rows, rows_ref, weight_ref, product, here, sems, out_sem):
    block = blocks[0].shape[0]
    fetches = [
        pltpu.make_async_copy(blocks[i], rows.at[pl.ds(i * block, block)], sems.at[i])
        for i in range(4)
    ]
    for fetch in fetches:
        fetch.start()
    for fetch in fetches:
        fetch.wait()
    kept = pltpu.make_async_copy(rows, rows_ref, out_sem)
    kept.start()
    product[here, :] = dot_f32(rows[...], weight_ref[...]).astype(jnp.bfloat16)
    return kept


def line_stitch_early_kernel(weight_ref, *refs):
    blocks, (product_ref, rows_ref, rows, sems, out_sem) = refs[:4], refs[4:]
    everything = pl.ds(0, rows.shape[0])
    line_stitch_half(
        blocks, rows, rows_ref, weight_ref, product_ref, everything, sems, out_sem
    ).wait()


def line_stitch_kernel(packs, rank_ref, token_ref, weight_ref, early_ref, *refs):
    blocks, out_refs = refs[:4], refs[4 : 4 + packs]
    rows_ref, rows, product, sems, out_sem = refs[4 + packs :]
    half = rows.shape[0]
    kept = line_stitch_half(
        blocks, rows, rows_ref, weight_ref, product, pl.ds(half, half), sems, out_sem
    )
    product[pl.ds(0, half), :] = early_ref[...]
    pack_len = out_refs[0].shape[0]
    place = token_ref[...] - lax.broadcasted_iota(jnp.int32, (pack_len, product.shape[0]), 0)
    for distance in range(packs):
        first = (rank_ref[0] ^ distance) * pack_len
        chosen = (place == first).astype(jnp.float32).astype(jnp.bfloat16)
        out_refs[distance][...] = dot_f32(chosen, product[...]).astype(jnp.bfloat16)
    kept.wait()


def line_stitched_early(blocks, weight):
    block, features = blocks[0].shape
    cols = weight.shape[1]
    whole, far = pl.BlockSpec(memory_space=pltpu.VMEM), pl.BlockSpec(memory_space=pl.ANY)
    return pl.pallas_call(
        line_stitch_early_kernel,
        in_specs=[whole] + [far] * 4,
        out_specs=[whole, far],
        out_shape=[
            jax.ShapeDtypeStruct((4 * block, cols), jnp.bfloat16),
            jax.ShapeDtypeStruct((4 * block, features), jnp.bfloat16),
        ],
        scratch_shapes=[
            pltpu.VMEM((4 * block, features), jnp.bfloat16),
            pltpu.SemaphoreType.DMA((4,)),
            pltpu.SemaphoreType.DMA,
        ],
        compiler_params=pltpu.CompilerParams(vmem_limit_bytes=20 * 2**20),
    )(weight, *blocks)


def line_stitched(packs, pack_len, rank, token_row, early, blocks, weight):
    block, features = blocks[0].shape
    cols = weight.shape[1]
    whole, far = pl.BlockSpec(memory_space=pltpu.VMEM), pl.BlockSpec(memory_space=pl.ANY)
    results = pl.pallas_call(
        functools.partial(line_stitch_kernel, packs),
        in_specs=[pl.BlockSpec(memory_space=pltpu.SMEM)] + [whole] * 3 + [far] * 4,
        out_specs=[whole] * packs + [far],
        out_shape=[jax.ShapeDtypeStruct((pack_len, cols), jnp.bfloat16)] * packs
        + [jax.ShapeDtypeStruct((4 * block, features), jnp.bfloat16)],
        scratch_shapes=[
            pltpu.VMEM((4 * block, features), jnp.bfloat16),
            pltpu.VMEM((8 * block, cols), jnp.bfloat16),
            pltpu.SemaphoreType.DMA((4,)),
            pltpu.SemaphoreType.DMA,
        ],
        compiler_params=pltpu.CompilerParams(vmem_limit_bytes=24 * 2**20),
    )(rank.reshape(1), token_row, weight, early, *blocks)
    return results[:packs], results[packs]


def line_grad_kernel(chips_ref, core_ref, weight_ref, *refs):
    blocks, out_ref, features, total, sems = refs[:8], *refs[8:]
    step = pl.program_id(0)
    cols = blocks[0].shape[1]

    def fetch(place, half):
        core = core_ref[0] if half == 0 else 1 - core_ref[0]
        there = features.at[place, :, pl.ds(pl.multiple_of(core * cols, cols), cols)]
        return there, sems.at[place, half]

    @pl.when(step == 0)
    def _():
        for i in range(8):
            pltpu.make_async_copy(blocks[i], *fetch(i // 2, i % 2)).start()
        total[...] = jnp.zeros_like(total)

    for half in range(2):
        pltpu.make_async_copy(blocks[half], *fetch(step, half)).wait()
    total[...] += dot_f32(features[step], weight_ref[...], ROWS_BY_ROWS)

    @pl.when(step == 3)
    def _():
        out_ref[...] = total[...].astype(out_ref.dtype)


def line_grad_context(chips, core, blocks, weight):
    rows, cols = blocks[0].shape
    heads_cols = weight.shape[0]
    far = pl.BlockSpec(memory_space=pl.ANY)
    return pl.pallas_call(
        line_grad_kernel,
        grid_spec=pltpu.PrefetchScalarGridSpec(
            num_scalar_prefetch=2,
            grid=(4,),
            in_specs=[pl.BlockSpec((heads_cols, 2 * cols), lambda i, chips, core: (0, chips[i]))]
            + [far] * 8,
            out_specs=pl.BlockSpec((rows, heads_cols), lambda i, chips, core: (0, 0)),
            scratch_shapes=[
                pltpu.VMEM((4, rows, 2 * cols), jnp.bfloat16),
                pltpu.VMEM((rows, heads_cols), jnp.float32),
                pltpu.SemaphoreType.DMA((4, 2)),
            ],
        ),
        out_shape=jax.ShapeDtypeStruct((rows, heads_cols), jnp.bfloat16),
        compiler_params=pltpu.CompilerParams(vmem_limit_bytes=VMEM_LIMIT),
    )(chips, core.reshape(1), weight, *blocks)


def line_attended_kernel(chips_ref, core_ref, context_ref, weight_ref, *refs):
    out_refs, product = refs[:8], refs[8]
    step = pl.program_id(0)
    cols = out_refs[0].shape[1]
    product[...] = dot_f32(context_ref[...], weight_ref[...]).astype(jnp.bfloat16)
    for i in range(4):

        @pl.when(step == i)
        def _(i=i):
            for half in range(2):
                core = core_ref[0] if half == 0 else 1 - core_ref[0]
                here = pl.ds(pl.multiple_of(core * cols, cols), cols)
                out_refs[2 * i + half][...] = product[:, here]


def line_attended(chips, core, context, weight):
    rows, heads_cols = context.shape
    cols = weight.shape[1] // 8
    fixed = lambda i, chips, core: (0, 0)
    return pl.pallas_call(
        line_attended_kernel,
        grid_spec=pltpu.PrefetchScalarGridSpec(
            num_scalar_prefetch=2,
            grid=(4,),
            in_specs=[
                pl.BlockSpec((rows, heads_cols), fixed),
                pl.BlockSpec((heads_cols, 2 * cols), lambda i, chips, core: (0, chips[i])),
            ],
            out_specs=[pl.BlockSpec((rows, cols), fixed)] * 8,
            scratch_shapes=[pltpu.VMEM((rows, 2 * cols), jnp.bfloat16)],
        ),
        out_shape=[jax.ShapeDtypeStruct((rows, cols), jnp.bfloat16)] * 8,
        compiler_params=pltpu.CompilerParams(vmem_limit_bytes=VMEM_LIMIT),
    )(chips, core.reshape(1), context, weight)


def line_project(
    places, from_ref, gain_ref, q_weight_ref, kv_weight_ref, blocks, hidden, q_weight, kv_weight,
    sems, query_sum, pair_sum, squares,
):
    rows, step = blocks[0].shape

    def part(place):
        return pl.ds(pl.multiple_of(from_ref[place] * step, step), step)

    def fetches(place):
        span = part(place)
        return (
            pltpu.make_async_copy(q_weight_ref.at[span], q_weight.at[span], sems.at[1, place]),
            pltpu.make_async_copy(kv_weight_ref.at[span], kv_weight.at[span], sems.at[2, place]),
        )

    def features(place):
        return pltpu.make_async_copy(blocks[0], hidden.at[place], sems.at[0, place])

    later = [place for place in range(len(blocks)) if place not in places]
    for place in [*places, *later]:
        pltpu.make_async_copy(blocks[place], hidden.at[place], sems.at[0, place]).start()
        for fetch in fetches(place):
            fetch.start()

    def project(place, squares):
        features(place).wait()
        for fetch in fetches(place):
            fetch.wait()
        span = part(place)
        wide = hidden[place].astype(jnp.float32)
        gained = (wide * gain_ref[:, span]).astype(jnp.bfloat16)
        query_sum[...] += dot_f32(gained, q_weight[span, :])
        pair_sum[...] += dot_f32(gained, kv_weight[span, :])
        return squares + jnp.sum(wide * wide, axis=1, keepdims=True)

    squares = lax.fori_loop(places[0], places[-1] + 1, project, squares)

    def finish():
        for place in later:
            features(place).wait()
            for fetch in fetches(place):
                fetch.wait()

    return squares, finish


def line_projected_kernel(
    from_ref, gain_ref, q_weight_ref, kv_weight_ref, *refs,
):
    blocks, (query_sum, pair_sum, squares_ref) = refs[:4], refs[4:7]
    hidden, q_weight, kv_weight, sems = refs[7:]
    query_sum[...] = jnp.zeros_like(query_sum)
    pair_sum[...] = jnp.zeros_like(pair_sum)
    squares, _ = line_project(
        range(4), from_ref, gain_ref, q_weight_ref, kv_weight_ref, blocks, hidden, q_weight,
        kv_weight, sems, query_sum, pair_sum, jnp.zeros(squares_ref.shape, jnp.float32),
    )
    squares_ref[...] = squares


def line_projected(sources, blocks, gain, q_weight, kv_weight):
    rows, step = blocks[0].shape
    heads_cols, kv_cols = q_weight.shape[1], kv_weight.shape[1]
    whole, far = pl.BlockSpec(memory_space=pltpu.VMEM), pl.BlockSpec(memory_space=pl.ANY)
    return pl.pallas_call(
        line_projected_kernel,
        in_specs=[pl.BlockSpec(memory_space=pltpu.SMEM), whole] + [far] * 6,
        out_specs=[whole] * 3,
        out_shape=[
            jax.ShapeDtypeStruct((rows, heads_cols), jnp.float32),
            jax.ShapeDtypeStruct((rows, kv_cols), jnp.float32),
            jax.ShapeDtypeStruct((rows, 1), jnp.float32),
        ],
        scratch_shapes=[
            pltpu.VMEM((4, rows, step), jnp.bfloat16),
            pltpu.VMEM(q_weight.shape, jnp.bfloat16),
            pltpu.VMEM(kv_weight.shape, jnp.bfloat16),
            pltpu.SemaphoreType.DMA((3, 4)),
        ],
        compiler_params=pltpu.CompilerParams(vmem_limit_bytes=VMEM_LIMIT),
    )(sources, gain[None, :], q_weight, kv_weight, *blocks)


def line_tokens_kernel(token_ref, order_ref, early_ref, late_ref, out_ref):
    half = early_ref.shape[0]
    total = None
    for place, rows_ref in enumerate((early_ref, late_ref)):
        tokens = token_ref[pl.ds(place * half, half), :]
        chosen = (tokens == order_ref[...]).astype(jnp.float32).astype(jnp.bfloat16)
        term = dot_f32(rows_ref[...], chosen, COLS_BY_COLS)
        total = term if total is None else total + term
    out_ref[...] = total.astype(out_ref.dtype)


def line_tokens_last(token_col, token_order, early_rows, late_rows):
    half, features = early_rows.shape
    tokens = token_order.shape[1]
    block = min(1024, features)
    fixed = lambda i: (0, 0)
    return pl.pallas_call(
        line_tokens_kernel,
        grid=(features // block,),
        in_specs=[
            pl.BlockSpec((2 * half, 1), fixed),
            pl.BlockSpec((1, tokens), fixed),
            pl.BlockSpec((half, block), lambda i: (0, i)),
            pl.BlockSpec((half, block), lambda i: (0, i)),
        ],
        out_specs=pl.BlockSpec((block, tokens), lambda i: (i, 0)),
        out_shape=jax.ShapeDtypeStruct((features, tokens), jnp.bfloat16),
        compiler_params=pltpu.CompilerParams(vmem_limit_bytes=VMEM_LIMIT),
    )(token_col, token_order, early_rows, late_rows)


def line_middle_kernel(
    repeat, from_ref, to_ref, gain_ref, cos_ref, sin_ref, seg_row_ref, seg_col_ref, grad_ref,
    early_query_ref, early_pair_ref, early_squares_ref, q_weight_ref, kv_weight_ref, *refs,
):
    blocks, context_ref, out_refs = refs[:8], refs[8], refs[9:17]
    hidden, q_weight, kv_weight, out, query_sum, pair_sum, query_grad, sems, out_sems = refs[17:]
    width = q_weight.shape[0]
    rows, step = blocks[0].shape

    def part(rank):
        return pl.ds(pl.multiple_of(rank * step, step), step)

    query_sum[...] = early_query_ref[...]
    pair_sum[...] = early_pair_ref[...]
    squares, finish = line_project(
        range(4, 8), from_ref, gain_ref, q_weight_ref, kv_weight_ref, blocks, hidden, q_weight,
        kv_weight, sems, query_sum, pair_sum, early_squares_ref[...],
    )
    row_scale = lax.rsqrt(squares / width + epsilon)
    cosines, sines = cos_ref[...], sin_ref[...]
    groups = kv_weight.shape[1] // (2 * HD)
    pair_plain = pair_sum[...] * row_scale
    halves = [pair_plain[:, i * HD : (i + 1) * HD] for i in range(2 * groups)]
    aligned, key_parts, value_parts = attend(
        repeat, lambda own: query_sum[:, own] * row_scale, cosines, sines, seg_row_ref[...],
        seg_col_ref[...], [turn(half, cosines, sines).astype(jnp.bfloat16) for half in halves[::2]],
        [half.astype(jnp.bfloat16) for half in halves[1::2]], grad_ref, context_ref, query_grad,
    )
    pair_grads = []
    for key_part, value_part in zip(key_parts, value_parts):
        pair_grads.append(turn(key_part, cosines, -sines).astype(jnp.bfloat16))
        pair_grads.append(value_part.astype(jnp.bfloat16))
    for half, pair_grad in zip(halves, pair_grads):
        aligned += half * pair_grad.astype(jnp.float32)
    aligned = jnp.sum(aligned, axis=1, keepdims=True) * (row_scale * row_scale / width)
    pair_grad = jnp.concatenate(pair_grads, axis=1)
    finish()

    @pl.loop(0, 8)
    def _(place):
        span = part(to_ref[place])
        grad_normed = dot_f32(query_grad[...], q_weight[span, :], ROWS_BY_ROWS)
        grad_normed += dot_f32(pair_grad, kv_weight[span, :], ROWS_BY_ROWS)
        features = hidden[6 - 2 * (place // 2) + place % 2].astype(jnp.float32)
        out[place] = (
            grad_normed * (row_scale * gain_ref[:, span]) - features * aligned
        ).astype(out.dtype)
        for i in range(8):

            @pl.when(place == i)
            def _(i=i):
                pltpu.make_async_copy(out.at[i], out_refs[i], out_sems.at[i]).start()

    for i in range(8):
        pltpu.make_async_copy(out.at[i], out_refs[i], out_sems.at[i]).wait()


def line_middle(
    repeat, sources, targets, blocks, early_sums, gain, q_weight, kv_weight, cosines, sines, seg_row,
    seg_col, context_grad,
):
    rows, step = blocks[0].shape
    heads_cols, kv_cols = q_weight.shape[1], kv_weight.shape[1]
    whole, far = pl.BlockSpec(memory_space=pltpu.VMEM), pl.BlockSpec(memory_space=pl.ANY)
    scalars = pl.BlockSpec(memory_space=pltpu.SMEM)
    results = pl.pallas_call(
        functools.partial(line_middle_kernel, repeat),
        in_specs=[scalars] * 2 + [whole] * 9 + [far] * 10,
        out_specs=[whole] + [far] * 8,
        out_shape=[jax.ShapeDtypeStruct((rows, heads_cols), jnp.bfloat16)]
        + [jax.ShapeDtypeStruct((rows, step), jnp.bfloat16)] * 8,
        scratch_shapes=[
            pltpu.VMEM((8, rows, step), jnp.bfloat16),
            pltpu.VMEM(q_weight.shape, jnp.bfloat16),
            pltpu.VMEM(kv_weight.shape, jnp.bfloat16),
            pltpu.VMEM((8, rows, step), jnp.bfloat16),
            pltpu.VMEM((rows, heads_cols), jnp.float32),
            pltpu.VMEM((rows, kv_cols), jnp.float32),
            pltpu.VMEM((rows, heads_cols), jnp.bfloat16),
            pltpu.SemaphoreType.DMA((3, 8)),
            pltpu.SemaphoreType.DMA((8,)),
        ],
        compiler_params=pltpu.CompilerParams(vmem_limit_bytes=VMEM_LIMIT),
    )(
        sources, targets, gain[None, :], cosines, sines, seg_row[None, :], seg_col,
        context_grad, *early_sums, q_weight, kv_weight, *blocks,
    )
    return results[0], results[1:]


def line_body(
    source, row_token, seg_ids, stitch_weight, norm_gain, q_weight, kv_weight, o_weight, out_grad
):
    tok_rank = lax.axis_index("tok")
    tp_rank = lax.axis_index("tp")
    packs = lax.axis_size("tok")
    pack_len = seg_ids.shape[1]
    width = q_weight.shape[0]
    own_cols = stitch_weight.shape[1]
    repeat = (q_weight.shape[1] // HD) // (kv_weight.shape[1] // (2 * HD))
    chip, core = tp_rank // 2, tp_rank % 2

    def chips(tables):
        return jnp.array(tables, jnp.int32)[:, chip]

    def ranks(tables):
        pairs = 2 * chips(tables)
        return jnp.stack([pairs + core, pairs + 1 - core], axis=1).reshape(-1)

    arrival, departure = (STAY, FIRST, SECOND, LAST), (LAST, SECOND, FIRST, STAY)
    sources, targets = ranks(arrival), ranks(departure)

    within = jnp.arange(pack_len, dtype=jnp.int32)
    seg_row = seg_ids[0]
    earlier = jnp.sum((seg_row[None, :] < seg_row[:, None]).astype(jnp.int32), axis=1)
    angles = (within - earlier).astype(jnp.float32)[:, None] * frequencies()[None, :]
    cosine, sine = jnp.cos(angles), jnp.sin(angles)
    cosines = jnp.concatenate([cosine, cosine], axis=1)
    sines = jnp.concatenate([-sine, sine], axis=1)

    token_row = row_token.reshape(8, -1)[sources].reshape(1, -1)
    first = gather_begun(source)
    seg_col, token_col = seg_row[:, None], token_row.reshape(-1, 1)
    arrivals, departures = chips(arrival), chips(departure)
    small = (token_row, token_col, seg_col, cosines, sines, sources, targets, arrivals, departures)
    source, (first, small) = after(source, (first, small))
    token_row, token_col, seg_col, cosines, sines, sources, targets, arrivals, departures = small
    second, last = gather_second(source), gather_last(source, first)
    early_source = early_blocks(source, first)
    early_product, early_rows = line_stitched_early(early_source, stitch_weight)
    out_grad, (second, last, early_product) = after(out_grad, (second, last, early_product))
    late_source = late_blocks(second, last)
    og_first = gather_begun(out_grad)
    placed, late_rows = line_stitched(
        packs, pack_len, tok_rank, token_row, early_product, late_source, stitch_weight
    )
    received = [swapped(placed[distance], "tok", distance) for distance in range(1, packs)]
    received[0], og_first = after(received[0], og_first)
    og_second, og_last = gather_second(out_grad), gather_last(out_grad, og_first)
    hidden = placed[0].astype(jnp.float32)
    for part in received:
        hidden += part.astype(jnp.float32)
    hidden_bf = hidden.astype(jnp.bfloat16)
    hidden_first = gather_begun(hidden_bf)
    early_rows, hidden_bf = after(early_rows, hidden_bf)
    token_order = (
        (tok_rank ^ jnp.arange(packs, dtype=jnp.int32))[:, None] * pack_len + within[None, :]
    ).reshape(-1)
    tokens_last = line_tokens_last(token_col, token_order[None, :], early_rows, late_rows)
    (hidden_bf, hidden_first), (og_second, og_last, tokens_last) = after(
        (hidden_bf, hidden_first), (og_second, og_last, tokens_last)
    )
    hidden_second, hidden_last = gather_second(hidden_bf), gather_last(hidden_bf, hidden_first)
    og_blocks = early_blocks(out_grad, og_first) + late_blocks(og_second, og_last)
    grad_context = line_grad_context(arrivals, core, og_blocks, o_weight)
    early_hidden = early_blocks(hidden_bf, hidden_first)
    early_sums = line_projected(sources, early_hidden, norm_gain, q_weight, kv_weight)
    hidden_last, (hidden_second, grad_context, early_sums) = after(
        hidden_last, (hidden_second, grad_context, early_sums)
    )
    hidden_blocks = early_hidden + late_blocks(hidden_second, hidden_last)

    context, grad_parts = line_middle(
        repeat, sources, targets, hidden_blocks, early_sums, norm_gain, q_weight, kv_weight,
        cosines, sines, seg_row, seg_col, grad_context,
    )
    last, far, near = scatter_begun(grad_parts)
    context, last = after(context, last)
    attended_parts = line_attended(departures, core, context, o_weight)
    second = scatter_second(grad_parts)
    far, (near, attended_parts) = after(far, (near, attended_parts))
    first = scatter_first(grad_parts, far)
    grad_sum = scatter_total(grad_parts, near, second, first)
    grad_hidden = (out_grad.astype(jnp.float32) + grad_sum).astype(jnp.bfloat16)
    every_pack = [grad_hidden] + [
        swapped(grad_hidden, "tok", distance) for distance in range(1, packs)
    ]
    _, far, near = scatter_begun(attended_parts)
    second = scatter_second(attended_parts)
    first = scatter_first(attended_parts, far)
    late_hidden, near, second, *every_pack = lax.optimization_barrier(
        (hidden_bf, near, second, *every_pack)
    )
    stitch_grad = outer_summed(tokens_last, every_pack)
    attended = scatter_total(attended_parts, near, second, first)
    layer_out = (late_hidden.astype(jnp.float32) + attended).astype(jnp.bfloat16)
    return (layer_out, stitch_grad)


def body(
    source, row_token, seg_ids, stitch_weight, norm_gain, q_weight, kv_weight, o_weight, out_grad
):
    tok_rank = lax.axis_index("tok")
    tp_rank = lax.axis_index("tp")
    packs = lax.axis_size("tok")
    pack_len = seg_ids.shape[1]
    width = q_weight.shape[0]
    own_cols = stitch_weight.shape[1]
    own_gain = lax.dynamic_slice_in_dim(norm_gain, tp_rank * own_cols, own_cols)

    gathered = lax.all_gather(source, "tp", axis=0, tiled=True)
    placed = stitched(packs, pack_len, tok_rank, row_token, gathered, stitch_weight)
    within = jnp.arange(pack_len, dtype=jnp.int32)
    hidden = placed[0].astype(jnp.float32)
    for distance in range(1, packs):
        hidden += swapped(placed[distance], "tok", distance).astype(jnp.float32)
    hidden_bf = hidden.astype(jnp.bfloat16)
    hidden_f = hidden_bf.astype(jnp.float32)
    square_sum = summed(jnp.sum(hidden_f * hidden_f, axis=1), "tp")
    inv_rms = lax.rsqrt(square_sum / width + epsilon)[:, None]
    gained = lax.all_gather((hidden_f * own_gain).astype(jnp.bfloat16), "tp", axis=1, tiled=True)

    token_order = (
        (tok_rank ^ jnp.arange(packs, dtype=jnp.int32))[:, None] * pack_len + within[None, :]
    ).reshape(-1)
    order = (row_token[:, None] == token_order[None, :]).astype(jnp.bfloat16)
    tokens_last = dot_f32(gathered, order, COLS_BY_COLS).astype(jnp.bfloat16)

    seg_row = seg_ids[0]
    earlier = jnp.sum((seg_row[None, :] < seg_row[:, None]).astype(jnp.int32), axis=1)
    angles = (within - earlier).astype(jnp.float32)[:, None] * frequencies()[None, :]
    cosine, sine = jnp.cos(angles), jnp.sin(angles)
    cosines = jnp.concatenate([cosine, cosine], axis=1)
    sines = jnp.concatenate([-sine, sine], axis=1)
    local_heads = q_weight.shape[1] // HD
    kv_cols = kv_weight.shape[1]
    paired = kv_cols == HD
    kv_local = 1 if paired else kv_cols // (2 * HD)
    repeat = local_heads // kv_local
    every_grad = lax.all_gather(out_grad, "tp", axis=1, tiled=True)
    grad_context = lax.dot_general(
        every_grad, o_weight, (((1,), (1,)), ((), ())), preferred_element_type=jnp.float32
    ).astype(jnp.bfloat16)
    if paired:
        query_pre = jnp.dot(gained, q_weight, preferred_element_type=jnp.float32)
        projected = jnp.dot(gained, kv_weight, preferred_element_type=jnp.float32) * inv_rms
        is_key = tp_rank % 2 == 0
        own_part = jnp.where(is_key, rotate(projected, cosine, sine), projected).astype(
            jnp.bfloat16
        )
        partner = swapped(own_part, "tp", 1)
        keys = jnp.where(is_key, own_part, partner)
        values = jnp.where(is_key, partner, own_part)
        context, grad_queries, key_part, value_part, aligned = attention_parts(
            repeat, query_pre, inv_rms, cosines, sines, seg_row, keys, values, grad_context
        )
        outgoing = jnp.where(is_key, value_part, key_part)
        incoming = swapped(outgoing.astype(jnp.bfloat16), "tp", 1).astype(outgoing.dtype)
        own_sum = jnp.where(is_key, key_part, value_part) + incoming
        grad_pairs = jnp.where(is_key, unrotate(own_sum, cosine, sine), own_sum).astype(
            jnp.bfloat16
        )
        aligned += jnp.sum(grad_pairs.astype(jnp.float32) * projected, axis=1, keepdims=True)
        grad_normed = back_projected(grad_queries, grad_pairs, q_weight, kv_weight)
    else:
        context, aligned, grad_normed = middle(
            repeat, gained, q_weight, kv_weight, inv_rms, cosines, sines, seg_row, grad_context
        )
    aligned = summed(aligned[:, 0], "tp")[:, None]
    grad_sum = lax.psum_scatter(grad_normed, "tp", scatter_dimension=1, tiled=True)
    attended = jnp.dot(context, o_weight, preferred_element_type=jnp.float32).astype(jnp.bfloat16)
    attended, grad_sum = lax.optimization_barrier((attended, grad_sum))
    grad_hidden = (
        out_grad.astype(jnp.float32)
        + inv_rms * own_gain * grad_sum.astype(jnp.float32)
        - hidden_f * (inv_rms * inv_rms * aligned / width)
    ).astype(jnp.bfloat16)
    every_pack = [grad_hidden] + [
        swapped(grad_hidden, "tok", distance) for distance in range(1, packs)
    ]
    late_hidden, *every_pack = lax.optimization_barrier((hidden_bf, *every_pack))
    stitch_grad = outer_summed(tokens_last, every_pack)

    attended = lax.psum_scatter(attended, "tp", scatter_dimension=1, tiled=True)
    layer_out = (late_hidden.astype(jnp.float32) + attended.astype(jnp.float32)).astype(
        jnp.bfloat16
    )
    return (layer_out, stitch_grad)


def solution(mesh):
    placed = (
        P("tp", "tok"),
        P(),
        P("tok", None),
        P("tok", "tp"),
        P(),
        P(None, "tp"),
        P(None, "tp"),
        P("tp", None),
        P("tok", "tp"),
    )
    on_line = mesh.shape["tp"] == 8
    return jax.shard_map(
        line_body if on_line else body,
        mesh=mesh,
        in_specs=placed,
        out_specs=(P("tok", "tp"), P("tok", "tp")),
        check_vma=False,
    )
```

```python
import functools
import math

import jax
import jax.numpy as jnp
from jax import lax
from jax.experimental import pallas as pl
from jax.experimental.pallas import tpu as pltpu
from jax.sharding import PartitionSpec as P

HD = 128


epsilon = 1e-05


def swapped(value, axis, mask):
    pairs = [(source, source ^ mask) for source in range(lax.axis_size(axis))]
    return lax.ppermute(value, axis, pairs)


def summed(value, axis):
    mask = 1
    while mask < lax.axis_size(axis):
        value = value + swapped(value, axis, mask)
        mask *= 2
    return value


def frequencies():
    exponent = jnp.arange(0, HD, 2).astype(jnp.float32) / HD
    plain_rate = 500000.0 ** (-exponent)
    wavelength = 2.0 * math.pi / plain_rate
    smoothing = (8192.0 / wavelength - 1.0) / 3.0
    blended = (1.0 - smoothing) * plain_rate / 8.0 + smoothing * plain_rate
    return jnp.where(
        wavelength < 2048.0, plain_rate, jnp.where(wavelength > 8192.0, plain_rate / 8.0, blended)
    )


def rotate(vector_in, cosine_table, sine_table):
    half_size = vector_in.shape[-1] // 2
    first_half = vector_in[..., :half_size]
    second = vector_in[..., half_size:]
    return jnp.concatenate(
        [
            first_half * cosine_table - second * sine_table,
            second * cosine_table + first_half * sine_table,
        ],
        axis=-1,
    )


def unrotate(vector_in, cosine_table, sine_table):
    return rotate(vector_in, cosine_table, -sine_table)


VMEM_LIMIT = 56 * 2**20
ROWS_BY_ROWS = (((1,), (1,)), ((), ()))
COLS_BY_COLS = (((0,), (0,)), ((), ()))


def dot_f32(left, right, dims=(((1,), (0,)), ((), ()))):
    return lax.dot_general(left, right, dims, preferred_element_type=jnp.float32)


def attend(
    repeat, read_query, cosines, sines, seg_row, seg_col, keys, values, grad_ref, context_ref,
    query_grad_ref,
):
    rows = cosines.shape[0]
    score_scale = 1.0 / math.sqrt(HD)
    later = lax.broadcasted_iota(jnp.int32, (rows, rows), 0)
    sooner = lax.broadcasted_iota(jnp.int32, (rows, rows), 1)
    allowed = (seg_col == seg_row) & (sooner <= later)
    aligned = jnp.zeros((rows, HD), jnp.float32)
    key_parts, value_parts = [], []
    for group in range(len(keys)):
        key_part = jnp.zeros((rows, HD), jnp.float32)
        value_part = jnp.zeros((rows, HD), jnp.float32)
        for member in range(repeat):
            own = pl.ds((group * repeat + member) * HD, HD)
            plain = read_query(own)
            query = turn(plain, cosines, sines).astype(jnp.bfloat16)
            scores = dot_f32(query, keys[group], ROWS_BY_ROWS) * score_scale
            scores = jnp.where(allowed, scores, -1e30)
            exponents = jnp.exp(scores - jnp.max(scores, axis=1, keepdims=True))
            attention = exponents / jnp.sum(exponents, axis=1, keepdims=True)
            attention_bf = attention.astype(jnp.bfloat16)
            context_ref[:, own] = dot_f32(attention_bf, values[group]).astype(jnp.bfloat16)
            context_grad = grad_ref[:, own]
            grad_probs = dot_f32(context_grad, values[group], ROWS_BY_ROWS)
            mean = jnp.sum(grad_probs * attention, axis=1, keepdims=True)
            score_grad = (attention * (grad_probs - mean) * score_scale).astype(jnp.bfloat16)
            query_grad = turn(dot_f32(score_grad, keys[group]), cosines, -sines).astype(
                jnp.bfloat16
            )
            query_grad_ref[:, own] = query_grad
            aligned += query_grad.astype(jnp.float32) * plain
            key_part += dot_f32(score_grad, query, COLS_BY_COLS)
            value_part += dot_f32(attention_bf, context_grad, COLS_BY_COLS)
        key_parts.append(key_part)
        value_parts.append(value_part)
    return aligned, key_parts, value_parts


def turn(vector_in, cosines, sines):
    return vector_in * cosines + pltpu.roll(vector_in, HD // 2, 1) * sines


def attention_kernel(
    repeat, query_ref, scale_ref, cos_ref, sin_ref, seg_row_ref, seg_col_ref, key_ref, value_ref,
    grad_ref, context_ref, query_grad_ref, key_part_ref, value_part_ref, aligned_ref,
):
    row_scale = scale_ref[...]
    groups = [pl.ds(group * HD, HD) for group in range(key_ref.shape[1] // HD)]
    aligned, key_parts, value_parts = attend(
        repeat, lambda own: query_ref[:, own] * row_scale, cos_ref[...], sin_ref[...],
        seg_row_ref[...], seg_col_ref[...], [key_ref[:, shared] for shared in groups],
        [value_ref[:, shared] for shared in groups], grad_ref, context_ref, query_grad_ref,
    )
    for shared, key_part, value_part in zip(groups, key_parts, value_parts):
        key_part_ref[:, shared] = key_part
        value_part_ref[:, shared] = value_part
    aligned_ref[...] = jnp.sum(aligned, axis=1, keepdims=True)


def attention_parts(repeat, query_pre, inv_rms, cosines, sines, seg_row, keys, values, context_grad):
    rows = query_pre.shape[0]
    whole = pl.BlockSpec(memory_space=pltpu.VMEM)
    return pl.pallas_call(
        functools.partial(attention_kernel, repeat),
        in_specs=[whole] * 9,
        out_specs=[whole] * 5,
        out_shape=[
            jax.ShapeDtypeStruct(query_pre.shape, jnp.bfloat16),
            jax.ShapeDtypeStruct(query_pre.shape, jnp.bfloat16),
            jax.ShapeDtypeStruct(keys.shape, jnp.float32),
            jax.ShapeDtypeStruct(keys.shape, jnp.float32),
            jax.ShapeDtypeStruct((rows, 1), jnp.float32),
        ],
        compiler_params=pltpu.CompilerParams(vmem_limit_bytes=VMEM_LIMIT),
    )(
        query_pre, inv_rms, cosines, sines, seg_row[None, :], seg_row[:, None], keys, values,
        context_grad,
    )


def middle_kernel(
    repeat, gained_ref, q_weight_ref, kv_weight_ref, scale_ref, cos_ref, sin_ref, seg_row_ref,
    seg_col_ref, grad_ref, context_ref, aligned_ref, out_ref, gained, q_weight, kv_weight, out,
    query_sum, pair_sum, query_grad, sems,
):
    width, heads_cols = q_weight.shape
    pieces = sems.shape[1]
    step = width // pieces

    def part(piece):
        return pl.ds(pl.multiple_of(piece * step, step), step)

    def fetches(piece):
        span = part(piece)
        return (
            pltpu.make_async_copy(
                gained_ref.at[:, span], gained.at[:, span], sems.at[0, piece]
            ),
            pltpu.make_async_copy(q_weight_ref.at[span], q_weight.at[span], sems.at[1, piece]),
            pltpu.make_async_copy(kv_weight_ref.at[span], kv_weight.at[span], sems.at[2, piece]),
        )

    def returned(piece):
        span = part(piece)
        return pltpu.make_async_copy(out.at[:, span], out_ref.at[:, span], sems.at[3, piece])

    @pl.loop(0, pieces)
    def _(piece):
        for fetch in fetches(piece):
            fetch.start()

    query_sum[...] = jnp.zeros_like(query_sum)
    pair_sum[...] = jnp.zeros_like(pair_sum)

    @pl.loop(0, pieces)
    def _(piece):
        for fetch in fetches(piece):
            fetch.wait()
        span = part(piece)
        features = gained[:, span]
        query_sum[...] += dot_f32(features, q_weight[span, :])
        pair_sum[...] += dot_f32(features, kv_weight[span, :])

    row_scale = scale_ref[...]
    cosines, sines = cos_ref[...], sin_ref[...]
    groups = kv_weight.shape[1] // (2 * HD)
    pair_plain = pair_sum[...] * row_scale
    halves = [pair_plain[:, i * HD : (i + 1) * HD] for i in range(2 * groups)]
    aligned, key_parts, value_parts = attend(
        repeat, lambda own: query_sum[:, own] * row_scale, cosines, sines, seg_row_ref[...],
        seg_col_ref[...], [turn(half, cosines, sines).astype(jnp.bfloat16) for half in halves[::2]],
        [half.astype(jnp.bfloat16) for half in halves[1::2]], grad_ref, context_ref, query_grad,
    )
    pair_grads = []
    for key_part, value_part in zip(key_parts, value_parts):
        pair_grads.append(turn(key_part, cosines, -sines).astype(jnp.bfloat16))
        pair_grads.append(value_part.astype(jnp.bfloat16))
    for half, pair_grad in zip(halves, pair_grads):
        aligned += half * pair_grad.astype(jnp.float32)
    aligned_ref[...] = jnp.sum(aligned, axis=1, keepdims=True)
    pair_grad = jnp.concatenate(pair_grads, axis=1)

    @pl.loop(0, pieces)
    def _(piece):
        span = part(piece)
        out[:, span] = (
            dot_f32(query_grad[...], q_weight[span, :], ROWS_BY_ROWS)
            + dot_f32(pair_grad, kv_weight[span, :], ROWS_BY_ROWS)
        ).astype(out.dtype)
        returned(piece).start()

    @pl.loop(0, pieces)
    def _(piece):
        returned(piece).wait()


def middle(
    repeat, gained, q_weight, kv_weight, inv_rms, cosines, sines, seg_row, context_grad
):
    rows, width = gained.shape
    heads_cols, kv_cols = q_weight.shape[1], kv_weight.shape[1]
    whole, far = pl.BlockSpec(memory_space=pltpu.VMEM), pl.BlockSpec(memory_space=pl.ANY)
    return pl.pallas_call(
        functools.partial(middle_kernel, repeat),
        in_specs=[far] * 3 + [whole] * 6,
        out_specs=[whole] * 2 + [far],
        out_shape=[
            jax.ShapeDtypeStruct((rows, heads_cols), jnp.bfloat16),
            jax.ShapeDtypeStruct((rows, 1), jnp.float32),
            jax.ShapeDtypeStruct((rows, width), jnp.bfloat16),
        ],
        scratch_shapes=[
            pltpu.VMEM(gained.shape, jnp.bfloat16),
            pltpu.VMEM(q_weight.shape, jnp.bfloat16),
            pltpu.VMEM(kv_weight.shape, jnp.bfloat16),
            pltpu.VMEM(gained.shape, jnp.bfloat16),
            pltpu.VMEM((rows, heads_cols), jnp.float32),
            pltpu.VMEM((rows, kv_cols), jnp.float32),
            pltpu.VMEM((rows, heads_cols), jnp.bfloat16),
            pltpu.SemaphoreType.DMA((4, 8)),
        ],
        compiler_params=pltpu.CompilerParams(vmem_limit_bytes=VMEM_LIMIT),
    )(
        gained, q_weight, kv_weight, inv_rms, cosines, sines, seg_row[None, :], seg_row[:, None],
        context_grad,
    )


def stitch_kernel(packs, rank_ref, token_ref, source_ref, weight_ref, *refs):
    out_refs, product = refs[:packs], refs[-1]
    block = source_ref.shape[0]
    step = pl.program_id(0)
    here = pl.ds(pl.multiple_of(step * block, block), block)
    product[here, :] = dot_f32(source_ref[...], weight_ref[...]).astype(jnp.bfloat16)

    @pl.when(step == pl.num_programs(0) - 1)
    def _():
        pack_len = out_refs[0].shape[0]
        shape = (pack_len, product.shape[0])
        place = token_ref[...] - lax.broadcasted_iota(jnp.int32, shape, 0)
        for distance in range(packs):
            first = (rank_ref[0] ^ distance) * pack_len
            rows = (place == first).astype(jnp.float32).astype(jnp.bfloat16)
            out_refs[distance][...] = dot_f32(rows, product[...]).astype(jnp.bfloat16)


def stitched(packs, pack_len, rank, row_token, source, weight):
    rows, features = source.shape
    cols = weight.shape[1]
    block = min(512, rows)
    fixed = lambda i: (0, 0)
    return pl.pallas_call(
        functools.partial(stitch_kernel, packs),
        grid=(rows // block,),
        in_specs=[
            pl.BlockSpec(memory_space=pltpu.SMEM),
            pl.BlockSpec((1, rows), fixed),
            pl.BlockSpec((block, features), lambda i: (i, 0)),
            pl.BlockSpec(weight.shape, fixed),
        ],
        out_specs=[pl.BlockSpec((pack_len, cols), fixed)] * packs,
        out_shape=[jax.ShapeDtypeStruct((pack_len, cols), jnp.bfloat16)] * packs,
        scratch_shapes=[pltpu.VMEM((rows, cols), jnp.bfloat16)],
        compiler_params=pltpu.CompilerParams(vmem_limit_bytes=VMEM_LIMIT),
    )(rank.reshape(1), row_token[None, :], source, weight)


def back_kernel(query_ref, pair_ref, q_weight_ref, kv_weight_ref, out_ref):
    out_ref[...] = (
        dot_f32(query_ref[...], q_weight_ref[...], ROWS_BY_ROWS)
        + dot_f32(pair_ref[...], kv_weight_ref[...], ROWS_BY_ROWS)
    ).astype(out_ref.dtype)


def back_projected(grad_queries, grad_pairs, q_weight, kv_weight):
    rows = grad_queries.shape[0]
    width = q_weight.shape[0]
    block = 2048
    fixed = lambda i: (0, 0)
    return pl.pallas_call(
        back_kernel,
        grid=(width // block,),
        in_specs=[
            pl.BlockSpec(grad_queries.shape, fixed),
            pl.BlockSpec(grad_pairs.shape, fixed),
            pl.BlockSpec((block, q_weight.shape[1]), lambda i: (i, 0)),
            pl.BlockSpec((block, kv_weight.shape[1]), lambda i: (i, 0)),
        ],
        out_specs=pl.BlockSpec((rows, block), lambda i: (0, i)),
        out_shape=jax.ShapeDtypeStruct((rows, width), jnp.bfloat16),
        compiler_params=pltpu.CompilerParams(vmem_limit_bytes=VMEM_LIMIT),
    )(grad_queries, grad_pairs, q_weight, kv_weight)


def outer_kernel(*refs):
    features_ref, out_ref = refs[0], refs[-1]
    total = None
    for place, grad_ref in enumerate(refs[1:-1]):
        rows = grad_ref.shape[0]
        term = dot_f32(features_ref[:, pl.ds(place * rows, rows)], grad_ref[...])
        total = term if total is None else total + term
    out_ref[...] = total


def outer_summed(features, grads):
    block = min(512, features.shape[0])
    cols = grads[0].shape[1]
    return pl.pallas_call(
        outer_kernel,
        grid=(features.shape[0] // block,),
        in_specs=[pl.BlockSpec((block, features.shape[1]), lambda i: (i, 0))]
        + [pl.BlockSpec(grad.shape, lambda i: (0, 0)) for grad in grads],
        out_specs=pl.BlockSpec((block, cols), lambda i: (i, 0)),
        out_shape=jax.ShapeDtypeStruct((features.shape[0], cols), jnp.float32),
        compiler_params=pltpu.CompilerParams(vmem_limit_bytes=20 * 2**20),
    )(features, *grads)


STAY, FIRST, SECOND, LAST = (0, 1, 2, 3), (1, 3, 0, 2), (2, 0, 3, 1), (3, 2, 1, 0)


OUTWARD = [(0, 1), (1, 0), (2, 3), (3, 2)]
INSIDE = [(0, 1), (1, 0), (2, 4), (3, 5), (4, 2), (5, 3), (6, 7), (7, 6)]


def is_inner():
    chip = lax.axis_index("tp") // 2
    return (chip == 1) | (chip == 2)


def along(value, pairs):
    both = [(2 * start + core, 2 * end + core) for start, end in pairs for core in range(2)]
    return lax.ppermute(value, "tp", both)


def towards(table):
    return [(start, end) for start, end in enumerate(table)]


def arriving(table):
    return [(start, end) for end, start in enumerate(table)]


def after(value, done):
    value, done = lax.optimization_barrier((value, done))
    return value, done


def gather_begun(block):
    return along(block, arriving(FIRST))


def gather_second(block):
    return along(block, arriving(SECOND))


def gather_last(block, first):
    return along(first, OUTWARD), lax.ppermute(block, "tp", INSIDE)


def early_blocks(block, first):
    return [block, swapped(block, "tp", 1), first, swapped(first, "tp", 1)]


def late_blocks(second, last):
    far, near = last
    last = jnp.where(is_inner(), near, far)
    return [second, swapped(second, "tp", 1), last, swapped(last, "tp", 1)]


def both_cores(parts, place):
    other = swapped(parts[2 * place + 1], "tp", 1)
    return parts[2 * place].astype(jnp.float32) + other.astype(jnp.float32)


def scatter_begun(parts):
    last = both_cores(parts, 0).astype(jnp.bfloat16)
    return last, along(last, OUTWARD), lax.ppermute(last, "tp", INSIDE)


def scatter_second(parts):
    return along(both_cores(parts, 1).astype(jnp.bfloat16), towards(SECOND))


def scatter_first(parts, far):
    first = both_cores(parts, 2)
    first += jnp.where(is_inner(), far.astype(jnp.float32), 0.0)
    return along(first.astype(jnp.bfloat16), towards(FIRST))


def scatter_total(parts, near, second, first):
    total = both_cores(parts, 3) + jnp.where(is_inner(), near.astype(jnp.float32), 0.0)
    return total + second.astype(jnp.float32) + first.astype(jnp.float32)


def line_stitch_half(blocks, rows, rows_ref, weight_ref, product, here, sems, out_sem):
    block = blocks[0].shape[0]
    fetches = [
        pltpu.make_async_copy(blocks[i], rows.at[pl.ds(i * block, block)], sems.at[i])
        for i in range(4)
    ]
    for fetch in fetches:
        fetch.start()
    for fetch in fetches:
        fetch.wait()
    kept = pltpu.make_async_copy(rows, rows_ref, out_sem)
    kept.start()
    product[here, :] = dot_f32(rows[...], weight_ref[...]).astype(jnp.bfloat16)
    return kept


def line_stitch_early_kernel(weight_ref, *refs):
    blocks, (product_ref, rows_ref, rows, sems, out_sem) = refs[:4], refs[4:]
    everything = pl.ds(0, rows.shape[0])
    line_stitch_half(
        blocks, rows, rows_ref, weight_ref, product_ref, everything, sems, out_sem
    ).wait()


def line_stitch_kernel(packs, rank_ref, token_ref, weight_ref, early_ref, *refs):
    blocks, out_refs = refs[:4], refs[4 : 4 + packs]
    rows_ref, rows, product, sems, out_sem = refs[4 + packs :]
    half = rows.shape[0]
    kept = line_stitch_half(
        blocks, rows, rows_ref, weight_ref, product, pl.ds(half, half), sems, out_sem
    )
    product[pl.ds(0, half), :] = early_ref[...]
    pack_len = out_refs[0].shape[0]
    place = token_ref[...] - lax.broadcasted_iota(jnp.int32, (pack_len, product.shape[0]), 0)
    for distance in range(packs):
        first = (rank_ref[0] ^ distance) * pack_len
        chosen = (place == first).astype(jnp.float32).astype(jnp.bfloat16)
        out_refs[distance][...] = dot_f32(chosen, product[...]).astype(jnp.bfloat16)
    kept.wait()


def line_stitched_early(blocks, weight):
    block, features = blocks[0].shape
    cols = weight.shape[1]
    whole, far = pl.BlockSpec(memory_space=pltpu.VMEM), pl.BlockSpec(memory_space=pl.ANY)
    return pl.pallas_call(
        line_stitch_early_kernel,
        in_specs=[whole] + [far] * 4,
        out_specs=[whole, far],
        out_shape=[
            jax.ShapeDtypeStruct((4 * block, cols), jnp.bfloat16),
            jax.ShapeDtypeStruct((4 * block, features), jnp.bfloat16),
        ],
        scratch_shapes=[
            pltpu.VMEM((4 * block, features), jnp.bfloat16),
            pltpu.SemaphoreType.DMA((4,)),
            pltpu.SemaphoreType.DMA,
        ],
        compiler_params=pltpu.CompilerParams(vmem_limit_bytes=20 * 2**20),
    )(weight, *blocks)


def line_stitched(packs, pack_len, rank, token_row, early, blocks, weight):
    block, features = blocks[0].shape
    cols = weight.shape[1]
    whole, far = pl.BlockSpec(memory_space=pltpu.VMEM), pl.BlockSpec(memory_space=pl.ANY)
    results = pl.pallas_call(
        functools.partial(line_stitch_kernel, packs),
        in_specs=[pl.BlockSpec(memory_space=pltpu.SMEM)] + [whole] * 3 + [far] * 4,
        out_specs=[whole] * packs + [far],
        out_shape=[jax.ShapeDtypeStruct((pack_len, cols), jnp.bfloat16)] * packs
        + [jax.ShapeDtypeStruct((4 * block, features), jnp.bfloat16)],
        scratch_shapes=[
            pltpu.VMEM((4 * block, features), jnp.bfloat16),
            pltpu.VMEM((8 * block, cols), jnp.bfloat16),
            pltpu.SemaphoreType.DMA((4,)),
            pltpu.SemaphoreType.DMA,
        ],
        compiler_params=pltpu.CompilerParams(vmem_limit_bytes=24 * 2**20),
    )(rank.reshape(1), token_row, weight, early, *blocks)
    return results[:packs], results[packs]


def line_grad_kernel(chips_ref, core_ref, weight_ref, *refs):
    blocks, out_ref, features, total, sems = refs[:8], *refs[8:]
    step = pl.program_id(0)
    cols = blocks[0].shape[1]

    def fetch(place, half):
        core = core_ref[0] if half == 0 else 1 - core_ref[0]
        there = features.at[place, :, pl.ds(pl.multiple_of(core * cols, cols), cols)]
        return there, sems.at[place, half]

    @pl.when(step == 0)
    def _():
        for i in range(8):
            pltpu.make_async_copy(blocks[i], *fetch(i // 2, i % 2)).start()
        total[...] = jnp.zeros_like(total)

    for half in range(2):
        pltpu.make_async_copy(blocks[half], *fetch(step, half)).wait()
    total[...] += dot_f32(features[step], weight_ref[...], ROWS_BY_ROWS)

    @pl.when(step == 3)
    def _():
        out_ref[...] = total[...].astype(out_ref.dtype)


def line_grad_context(chips, core, blocks, weight):
    rows, cols = blocks[0].shape
    heads_cols = weight.shape[0]
    far = pl.BlockSpec(memory_space=pl.ANY)
    return pl.pallas_call(
        line_grad_kernel,
        grid_spec=pltpu.PrefetchScalarGridSpec(
            num_scalar_prefetch=2,
            grid=(4,),
            in_specs=[pl.BlockSpec((heads_cols, 2 * cols), lambda i, chips, core: (0, chips[i]))]
            + [far] * 8,
            out_specs=pl.BlockSpec((rows, heads_cols), lambda i, chips, core: (0, 0)),
            scratch_shapes=[
                pltpu.VMEM((4, rows, 2 * cols), jnp.bfloat16),
                pltpu.VMEM((rows, heads_cols), jnp.float32),
                pltpu.SemaphoreType.DMA((4, 2)),
            ],
        ),
        out_shape=jax.ShapeDtypeStruct((rows, heads_cols), jnp.bfloat16),
        compiler_params=pltpu.CompilerParams(vmem_limit_bytes=VMEM_LIMIT),
    )(chips, core.reshape(1), weight, *blocks)


def line_attended_kernel(chips_ref, core_ref, context_ref, weight_ref, *refs):
    out_refs, product = refs[:8], refs[8]
    step = pl.program_id(0)
    cols = out_refs[0].shape[1]
    product[...] = dot_f32(context_ref[...], weight_ref[...]).astype(jnp.bfloat16)
    for i in range(4):

        @pl.when(step == i)
        def _(i=i):
            for half in range(2):
                core = core_ref[0] if half == 0 else 1 - core_ref[0]
                here = pl.ds(pl.multiple_of(core * cols, cols), cols)
                out_refs[2 * i + half][...] = product[:, here]


def line_attended(chips, core, context, weight):
    rows, heads_cols = context.shape
    cols = weight.shape[1] // 8
    fixed = lambda i, chips, core: (0, 0)
    return pl.pallas_call(
        line_attended_kernel,
        grid_spec=pltpu.PrefetchScalarGridSpec(
            num_scalar_prefetch=2,
            grid=(4,),
            in_specs=[
                pl.BlockSpec((rows, heads_cols), fixed),
                pl.BlockSpec((heads_cols, 2 * cols), lambda i, chips, core: (0, chips[i])),
            ],
            out_specs=[pl.BlockSpec((rows, cols), fixed)] * 8,
            scratch_shapes=[pltpu.VMEM((rows, 2 * cols), jnp.bfloat16)],
        ),
        out_shape=[jax.ShapeDtypeStruct((rows, cols), jnp.bfloat16)] * 8,
        compiler_params=pltpu.CompilerParams(vmem_limit_bytes=VMEM_LIMIT),
    )(chips, core.reshape(1), context, weight)


def line_project(
    places, from_ref, gain_ref, q_weight_ref, kv_weight_ref, blocks, hidden, q_weight, kv_weight,
    sems, query_sum, pair_sum, squares,
):
    rows, step = blocks[0].shape

    def part(place):
        return pl.ds(pl.multiple_of(from_ref[place] * step, step), step)

    def fetches(place):
        span = part(place)
        return (
            pltpu.make_async_copy(q_weight_ref.at[span], q_weight.at[span], sems.at[1, place]),
            pltpu.make_async_copy(kv_weight_ref.at[span], kv_weight.at[span], sems.at[2, place]),
        )

    def features(place):
        return pltpu.make_async_copy(blocks[0], hidden.at[place], sems.at[0, place])

    later = [place for place in range(len(blocks)) if place not in places]
    for place in [*places, *later]:
        pltpu.make_async_copy(blocks[place], hidden.at[place], sems.at[0, place]).start()
        for fetch in fetches(place):
            fetch.start()

    def project(place, squares):
        features(place).wait()
        for fetch in fetches(place):
            fetch.wait()
        span = part(place)
        wide = hidden[place].astype(jnp.float32)
        gained = (wide * gain_ref[:, span]).astype(jnp.bfloat16)
        query_sum[...] += dot_f32(gained, q_weight[span, :])
        pair_sum[...] += dot_f32(gained, kv_weight[span, :])
        return squares + jnp.sum(wide * wide, axis=1, keepdims=True)

    squares = lax.fori_loop(places[0], places[-1] + 1, project, squares)

    def finish():
        for place in later:
            features(place).wait()
            for fetch in fetches(place):
                fetch.wait()

    return squares, finish


def line_projected_kernel(
    from_ref, gain_ref, q_weight_ref, kv_weight_ref, *refs,
):
    blocks, (query_sum, pair_sum, squares_ref) = refs[:4], refs[4:7]
    hidden, q_weight, kv_weight, sems = refs[7:]
    query_sum[...] = jnp.zeros_like(query_sum)
    pair_sum[...] = jnp.zeros_like(pair_sum)
    squares, _ = line_project(
        range(4), from_ref, gain_ref, q_weight_ref, kv_weight_ref, blocks, hidden, q_weight,
        kv_weight, sems, query_sum, pair_sum, jnp.zeros(squares_ref.shape, jnp.float32),
    )
    squares_ref[...] = squares


def line_projected(sources, blocks, gain, q_weight, kv_weight):
    rows, step = blocks[0].shape
    heads_cols, kv_cols = q_weight.shape[1], kv_weight.shape[1]
    whole, far = pl.BlockSpec(memory_space=pltpu.VMEM), pl.BlockSpec(memory_space=pl.ANY)
    return pl.pallas_call(
        line_projected_kernel,
        in_specs=[pl.BlockSpec(memory_space=pltpu.SMEM), whole] + [far] * 6,
        out_specs=[whole] * 3,
        out_shape=[
            jax.ShapeDtypeStruct((rows, heads_cols), jnp.float32),
            jax.ShapeDtypeStruct((rows, kv_cols), jnp.float32),
            jax.ShapeDtypeStruct((rows, 1), jnp.float32),
        ],
        scratch_shapes=[
            pltpu.VMEM((4, rows, step), jnp.bfloat16),
            pltpu.VMEM(q_weight.shape, jnp.bfloat16),
            pltpu.VMEM(kv_weight.shape, jnp.bfloat16),
            pltpu.SemaphoreType.DMA((3, 4)),
        ],
        compiler_params=pltpu.CompilerParams(vmem_limit_bytes=VMEM_LIMIT),
    )(sources, gain[None, :], q_weight, kv_weight, *blocks)


def line_tokens_kernel(token_ref, order_ref, early_ref, late_ref, out_ref):
    half = early_ref.shape[0]
    total = None
    for place, rows_ref in enumerate((early_ref, late_ref)):
        tokens = token_ref[pl.ds(place * half, half), :]
        chosen = (tokens == order_ref[...]).astype(jnp.float32).astype(jnp.bfloat16)
        term = dot_f32(rows_ref[...], chosen, COLS_BY_COLS)
        total = term if total is None else total + term
    out_ref[...] = total.astype(out_ref.dtype)


def line_tokens_last(token_col, token_order, early_rows, late_rows):
    half, features = early_rows.shape
    tokens = token_order.shape[1]
    block = min(1024, features)
    fixed = lambda i: (0, 0)
    return pl.pallas_call(
        line_tokens_kernel,
        grid=(features // block,),
        in_specs=[
            pl.BlockSpec((2 * half, 1), fixed),
            pl.BlockSpec((1, tokens), fixed),
            pl.BlockSpec((half, block), lambda i: (0, i)),
            pl.BlockSpec((half, block), lambda i: (0, i)),
        ],
        out_specs=pl.BlockSpec((block, tokens), lambda i: (i, 0)),
        out_shape=jax.ShapeDtypeStruct((features, tokens), jnp.bfloat16),
        compiler_params=pltpu.CompilerParams(vmem_limit_bytes=VMEM_LIMIT),
    )(token_col, token_order, early_rows, late_rows)


def line_middle_kernel(
    repeat, from_ref, to_ref, gain_ref, cos_ref, sin_ref, seg_row_ref, seg_col_ref, grad_ref,
    early_query_ref, early_pair_ref, early_squares_ref, q_weight_ref, kv_weight_ref, *refs,
):
    blocks, context_ref, out_refs = refs[:8], refs[8], refs[9:17]
    hidden, q_weight, kv_weight, out, query_sum, pair_sum, query_grad, sems, out_sems = refs[17:]
    width = q_weight.shape[0]
    rows, step = blocks[0].shape

    def part(rank):
        return pl.ds(pl.multiple_of(rank * step, step), step)

    query_sum[...] = early_query_ref[...]
    pair_sum[...] = early_pair_ref[...]
    squares, finish = line_project(
        range(4, 8), from_ref, gain_ref, q_weight_ref, kv_weight_ref, blocks, hidden, q_weight,
        kv_weight, sems, query_sum, pair_sum, early_squares_ref[...],
    )
    row_scale = lax.rsqrt(squares / width + epsilon)
    cosines, sines = cos_ref[...], sin_ref[...]
    groups = kv_weight.shape[1] // (2 * HD)
    pair_plain = pair_sum[...] * row_scale
    halves = [pair_plain[:, i * HD : (i + 1) * HD] for i in range(2 * groups)]
    aligned, key_parts, value_parts = attend(
        repeat, lambda own: query_sum[:, own] * row_scale, cosines, sines, seg_row_ref[...],
        seg_col_ref[...], [turn(half, cosines, sines).astype(jnp.bfloat16) for half in halves[::2]],
        [half.astype(jnp.bfloat16) for half in halves[1::2]], grad_ref, context_ref, query_grad,
    )
    pair_grads = []
    for key_part, value_part in zip(key_parts, value_parts):
        pair_grads.append(turn(key_part, cosines, -sines).astype(jnp.bfloat16))
        pair_grads.append(value_part.astype(jnp.bfloat16))
    for half, pair_grad in zip(halves, pair_grads):
        aligned += half * pair_grad.astype(jnp.float32)
    aligned = jnp.sum(aligned, axis=1, keepdims=True) * (row_scale * row_scale / width)
    pair_grad = jnp.concatenate(pair_grads, axis=1)
    finish()

    @pl.loop(0, 8)
    def _(place):
        span = part(to_ref[place])
        grad_normed = dot_f32(query_grad[...], q_weight[span, :], ROWS_BY_ROWS)
        grad_normed += dot_f32(pair_grad, kv_weight[span, :], ROWS_BY_ROWS)
        features = hidden[6 - 2 * (place // 2) + place % 2].astype(jnp.float32)
        out[place] = (
            grad_normed * (row_scale * gain_ref[:, span]) - features * aligned
        ).astype(out.dtype)
        for i in range(8):

            @pl.when(place == i)
            def _(i=i):
                pltpu.make_async_copy(out.at[i], out_refs[i], out_sems.at[i]).start()

    for i in range(8):
        pltpu.make_async_copy(out.at[i], out_refs[i], out_sems.at[i]).wait()


def line_middle(
    repeat, sources, targets, blocks, early_sums, gain, q_weight, kv_weight, cosines, sines, seg_row,
    seg_col, context_grad,
):
    rows, step = blocks[0].shape
    heads_cols, kv_cols = q_weight.shape[1], kv_weight.shape[1]
    whole, far = pl.BlockSpec(memory_space=pltpu.VMEM), pl.BlockSpec(memory_space=pl.ANY)
    scalars = pl.BlockSpec(memory_space=pltpu.SMEM)
    results = pl.pallas_call(
        functools.partial(line_middle_kernel, repeat),
        in_specs=[scalars] * 2 + [whole] * 9 + [far] * 10,
        out_specs=[whole] + [far] * 8,
        out_shape=[jax.ShapeDtypeStruct((rows, heads_cols), jnp.bfloat16)]
        + [jax.ShapeDtypeStruct((rows, step), jnp.bfloat16)] * 8,
        scratch_shapes=[
            pltpu.VMEM((8, rows, step), jnp.bfloat16),
            pltpu.VMEM(q_weight.shape, jnp.bfloat16),
            pltpu.VMEM(kv_weight.shape, jnp.bfloat16),
            pltpu.VMEM((8, rows, step), jnp.bfloat16),
            pltpu.VMEM((rows, heads_cols), jnp.float32),
            pltpu.VMEM((rows, kv_cols), jnp.float32),
            pltpu.VMEM((rows, heads_cols), jnp.bfloat16),
            pltpu.SemaphoreType.DMA((3, 8)),
            pltpu.SemaphoreType.DMA((8,)),
        ],
        compiler_params=pltpu.CompilerParams(vmem_limit_bytes=VMEM_LIMIT),
    )(
        sources, targets, gain[None, :], cosines, sines, seg_row[None, :], seg_col,
        context_grad, *early_sums, q_weight, kv_weight, *blocks,
    )
    return results[0], results[1:]


def line_body(
    source, row_token, seg_ids, stitch_weight, norm_gain, q_weight, kv_weight, o_weight, out_grad
):
    tok_rank = lax.axis_index("tok")
    tp_rank = lax.axis_index("tp")
    packs = lax.axis_size("tok")
    pack_len = seg_ids.shape[1]
    width = q_weight.shape[0]
    own_cols = stitch_weight.shape[1]
    repeat = (q_weight.shape[1] // HD) // (kv_weight.shape[1] // (2 * HD))
    chip, core = tp_rank // 2, tp_rank % 2

    def chips(tables):
        return jnp.array(tables, jnp.int32)[:, chip]

    def ranks(tables):
        pairs = 2 * chips(tables)
        return jnp.stack([pairs + core, pairs + 1 - core], axis=1).reshape(-1)

    arrival, departure = (STAY, FIRST, SECOND, LAST), (LAST, SECOND, FIRST, STAY)
    sources, targets = ranks(arrival), ranks(departure)

    within = jnp.arange(pack_len, dtype=jnp.int32)
    seg_row = seg_ids[0]
    earlier = jnp.sum((seg_row[None, :] < seg_row[:, None]).astype(jnp.int32), axis=1)
    angles = (within - earlier).astype(jnp.float32)[:, None] * frequencies()[None, :]
    cosine, sine = jnp.cos(angles), jnp.sin(angles)
    cosines = jnp.concatenate([cosine, cosine], axis=1)
    sines = jnp.concatenate([-sine, sine], axis=1)

    token_row = row_token.reshape(8, -1)[sources].reshape(1, -1)
    first = gather_begun(source)
    seg_col, token_col = seg_row[:, None], token_row.reshape(-1, 1)
    arrivals, departures = chips(arrival), chips(departure)
    small = (token_row, token_col, seg_col, cosines, sines, sources, targets, arrivals, departures)
    source, (first, small) = after(source, (first, small))
    token_row, token_col, seg_col, cosines, sines, sources, targets, arrivals, departures = small
    second, last = gather_second(source), gather_last(source, first)
    early_source = early_blocks(source, first)
    early_product, early_rows = line_stitched_early(early_source, stitch_weight)
    out_grad, (second, last, early_product) = after(out_grad, (second, last, early_product))
    late_source = late_blocks(second, last)
    og_first = gather_begun(out_grad)
    placed, late_rows = line_stitched(
        packs, pack_len, tok_rank, token_row, early_product, late_source, stitch_weight
    )
    received = [swapped(placed[distance], "tok", distance) for distance in range(1, packs)]
    received[0], og_first = after(received[0], og_first)
    og_second, og_last = gather_second(out_grad), gather_last(out_grad, og_first)
    received[1], (og_second, og_near) = after(received[1], (og_second, og_last[1]))
    og_last = (og_last[0], og_near)
    hidden = placed[0].astype(jnp.float32)
    for part in received:
        hidden += part.astype(jnp.float32)
    hidden_bf = hidden.astype(jnp.bfloat16)
    hidden_first = gather_begun(hidden_bf)
    early_rows, hidden_bf = after(early_rows, hidden_bf)
    token_order = (
        (tok_rank ^ jnp.arange(packs, dtype=jnp.int32))[:, None] * pack_len + within[None, :]
    ).reshape(-1)
    tokens_last = line_tokens_last(token_col, token_order[None, :], early_rows, late_rows)
    (hidden_bf, hidden_first), (og_second, og_last, tokens_last) = after(
        (hidden_bf, hidden_first), (og_second, og_last, tokens_last)
    )
    hidden_second, hidden_last = gather_second(hidden_bf), gather_last(hidden_bf, hidden_first)
    og_blocks = early_blocks(out_grad, og_first) + late_blocks(og_second, og_last)
    grad_context = line_grad_context(arrivals, core, og_blocks, o_weight)
    early_hidden = early_blocks(hidden_bf, hidden_first)
    early_sums = line_projected(sources, early_hidden, norm_gain, q_weight, kv_weight)
    hidden_last, (hidden_second, grad_context, early_sums) = after(
        hidden_last, (hidden_second, grad_context, early_sums)
    )
    hidden_blocks = early_hidden + late_blocks(hidden_second, hidden_last)

    context, grad_parts = line_middle(
        repeat, sources, targets, hidden_blocks, early_sums, norm_gain, q_weight, kv_weight,
        cosines, sines, seg_row, seg_col, grad_context,
    )
    last, far, near = scatter_begun(grad_parts)
    context, last = after(context, last)
    attended_parts = line_attended(departures, core, context, o_weight)
    second = scatter_second(grad_parts)
    far, (near, attended_parts) = after(far, (near, attended_parts))
    first = scatter_first(grad_parts, far)
    grad_sum = scatter_total(grad_parts, near, second, first)
    grad_hidden = (out_grad.astype(jnp.float32) + grad_sum).astype(jnp.bfloat16)
    every_pack = [grad_hidden] + [
        swapped(grad_hidden, "tok", distance) for distance in range(1, packs)
    ]
    _, far, near = scatter_begun(attended_parts)
    second = scatter_second(attended_parts)
    first = scatter_first(attended_parts, far)
    late_hidden, near, second, *every_pack = lax.optimization_barrier(
        (hidden_bf, near, second, *every_pack)
    )
    stitch_grad = outer_summed(tokens_last, every_pack)
    attended = scatter_total(attended_parts, near, second, first)
    layer_out = (late_hidden.astype(jnp.float32) + attended).astype(jnp.bfloat16)
    return (layer_out, stitch_grad)


def body(
    source, row_token, seg_ids, stitch_weight, norm_gain, q_weight, kv_weight, o_weight, out_grad
):
    tok_rank = lax.axis_index("tok")
    tp_rank = lax.axis_index("tp")
    packs = lax.axis_size("tok")
    pack_len = seg_ids.shape[1]
    width = q_weight.shape[0]
    own_cols = stitch_weight.shape[1]
    own_gain = lax.dynamic_slice_in_dim(norm_gain, tp_rank * own_cols, own_cols)

    gathered = lax.all_gather(source, "tp", axis=0, tiled=True)
    placed = stitched(packs, pack_len, tok_rank, row_token, gathered, stitch_weight)
    within = jnp.arange(pack_len, dtype=jnp.int32)
    hidden = placed[0].astype(jnp.float32)
    for distance in range(1, packs):
        hidden += swapped(placed[distance], "tok", distance).astype(jnp.float32)
    hidden_bf = hidden.astype(jnp.bfloat16)
    hidden_f = hidden_bf.astype(jnp.float32)
    square_sum = summed(jnp.sum(hidden_f * hidden_f, axis=1), "tp")
    inv_rms = lax.rsqrt(square_sum / width + epsilon)[:, None]
    gained = lax.all_gather((hidden_f * own_gain).astype(jnp.bfloat16), "tp", axis=1, tiled=True)

    token_order = (
        (tok_rank ^ jnp.arange(packs, dtype=jnp.int32))[:, None] * pack_len + within[None, :]
    ).reshape(-1)
    order = (row_token[:, None] == token_order[None, :]).astype(jnp.bfloat16)
    tokens_last = dot_f32(gathered, order, COLS_BY_COLS).astype(jnp.bfloat16)

    seg_row = seg_ids[0]
    earlier = jnp.sum((seg_row[None, :] < seg_row[:, None]).astype(jnp.int32), axis=1)
    angles = (within - earlier).astype(jnp.float32)[:, None] * frequencies()[None, :]
    cosine, sine = jnp.cos(angles), jnp.sin(angles)
    cosines = jnp.concatenate([cosine, cosine], axis=1)
    sines = jnp.concatenate([-sine, sine], axis=1)
    local_heads = q_weight.shape[1] // HD
    kv_cols = kv_weight.shape[1]
    paired = kv_cols == HD
    kv_local = 1 if paired else kv_cols // (2 * HD)
    repeat = local_heads // kv_local
    every_grad = lax.all_gather(out_grad, "tp", axis=1, tiled=True)
    grad_context = lax.dot_general(
        every_grad, o_weight, (((1,), (1,)), ((), ())), preferred_element_type=jnp.float32
    ).astype(jnp.bfloat16)
    if paired:
        query_pre = jnp.dot(gained, q_weight, preferred_element_type=jnp.float32)
        projected = jnp.dot(gained, kv_weight, preferred_element_type=jnp.float32) * inv_rms
        is_key = tp_rank % 2 == 0
        own_part = jnp.where(is_key, rotate(projected, cosine, sine), projected).astype(
            jnp.bfloat16
        )
        partner = swapped(own_part, "tp", 1)
        keys = jnp.where(is_key, own_part, partner)
        values = jnp.where(is_key, partner, own_part)
        context, grad_queries, key_part, value_part, aligned = attention_parts(
            repeat, query_pre, inv_rms, cosines, sines, seg_row, keys, values, grad_context
        )
        outgoing = jnp.where(is_key, value_part, key_part)
        incoming = swapped(outgoing.astype(jnp.bfloat16), "tp", 1).astype(outgoing.dtype)
        own_sum = jnp.where(is_key, key_part, value_part) + incoming
        grad_pairs = jnp.where(is_key, unrotate(own_sum, cosine, sine), own_sum).astype(
            jnp.bfloat16
        )
        aligned += jnp.sum(grad_pairs.astype(jnp.float32) * projected, axis=1, keepdims=True)
        grad_normed = back_projected(grad_queries, grad_pairs, q_weight, kv_weight)
    else:
        context, aligned, grad_normed = middle(
            repeat, gained, q_weight, kv_weight, inv_rms, cosines, sines, seg_row, grad_context
        )
    aligned = summed(aligned[:, 0], "tp")[:, None]
    grad_sum = lax.psum_scatter(grad_normed, "tp", scatter_dimension=1, tiled=True)
    attended = jnp.dot(context, o_weight, preferred_element_type=jnp.float32).astype(jnp.bfloat16)
    attended, grad_sum = lax.optimization_barrier((attended, grad_sum))
    grad_hidden = (
        out_grad.astype(jnp.float32)
        + inv_rms * own_gain * grad_sum.astype(jnp.float32)
        - hidden_f * (inv_rms * inv_rms * aligned / width)
    ).astype(jnp.bfloat16)
    every_pack = [grad_hidden] + [
        swapped(grad_hidden, "tok", distance) for distance in range(1, packs)
    ]
    late_hidden, *every_pack = lax.optimization_barrier((hidden_bf, *every_pack))
    stitch_grad = outer_summed(tokens_last, every_pack)

    attended = lax.psum_scatter(attended, "tp", scatter_dimension=1, tiled=True)
    layer_out = (late_hidden.astype(jnp.float32) + attended.astype(jnp.float32)).astype(
        jnp.bfloat16
    )
    return (layer_out, stitch_grad)


def solution(mesh):
    placed = (
        P("tp", "tok"),
        P(),
        P("tok", None),
        P("tok", "tp"),
        P(),
        P(None, "tp"),
        P(None, "tp"),
        P("tp", None),
        P("tok", "tp"),
    )
    on_line = mesh.shape["tp"] == 8
    return jax.shard_map(
        line_body if on_line else body,
        mesh=mesh,
        in_specs=placed,
        out_specs=(P("tok", "tp"), P("tok", "tp")),
        check_vma=False,
    )
```
